32 devices in a mesh: row: 2 (over x), col: 16 (over z, y, core), smp: 1.
Axes of the slice: x: 2, y: 2, z: 4, core: 2. Of those that a mesh axis runs over, the one named last changes fastest.
Arguments:
- pair_repr: bfloat16 [256, 256, 128], P('row', 'col'), may hold values from -6 to 6
- tri_weight: bfloat16 [128, 512], replicated, may hold values from -0.75 to 0.75
- tri_bias_weight: bfloat16 [128, 4], replicated, may hold values from -40 to 40
- tri_output_weight: bfloat16 [128, 128], replicated, may hold values from -0.5 to 0.5
- samples: bfloat16 [4, 256, 768], P('smp'), may hold values from -6 to 6
- levels: int32 [4], P('smp'), may hold values from 0 to 199
- single_cond: bfloat16 [256, 384], replicated, may hold values from -6 to 6
- noise_weight: bfloat16 [256, 384], replicated, may hold values from -0.375 to 0.375
- modulation_weight: bfloat16 [384, 1536], replicated, may hold values from -0.3125 to 0.3125
- attention_weight: bfloat16 [768, 3072], replicated, may hold values from -0.5 to 0.5
- pair_bias_weight: bfloat16 [128, 16], replicated, may hold values from -40 to 40
- output_weight: bfloat16 [768, 768], replicated, may hold values from -0.21875 to 0.21875
- output_gate_weight: bfloat16 [384, 768], replicated, may hold values from -0.3125 to 0.3125
Outputs:
- new_pair: bfloat16 [256, 256, 128], P('row', 'col')
- attn_update: bfloat16 [4, 256, 768], P('smp', ('row', 'col'))
The draws below stay inside these ranges and needn't reach their ends.
All inputs are finite; a program needn't handle non-finite values.
Results may differ from the reference program's by a relative error of at most 0.02.
The reference program's roundings to bfloat16 on the way count: a program that leaves them out, or rounds other values in their place, can miss the bound.
Values may be sent and summed in bfloat16 or wider, within the bound.
No kernel may reach another device: no remote copies, remote signals or barrier semaphores. Data moves between devices by JAX's collectives and lax.ppermute only.
A program may use at most 128 MiB of HBM per device.

```python
import math
import jax
import jax.numpy as jnp
from jax import lax

CZ = 128
HT = 4
DT = 32
CA = 768
HD = 16
DH = 48
CS = 384
NE = 256
LEVELS = 200
N = 256
SAMPLES = 4


def bias_weights(key, channels, head_count):
    normal_part = jax.random.normal(jax.random.fold_in(key, 17), (channels, head_count), jnp.float32) * (2.5 / math.sqrt(channels))
    return jnp.clip(normal_part, -40.0, 40.0)


def draw_tri_bias_weight(key, part):
    return bias_weights(jax.random.fold_in(key, 3), CZ, HT).astype(jnp.bfloat16)


def draw_pair_bias_weight(key, part):
    return bias_weights(jax.random.fold_in(key, 5), CZ, HD).astype(jnp.bfloat16)


def draw_tri_weight(key, part):
    width = HT * DT
    spread = CZ ** (-0.5)
    base = jax.random.normal(jax.random.fold_in(key, 71), (CZ, 4 * width), jnp.float32) * spread
    base = jnp.clip(base, -6.0 * spread, 6.0 * spread)
    return jnp.clip(base, -0.75, 0.75).astype(jnp.bfloat16)


def draw_attention_weight(key, part):
    spread = CA ** (-0.5)
    base = jax.random.normal(jax.random.fold_in(key, 41), (CA, 4 * CA), jnp.float32) * spread
    base = jnp.clip(base, -6.0 * spread, 6.0 * spread)
    return jnp.clip(base, -0.5, 0.5).astype(jnp.bfloat16)


def with_ends(values, stream_key, smallest, high):
    longest = values.shape.index(max(values.shape))
    spots = []
    for shift in (0, 1):
        where = [jax.random.randint(jax.random.fold_in(stream_key, axis), (), 0, length) for axis, length in enumerate(values.shape)]
        where[longest] = (where[longest] + shift) % values.shape[longest]
        spots.append(tuple(where))
    return values.at[spots[0]].set(smallest).at[spots[1]].set(high)


def block_levels(stream_key, shape, shards, low, largest):
    gain, own = 1.0, jax.random.fold_in(stream_key, 6)
    for axis_at, parts in shards:
        heights = jnp.exp(jax.random.uniform(jax.random.fold_in(own, axis_at), (parts,), jnp.float32, low / len(shards), largest / len(shards)))
        gain = gain * jnp.repeat(heights, shape[axis_at] // parts).reshape([-1 if axis == axis_at else 1 for axis in range(len(shape))])
    return gain


def normal_values(key, dims, scale, limit, shards=(), kind=jnp.bfloat16):
    drawn = jax.random.normal(key, dims, jnp.float32) * scale
    if len(shards) > 0:
        drawn = block_levels(key, dims, shards, -0.22, 0.18) * drawn
    return jnp.clip(drawn, min=-limit, max=limit).astype(kind)


def setup_inputs(seed: int = 0) -> dict:
    keys = jax.random.split(jax.random.key(seed), 14)
    return {
        "pair_repr": normal_values(keys[0], (N, N, CZ), 1.0, 6.0, ((0, 2), (1, 16))),
        "tri_weight": draw_tri_weight(jax.random.fold_in(keys[13], 71), 0),
        "tri_bias_weight": draw_tri_bias_weight(jax.random.fold_in(keys[13], 71), 0),
        "tri_output_weight": normal_values(keys[3], (HT * DT, CZ), (HT * DT) ** -0.5, 0.5),
        "samples": normal_values(keys[4], (SAMPLES, N, CA), 1.0, 6.0),
        "levels": with_ends(jax.random.randint(keys[5], (SAMPLES,), 0, LEVELS), jax.random.fold_in(keys[5], 1), 0, LEVELS - 1).astype(jnp.int32),
        "single_cond": normal_values(keys[6], (N, CS), 1.0, 6.0),
        "noise_weight": normal_values(keys[7], (NE, CS), NE ** -0.5, 0.375),
        "modulation_weight": normal_values(keys[8], (CS, 2 * CA), CS ** -0.5, 0.3125),
        "attention_weight": draw_attention_weight(jax.random.fold_in(keys[13], 71), 0),
        "pair_bias_weight": draw_pair_bias_weight(jax.random.fold_in(keys[13], 71), 0),
        "output_weight": normal_values(keys[11], (CA, CA), CA ** -0.5, 0.21875),
        "output_gate_weight": normal_values(keys[12], (CS, CA), CS ** -0.5, 0.3125),
    }


NORM_EPSILON = 1e-05
SIGMA_DATA = 16.0
SIGMA_MAX = 160.0
SIGMA_MIN = 0.0004

def normalize(values):
    values = values.astype(jnp.float32)
    average = lax.optimization_barrier(jnp.mean(values, axis=-1, keepdims=True))
    centred = values - average
    variance = lax.optimization_barrier(jnp.mean(centred * centred, axis=-1, keepdims=True))
    return centred * lax.rsqrt(variance + NORM_EPSILON)

def noise_features(levels):
    fraction = levels.astype(jnp.float32) / (LEVELS - 1)
    upper_root = SIGMA_MAX ** (1.0 / 7.0)
    lower_root = SIGMA_MIN ** (1.0 / 7.0)
    noise_sigma = SIGMA_DATA * (upper_root + fraction * (lower_root - upper_root)) ** 7
    scaled = 0.25 * jnp.log(noise_sigma / SIGMA_DATA)
    frequency = 2.0 * math.pi * jnp.exp(jnp.arange(NE // 2, dtype=jnp.float32) * (math.log(100.0) / (NE // 2)))
    angles = scaled[:, None] * frequency[None, :]
    return jnp.concatenate([jnp.cos(angles), jnp.sin(angles)], axis=-1)

def attend_columns(pair_cols, bias_full, tri_weight, tri_output_weight):
    row_count, col_count, channels = pair_cols.shape
    normed = normalize(pair_cols).astype(jnp.bfloat16)
    projected = jnp.dot(normed.reshape(row_count * col_count, channels), tri_weight, preferred_element_type=jnp.float32)
    projected = projected.reshape(row_count, col_count, 4, HT * DT)
    query_part = (projected[:, :, 0] * DT ** (-0.5)).astype(jnp.bfloat16)
    key_part = projected[:, :, 1].astype(jnp.bfloat16)
    value_part = projected[:, :, 2].astype(jnp.bfloat16)
    gate_part = projected[:, :, 3]

    def one_column(column):
        query_col = lax.dynamic_index_in_dim(query_part, column, 1, keepdims=False).reshape(row_count, HT, DT)
        key_col = lax.dynamic_index_in_dim(key_part, column, 1, keepdims=False).reshape(row_count, HT, DT)
        value_col = lax.dynamic_index_in_dim(value_part, column, 1, keepdims=False).reshape(row_count, HT, DT)
        gate_col = lax.dynamic_index_in_dim(gate_part, column, 1, keepdims=False)
        scores = jnp.einsum('ihd,khd->hik', query_col.astype(jnp.float32), key_col.astype(jnp.float32))
        scores = scores + bias_full
        row_peak = lax.optimization_barrier(jnp.max(scores, axis=-1, keepdims=True))
        exponent = jnp.exp(scores - row_peak)
        row_total = lax.optimization_barrier(jnp.sum(exponent, axis=-1))
        weights = exponent.astype(jnp.bfloat16)
        attended = jnp.einsum('hik,khd->ihd', weights.astype(jnp.float32), value_col.astype(jnp.float32))
        attended = attended / jnp.transpose(row_total)[:, :, None]
        return (jax.nn.sigmoid(gate_col) * attended.reshape(row_count, HT * DT)).astype(jnp.bfloat16)
    gated = lax.map(one_column, jnp.arange(col_count, dtype=jnp.int32))
    update = jnp.einsum('jic,cz->ijz', gated.astype(jnp.float32), tri_output_weight.astype(jnp.float32))
    return (pair_cols.astype(jnp.float32) + update).astype(jnp.bfloat16)

def reference(pair_repr, tri_weight, tri_bias_weight, tri_output_weight, samples, levels, single_cond, noise_weight, modulation_weight, attention_weight, pair_bias_weight, output_weight, output_gate_weight):
    normed = normalize(pair_repr).astype(jnp.bfloat16)
    bias_full = jnp.einsum('kiz,zh->hik', normed.astype(jnp.float32), tri_bias_weight.astype(jnp.float32))
    new_pair = attend_columns(pair_repr, bias_full, tri_weight, tri_output_weight)
    pair_renormed = normalize(new_pair).astype(jnp.bfloat16)
    pair_bias = jnp.einsum('ikz,zh->hik', pair_renormed.astype(jnp.float32), pair_bias_weight.astype(jnp.float32))
    features = noise_features(levels).astype(jnp.bfloat16)
    noise_terms = jnp.dot(features, noise_weight, preferred_element_type=jnp.float32)
    conditioned = normalize(single_cond.astype(jnp.float32)[None, :, :] + noise_terms[:, None, :]).astype(jnp.bfloat16)
    modulation = jnp.einsum('stc,cd->std', conditioned.astype(jnp.float32), modulation_weight.astype(jnp.float32))
    adapted = (jax.nn.sigmoid(modulation[..., :CA]) * normalize(samples) + modulation[..., CA:]).astype(jnp.bfloat16)
    out_gate = jax.nn.sigmoid(jnp.einsum('stc,cd->std', conditioned.astype(jnp.float32), output_gate_weight.astype(jnp.float32)))

    def one_sample(inputs):
        adapted_one, gate_one = inputs
        token_count = adapted_one.shape[0]
        projected = jnp.dot(adapted_one, attention_weight, preferred_element_type=jnp.float32)
        query_part = (projected[:, :CA] * DH ** (-0.5)).astype(jnp.bfloat16).reshape(token_count, HD, DH)
        key_part = projected[:, CA:2 * CA].astype(jnp.bfloat16).reshape(token_count, HD, DH)
        value_part = projected[:, 2 * CA:3 * CA].astype(jnp.bfloat16).reshape(token_count, HD, DH)
        gate_part = projected[:, 3 * CA:]
        scores = jnp.einsum('ihd,khd->hik', query_part.astype(jnp.float32), key_part.astype(jnp.float32)) + pair_bias
        row_peak = lax.optimization_barrier(jnp.max(scores, axis=-1, keepdims=True))
        exponent = jnp.exp(scores - row_peak)
        row_total = lax.optimization_barrier(jnp.sum(exponent, axis=-1))
        weights = exponent.astype(jnp.bfloat16)
        attended = jnp.einsum('hik,khd->ihd', weights.astype(jnp.float32), value_part.astype(jnp.float32))
        attended = attended / jnp.transpose(row_total)[:, :, None]
        gated = (jax.nn.sigmoid(gate_part) * attended.reshape(token_count, CA)).astype(jnp.bfloat16)
        projected_out = jnp.dot(gated, output_weight, preferred_element_type=jnp.float32)
        return (gate_one * projected_out).astype(jnp.bfloat16)
    attn_update = lax.map(one_sample, (adapted, out_gate))
    return (new_pair, attn_update)
```

```python
import functools
import math

import jax
import jax.numpy as jnp
from jax import lax
from jax.experimental import pallas as pl
from jax.experimental.pallas import tpu as pltpu
from jax.sharding import PartitionSpec as P

HT = 4
DT = 32
CA = 768
HD = 16
DH = 48
NE = 256
LEVELS = 200

NORM_EPSILON = 1e-05
SIGMA_DATA = 16.0
SIGMA_MAX = 160.0
SIGMA_MIN = 0.0004

VMEM_LIMIT = 60 << 20

F32 = jnp.float32
BF16 = jnp.bfloat16
NT = (((1,), (1,)), ((), ()))


def normalize(values):
    values = values.astype(F32)
    average = jnp.mean(values, axis=-1, keepdims=True)
    centred = values - average
    variance = jnp.mean(centred * centred, axis=-1, keepdims=True)
    return centred * lax.rsqrt(variance + NORM_EPSILON)


def noise_features(levels):
    fraction = levels.astype(F32) / (LEVELS - 1)
    upper_root = SIGMA_MAX ** (1.0 / 7.0)
    lower_root = SIGMA_MIN ** (1.0 / 7.0)
    noise_sigma = SIGMA_DATA * (upper_root + fraction * (lower_root - upper_root)) ** 7
    scaled = 0.25 * jnp.log(noise_sigma / SIGMA_DATA)
    frequency = (
        2.0 * math.pi * jnp.exp(jnp.arange(NE // 2, dtype=F32) * (math.log(100.0) / (NE // 2)))
    )
    angles = scaled[:, None] * frequency[None, :]
    return jnp.concatenate([jnp.cos(angles), jnp.sin(angles)], axis=-1)


def nbytes(*shapes):
    return sum(math.prod(s.shape) * jnp.dtype(s.dtype).itemsize for s in shapes)


def held(operand):
    return pltpu.VMEM(operand.shape, operand.dtype)


def call(kernel, out_shape, operands, scratch=(), copies=0, after=(), flops=0, exps=0):
    in_specs = [pl.BlockSpec(memory_space=pltpu.HBM)] * len(operands)
    in_specs += [pl.BlockSpec(memory_space=pl.ANY)] * len(after)
    moved = nbytes(*operands, *out_shape)
    count = len(operands)

    def body(*refs):
        kernel(*refs[:count], *refs[count + len(after) :])

    return pl.pallas_call(
        body,
        out_shape=out_shape,
        in_specs=in_specs,
        out_specs=tuple(pl.BlockSpec(memory_space=pltpu.HBM) for _ in out_shape),
        scratch_shapes=[*scratch, pltpu.SemaphoreType.DMA((copies,))],
        compiler_params=pltpu.CompilerParams(vmem_limit_bytes=VMEM_LIMIT),
        cost_estimate=pl.CostEstimate(flops=flops, bytes_accessed=moved, transcendentals=exps),
    )(*operands, *after)


def start(pairs, sems, first=0):
    copies = [
        pltpu.make_async_copy(source, target, sems.at[first + at])
        for at, (source, target) in enumerate(pairs)
    ]
    for copy in copies:
        copy.start()
    return copies


def places(high, ranks, lo):
    span = high // ranks
    rest = [(h + lo % ranks * span) % high for h in range(high)]
    if lo % ranks == 0:
        rest = [h // span * span + span - 1 - h % span for h in rest]
    return rest


def turns(high, low):
    slow = sorted(range(high), key=lambda h: (h < high // 2, abs(2 * h - high)))
    return [h * low + lo for h in slow for lo in range(low)]


def hold(value, after):
    return pl.pallas_call(
        lambda *refs: None,
        out_shape=jax.ShapeDtypeStruct(value.shape, value.dtype),
        in_specs=[
            pl.BlockSpec(memory_space=pltpu.HBM),
            pl.BlockSpec(memory_space=pl.ANY),
        ],
        out_specs=pl.BlockSpec(memory_space=pltpu.HBM),
        input_output_aliases={0: 0},
        compiler_params=pltpu.CompilerParams(vmem_limit_bytes=VMEM_LIMIT),
    )(value, after)


def own_place():
    low = lax.axis_size("lo")
    return lax.axis_index("hi") * low + lax.axis_index("lo"), lax.axis_size("hi") * low


def norm_kernel(pair_hbm, weight_hbm, bias_hbm, normed_hbm, pair, weight, wide, bias, normed, sems):
    rows, cols, channels = pair.shape
    pieces = 4
    some = rows // pieces
    slices = [pl.ds(at * some, some) for at in range(pieces)]
    loads = start([(weight_hbm, weight)] + [(pair_hbm.at[h], pair.at[h]) for h in slices], sems)
    for at, load in enumerate(loads[1:]):
        load.wait()
        tile = pair[at * some : (at + 1) * some].astype(F32).reshape(some * cols, channels)
        wide[at * some * cols : (at + 1) * some * cols, :] = normalize(tile)
    loads[0].wait()
    for col in range(cols):
        one = wide[pl.ds(col, rows, stride=cols), :].astype(BF16)
        normed[col] = one
        bias[:, col, :] = lax.dot_general(weight[...], one, NT, preferred_element_type=F32)
    copies = bias_hbm.shape[0]
    pairs = [(bias, bias_hbm.at[at]) for at in range(copies)] + [(normed, normed_hbm)]
    for copy in start(pairs, sems, 1 + pieces):
        copy.wait()


def first_sample(share, each, flip=0):
    return (lax.rem(lax.axis_index("lo"), share) ^ flip) * each


def condition_kernel(share, *refs):
    levels_hbm, cond_hbm, noise_hbm, modulation_hbm, samples_hbm, attention_hbm = refs[:6]
    key_hbm, value_hbm, rows_hbm, cond_rows_hbm = refs[6:10]
    levels, cond, noise, modulation, samples, attention, key, value = refs[10:18]
    adapted, conditions, sems = refs[18:]
    count, tokens, width = samples.shape
    extra = rows_hbm.shape[1]
    first = first_sample(share, count)
    loads = start(
        [
            (levels_hbm, levels),
            (noise_hbm, noise),
            (cond_hbm, cond),
            (modulation_hbm, modulation),
            (samples_hbm.at[pl.ds(first, count)], samples),
            (attention_hbm.at[:, pl.ds(width, width)], attention.at[0]),
            (attention_hbm.at[:, pl.ds(2 * width, width)], attention.at[1]),
        ],
        sems,
    )
    loads[0].wait()
    row = lax.broadcasted_iota(jnp.int32, (8, NE // 2), 0)
    level = jnp.zeros((8, NE // 2), F32)
    for sample in range(count):
        level = jnp.where(row == sample, levels[first + sample].astype(F32), level)
    fraction = level / (LEVELS - 1)
    upper_root = SIGMA_MAX ** (1.0 / 7.0)
    lower_root = SIGMA_MIN ** (1.0 / 7.0)
    root = upper_root + fraction * (lower_root - upper_root)
    square = root * root
    sigma = SIGMA_DATA * (square * square * square * root)
    scaled = 0.25 * jnp.log(sigma / SIGMA_DATA)
    step = lax.broadcasted_iota(jnp.int32, scaled.shape, 1).astype(F32)
    angles = scaled * (2.0 * math.pi * jnp.exp(step * (math.log(100.0) / (NE // 2))))
    features = jnp.concatenate([jnp.cos(angles), jnp.sin(angles)], axis=-1).astype(BF16)
    loads[1].wait()
    terms = jnp.dot(features, noise[...], preferred_element_type=F32)
    for load in loads[2:4]:
        load.wait()

    loads[4].wait()
    for sample in range(count):
        trunk = cond[...].astype(F32) + terms[sample : sample + 1]
        conditioned = normalize(trunk).astype(BF16)
        conditions[sample] = conditioned
        modulated = jnp.dot(conditioned, modulation[...], preferred_element_type=F32)
        gain = jax.nn.sigmoid(modulated[:, :width])
        one = gain * normalize(samples[sample]) + modulated[:, width:]
        adapted[sample] = one.astype(BF16)
    place, places = own_place()
    chip = lax.div(lax.axis_index("row") * places + place, share) * extra
    here = pl.ds(pl.multiple_of(chip, extra), extra)
    stores = start(
        [(adapted.at[:, here], rows_hbm), (conditions.at[:, here], cond_rows_hbm)], sems, 7
    )
    for at, (part, target) in enumerate(((key, key_hbm), (value, value_hbm))):
        loads[5 + at].wait()
        for sample in range(count):
            part[sample] = jnp.dot(
                adapted[sample], attention[at], preferred_element_type=F32
            ).astype(BF16)
        stores += start([(part, target)], sems, 9 + at)
    for store in stores:
        store.wait()


def token_kernel(share, *refs):
    attention_hbm, gate_hbm, rows_hbm, cond_hbm, key_hbm = refs[:5]
    targets, refs = refs[5 : 5 + share], refs[5 + share :]
    attention, gate_weight, rows, cond, key, found, wide, sems = refs
    count, tokens, width = key.shape
    extra = rows.shape[1]
    own = extra // share
    loads = start(
        [
            (rows_hbm, rows),
            (attention_hbm.at[:, pl.ds(0, width)], attention.at[0]),
            (key_hbm, key),
            (attention_hbm.at[:, pl.ds(3 * width, width)], attention.at[1]),
            (cond_hbm, cond),
            (gate_hbm, gate_weight),
        ],
        sems,
    )
    for load in loads[:2]:
        load.wait()
    flat = rows[...].reshape(count * extra, width)
    raw = jnp.dot(flat, attention[0], preferred_element_type=F32)
    query = (raw * DH ** (-0.5)).astype(BF16).astype(F32)
    masks = head_masks(width)
    loads[2].wait()
    for sample in range(count):
        stacked = []
        for core in range(share):
            at = sample * extra + core * own
            one = query[at : at + own]
            stacked += [jnp.where(m, one, 0.0) for m in masks]
        stacked = jnp.concatenate(stacked, axis=0).astype(BF16)
        raw = lax.dot_general(key[sample], stacked, NT, preferred_element_type=F32)
        for core in range(share):
            found[core, sample, :tokens, :] = raw[:, core * HD * own : (core + 1) * HD * own]
    loads[3].wait()
    wide[0] = jax.nn.sigmoid(jnp.dot(flat, attention[1], preferred_element_type=F32))
    for load in loads[4:]:
        load.wait()
    flat = cond[...].reshape(count * extra, cond.shape[2])
    wide[1] = jax.nn.sigmoid(jnp.dot(flat, gate_weight[...], preferred_element_type=F32))
    lanes = found.shape[3]
    for core in range(share):
        for sample in range(count):
            at = sample * extra + core * own
            to = tokens
            for kind in range(2):
                for lane in range(0, width, lanes):
                    found[core, sample, to : to + own, :] = wide[
                        kind, at : at + own, lane : lane + lanes
                    ]
                    to += own
    mine = lax.rem(lax.axis_index("lo"), share)
    stores = start(
        [(found.at[mine ^ flip], targets[flip]) for flip in range(share)], sems, len(loads)
    )
    for store in stores:
        store.wait()


def triangle_kernel(ranks, low, *refs):
    pair_hbm, weight_hbm, out_weight_hbm, bias_weight_hbm = refs[:4]
    gathered_hbm, refs = refs[4 : 4 + low], refs[4 + low :]
    normed_hbm, refs = refs[:ranks], refs[ranks:]
    new_hbm, pair_bias_hbm, refs = refs[0], refs[1], refs[2:]
    pair, weight, out_weight, bias_weight = refs[:4]
    gathered, normed, new, pair_bias, refs = refs[4], refs[5], refs[6], refs[7], refs[8:]
    bias_rows, bias, query, key, value, gate, wide = refs[:7]
    slots, sems = (refs[7:10], refs[10:13]), refs[13]
    rows, cols, channels = pair.shape
    width = HT * DT
    span = gathered.shape[2]
    loads = start(
        [
            (weight_hbm, weight),
            *[(normed_hbm[at], normed.at[at]) for at in range(ranks)],
            *[(gathered_hbm[at], gathered.at[at]) for at in range(low)],
            (pair_hbm, pair),
            (out_weight_hbm, out_weight),
            (bias_weight_hbm, bias_weight),
        ],
        sems,
    )
    for load in loads[: 1 + ranks + low]:
        load.wait()
    row, fast = lax.axis_index("row"), lax.axis_index("lo")
    for flip in range(low):
        for slow in range(span):
            sender = fast ^ flip
            block = jnp.where(lax.rem(sender, ranks) == 0, span - 1 - slow, slow)
            first = pl.multiple_of((block * low + sender) * cols, cols)
            for source in range(ranks):
                step = lax.rem(source + ranks - row, ranks)
                bias_rows[step, :, pl.ds(first, cols), :] = gathered[flip, source, slow]
    turned = jnp.transpose(weight[...].astype(F32)).astype(BF16)
    own_lines = jnp.concatenate([turned[:width], turned[2 * width :]], axis=0)
    peer_lines = turned[2 * width : 3 * width]
    batch = 4
    tiles = [(step, head) for step in range(ranks) for head in range(HT)]
    groups = cols // batch
    for group in range(groups):
        at = group * batch
        for step in range(ranks):
            some = normed[step, at : at + batch].reshape(batch * rows, channels)
            here = slice(step * rows, (step + 1) * rows)
            raw = jnp.dot(some, weight[:, width : 2 * width], preferred_element_type=F32)
            key[at : at + batch, here, :] = raw.astype(BF16).reshape(batch, rows, width)
            lines = own_lines if step == 0 else peer_lines
            raw = lax.dot_general(lines, some, NT, preferred_element_type=F32)
            for side in range(batch):
                part = raw[:, side * rows : (side + 1) * rows]
                if step == 0:
                    query[at + side] = (part[:width] * DT ** (-0.5)).astype(BF16)
                    gate[at + side] = jax.nn.sigmoid(part[2 * width :])
                    part = part[width : 2 * width]
                value[at + side, :, here] = part.astype(BF16)
        for step, head in tiles[group::groups]:
            bias[step * rows : (step + 1) * rows, head * rows : (head + 1) * rows] = jnp.transpose(
                bias_rows[step, head]
            )
    for load in loads[1 + ranks + low :]:
        load.wait()

    def score(col, slot):
        scores, peak, _ = slots[slot]
        own = query[col]
        blocks = []
        for head in range(HT):
            zeros = [jnp.zeros((size, rows), BF16) for size in (head * DT, width - (head + 1) * DT)]
            block = [zeros[0], own[head * DT : (head + 1) * DT], zeros[1]]
            blocks.append(jnp.concatenate([b for b in block if b.shape[0]], axis=0))
        stacked = jnp.concatenate(blocks, axis=1)
        raw = jnp.dot(key[col], stacked, preferred_element_type=F32) + bias[...]
        scores[...] = raw
        peak[...] = jnp.max(raw, axis=0, keepdims=True)

    def attend(col, slot):
        scores, peak, weights = slots[slot]
        exponent = jnp.exp(scores[...] - peak[...])
        scale = 1.0 / jnp.sum(exponent, axis=0, keepdims=True)
        weights[...] = exponent.astype(BF16)
        parts = []
        for head in range(0, HT, 2):
            here = slice(head * rows, (head + 2) * rows)
            summed = jnp.dot(
                value[col, head * DT : (head + 2) * DT, :],
                weights[:, here],
                preferred_element_type=F32,
            )
            summed = summed * scale[:, here]
            parts += [summed[:DT, :rows], summed[DT:, rows:]]
        gated = (gate[col] * jnp.concatenate(parts, axis=0)).astype(BF16)
        wide[pl.ds(col, rows, stride=cols), :] = lax.dot_general(
            gated, out_weight[...], (((0,), (0,)), ((), ())), preferred_element_type=F32
        )

    score(0, 0)

    @pl.loop(0, cols // batch)
    def _(group):
        for side in range(batch):
            col = group * batch + side
            score(jnp.minimum(col + 1, cols - 1), (side + 1) % 2)
            attend(col, side % 2)

    updated = (pair[...].astype(F32).reshape(rows * cols, channels) + wide[...]).astype(BF16)
    new[...] = updated.reshape(rows, cols, channels)
    stores = start([(new, new_hbm)], sems, len(loads))
    owners, _, lanes = pair_bias.shape
    own = rows // owners
    lane = lax.broadcasted_iota(jnp.int32, (lanes, HD), 0)
    pick = (lane // own == lax.broadcasted_iota(jnp.int32, (lanes, HD), 1)).astype(BF16)
    spread = jnp.dot(pick, bias_weight[...], preferred_element_type=F32)
    token_of = lax.rem(lax.broadcasted_iota(jnp.int32, (lanes, channels), 0), own)
    renormed = normalize(updated).astype(BF16).reshape(owners, own, cols, channels)
    total = jnp.zeros((owners * cols, lanes), F32)
    for token in range(own):
        total += lax.dot_general(
            renormed[:, token].reshape(owners * cols, channels),
            jnp.where(token_of == token, spread, 0.0).astype(BF16),
            NT,
            preferred_element_type=F32,
        )
    total = total.reshape(owners, cols, lanes)
    for place, owner in enumerate(turns(owners // low, low)):
        pair_bias[place] = total[owner]
    stores += start([(pair_bias, pair_bias_hbm)], sems, len(loads) + 1)
    for store in stores:
        store.wait()


def head_masks(width):
    lane = lax.broadcasted_iota(jnp.int32, (1, width), 1)
    return [(lane >= head * DH) & (lane < (head + 1) * DH) for head in range(HD)]


def attend_kernel(share, *refs):
    bias_hbm, weight_hbm = refs[:2]
    found_hbm, value_hbm, refs = refs[2 : 2 + share], refs[2 + share : 2 + 2 * share], refs[2 + 2 * share :]
    out_hbm, bias, weight, found, value, out, sems = refs
    count, tokens, wider = value.shape
    width = weight.shape[0]
    each = count // share
    own = out.shape[0] // count
    value[:, :, width:] = jnp.ones((count, tokens, wider - width), BF16)
    firsts = [first_sample(share, each, flip) for flip in range(share)]
    loads = start(
        [
            (bias_hbm, bias),
            *[(found_hbm[flip], found.at[pl.ds(firsts[flip], each)]) for flip in range(share)],
            *[
                (value_hbm[flip].at[at], value.at[firsts[flip] + at, :, pl.ds(0, width)])
                for flip in range(share)
                for at in range(each)
            ],
            (weight_hbm, weight),
        ],
        sems,
    )
    for load in loads[: 1 + share]:
        load.wait()
    low = lax.axis_size("lo")
    order = turns(bias.shape[0] // low, low)
    turned = jnp.concatenate([bias[order.index(c)] for c in range(len(order))], axis=0)
    masks = head_masks(width)
    weights = []
    for sample in range(count):
        total_scores = found[sample, :tokens] + turned
        peak = jnp.max(total_scores, axis=0, keepdims=True)
        weights.append(jnp.exp(total_scores - peak).astype(BF16))
    rows = []
    for sample in range(count):
        if sample == 0:
            for load in loads[1 + share : 1 + share + count]:
                load.wait()
        summed = lax.dot_general(
            weights[sample], value[sample], (((0,), (0,)), ((), ())), preferred_element_type=F32
        )
        scale = 1.0 / summed[:, width : width + 1]
        summed = summed[:, :width] * scale
        attended = jnp.where(masks[0], summed[:own], 0.0)
        for head in range(1, HD):
            attended = jnp.where(masks[head], summed[head * own : (head + 1) * own], attended)
        rows.append(attended)

    def gates(kind):
        parts = []
        lanes = found.shape[2]
        for sample in range(count):
            first = tokens + kind * own * (width // lanes)
            blocks = [
                found[sample, first + at * own : first + (at + 1) * own]
                for at in range(width // lanes)
            ]
            parts.append(jnp.concatenate(blocks, axis=1))
        return jnp.concatenate(parts, axis=0)

    loads[-1].wait()
    gated = (gates(0) * jnp.concatenate(rows, axis=0)).astype(BF16)
    projected = jnp.dot(gated, weight[...], preferred_element_type=F32)
    out[...] = (gates(1) * projected).astype(BF16)
    for store in start([(out, out_hbm)], sems, len(loads)):
        store.wait()


def local(
    pair_repr,
    tri_weight,
    tri_bias_weight,
    tri_output_weight,
    samples,
    levels,
    single_cond,
    noise_weight,
    modulation_weight,
    attention_weight,
    pair_bias_weight,
    output_weight,
    output_gate_weight,
):
    rows, cols, channels = pair_repr.shape
    ranks, high, low = (lax.axis_size(name) for name in ("row", "hi", "lo"))
    col_count = high * low
    sample_count, tokens, width = samples.shape
    own = rows // col_count
    span = high // ranks
    keys = ranks * rows
    shape = jax.ShapeDtypeStruct

    turned = jnp.transpose(tri_bias_weight)
    normed_shape = shape((cols, rows, channels), BF16)
    bias_shape = shape((HT, cols, rows), F32)
    wide = pltpu.VMEM((rows * cols, channels), F32)
    copies_shape = shape((ranks * high, *bias_shape.shape), F32)
    bias, normed = call(
        norm_kernel,
        (copies_shape, normed_shape),
        (pair_repr, turned),
        scratch=(held(pair_repr), held(turned), wide, held(bias_shape), held(normed_shape)),
        copies=6 + ranks * high,
        flops=2 * rows * cols * channels * HT,
    )
    groups = [
        [
            (r * high + h) * low + lo
            for r in range(ranks)
            for h in places(high, ranks, lo)
        ]
        for lo in range(low)
    ]
    placed = lax.all_to_all(
        bias, ("row", "hi", "lo"), split_axis=0, concat_axis=0, axis_index_groups=groups
    )
    peers = [
        lax.ppermute(normed, "row", [((r + step) % ranks, r) for r in range(ranks)])
        for step in range(1, ranks)
    ]

    share = 2 if low % 2 == 0 and sample_count % 2 == 0 else 1
    each = sample_count // share
    part = (each, tokens, width)
    extra = share * own
    conditions = single_cond.shape[1]
    key, value, own_rows, cond_rows = call(
        functools.partial(condition_kernel, share),
        (
            shape(part, BF16),
            shape(part, BF16),
            shape((each, extra, width), BF16),
            shape((each, extra, conditions), BF16),
        ),
        (
            levels,
            single_cond,
            noise_weight,
            modulation_weight,
            samples,
            attention_weight,
        ),
        scratch=(
            pltpu.SMEM(levels.shape, levels.dtype),
            held(single_cond),
            held(noise_weight),
            held(modulation_weight),
            pltpu.VMEM(part, BF16),
            pltpu.VMEM((2, width, width), BF16),
            pltpu.VMEM(part, BF16),
            pltpu.VMEM(part, BF16),
            pltpu.VMEM(part, BF16),
            pltpu.VMEM((each, *single_cond.shape), BF16),
        ),
        copies=11,
        after=(bias,),
        flops=4 * each * tokens * width * 2 * width,
        exps=each * tokens * width,
    )
    placed = placed.reshape(ranks, high, *bias_shape.shape)
    place = lax.axis_index("row") + ranks - lax.rem(lax.axis_index("lo"), ranks)
    gathered = [lax.dynamic_slice_in_dim(placed, lax.rem(place, ranks) * span, span, 1)]
    found_shape = shape((each, tokens + 2 * width // HD, HD * own), F32)
    found = list(
        call(
            functools.partial(token_kernel, share),
            (found_shape,) * share,
            (attention_weight, output_gate_weight, own_rows, cond_rows, key),
            scratch=(
                pltpu.VMEM((2, width, width), BF16),
                held(output_gate_weight),
                held(own_rows),
                held(cond_rows),
                held(key),
                pltpu.VMEM((share, *found_shape.shape), F32),
                pltpu.VMEM((2, each * extra, width), F32),
            ),
            copies=6 + share,
            after=(gathered[0],),
            flops=64 * rows * cols * channels * HT * DT,
        )
    )
    bit = low // 2
    while bit:
        flip = [(c ^ bit, c) for c in range(low)]
        ready = [gathered[0], *(hold(part, found[0]) for part in gathered[1:])]
        more = [lax.ppermute(part, "lo", flip) for part in ready]
        gathered = [part for both in zip(ready, more) for part in both]
        bit //= 2
    values = [value]
    if share == 2:
        other = [(c ^ 1, c) for c in range(low)]
        values.append(lax.ppermute(value, "lo", other))
        found[1] = lax.ppermute(found[1], "lo", other)

    pair_weight = jnp.transpose(pair_bias_weight)
    outs = (shape((rows, cols, channels), BF16), shape((col_count, cols, HD * own), F32))
    new_pair, pair_bias = call(
        functools.partial(triangle_kernel, ranks, low),
        outs,
        (
            pair_repr,
            tri_weight,
            tri_output_weight,
            pair_weight,
            *gathered,
            normed,
            *peers,
        ),
        scratch=(
            held(pair_repr),
            held(tri_weight),
            held(tri_output_weight),
            held(pair_weight),
            pltpu.VMEM((low, ranks, span, HT, cols, rows), F32),
            pltpu.VMEM((ranks, cols, rows, channels), BF16),
            held(outs[0]),
            held(outs[1]),
            pltpu.VMEM((ranks, HT, rows, rows), F32),
            pltpu.VMEM((keys, HT * rows), F32),
            pltpu.VMEM((cols, HT * DT, rows), BF16),
            pltpu.VMEM((cols, keys, HT * DT), BF16),
            pltpu.VMEM((cols, HT * DT, keys), BF16),
            pltpu.VMEM((cols, HT * DT, rows), F32),
            wide,
            *[
                pltpu.VMEM(*slot)
                for slot in (
                    ((keys, HT * rows), F32),
                    ((1, HT * rows), F32),
                    ((keys, HT * rows), BF16),
                )
                * 2
            ],
        ),
        copies=6 + ranks + low,
        after=(found[0],),
        flops=4 * HT * rows * cols * keys * HT * DT,
        exps=HT * rows * cols * keys,
    )
    own_bias = lax.all_to_all(
        pair_bias, ("hi", "lo"), split_axis=0, concat_axis=0, axis_index_groups=[turns(high, low)]
    )

    outs = (shape((sample_count * own, width), BF16),)
    (attn_update,) = call(
        functools.partial(attend_kernel, share),
        outs,
        (own_bias, output_weight, *found, *values),
        scratch=(
            held(own_bias),
            held(output_weight),
            pltpu.VMEM((sample_count, *found_shape.shape[1:]), F32),
            pltpu.VMEM((sample_count, tokens, width + 128), BF16),
            held(outs[0]),
        ),
        copies=3 + share + sample_count,
        flops=2 * sample_count * HD * own * tokens * width,
        exps=sample_count * HD * own * tokens,
    )
    return (new_pair, attn_update.reshape(sample_count, own, width))


def solution(mesh):
    ranks, col_count, groups = (mesh.shape[name] for name in ("row", "col", "smp"))
    low = math.gcd(col_count // ranks, 4)
    finer = jax.sharding.Mesh(
        mesh.devices.reshape(ranks, col_count // low, low, groups), ("row", "hi", "lo", "smp")
    )
    tile = P("row", ("hi", "lo"), None)
    return jax.shard_map(
        local,
        mesh=finer,
        in_specs=(tile, P(), P(), P(), P("smp", None, None), P("smp"), *[P()] * 7),
        out_specs=(tile, P("smp", ("row", "hi", "lo"), None)),
        check_vma=False,
    )
```

```python
import functools
import math

import jax
import jax.numpy as jnp
from jax import lax
from jax.experimental import pallas as pl
from jax.experimental.pallas import tpu as pltpu
from jax.sharding import PartitionSpec as P

HT = 4
DT = 32
CA = 768
HD = 16
DH = 48
NE = 256
LEVELS = 200

NORM_EPSILON = 1e-05
SIGMA_DATA = 16.0
SIGMA_MAX = 160.0
SIGMA_MIN = 0.0004

VMEM_LIMIT = 60 << 20
NEAR_LIMIT = 48 << 20

F32 = jnp.float32
BF16 = jnp.bfloat16
NT = (((1,), (1,)), ((), ()))


def normalize(values):
    values = values.astype(F32)
    average = jnp.mean(values, axis=-1, keepdims=True)
    centred = values - average
    variance = jnp.mean(centred * centred, axis=-1, keepdims=True)
    return centred * lax.rsqrt(variance + NORM_EPSILON)


def noise_features(levels):
    fraction = levels.astype(F32) / (LEVELS - 1)
    upper_root = SIGMA_MAX ** (1.0 / 7.0)
    lower_root = SIGMA_MIN ** (1.0 / 7.0)
    noise_sigma = SIGMA_DATA * (upper_root + fraction * (lower_root - upper_root)) ** 7
    scaled = 0.25 * jnp.log(noise_sigma / SIGMA_DATA)
    frequency = (
        2.0 * math.pi * jnp.exp(jnp.arange(NE // 2, dtype=F32) * (math.log(100.0) / (NE // 2)))
    )
    angles = scaled[:, None] * frequency[None, :]
    return jnp.concatenate([jnp.cos(angles), jnp.sin(angles)], axis=-1)


def nbytes(*shapes):
    return sum(math.prod(s.shape) * jnp.dtype(s.dtype).itemsize for s in shapes)


def held(operand):
    return pltpu.VMEM(operand.shape, operand.dtype)


def call(kernel, out_shape, operands, scratch=(), copies=0, after=(), near=False, flops=0, exps=0):
    in_specs = [pl.BlockSpec(memory_space=pltpu.VMEM if near else pltpu.HBM)] * len(operands)
    in_specs += [pl.BlockSpec(memory_space=pl.ANY)] * len(after)
    moved = nbytes(*operands, *out_shape)
    count = len(operands)

    def body(*refs):
        kernel(*refs[:count], *refs[count + len(after) :])

    return pl.pallas_call(
        body,
        out_shape=out_shape,
        in_specs=in_specs,
        out_specs=tuple(pl.BlockSpec(memory_space=pltpu.HBM) for _ in out_shape),
        scratch_shapes=[*scratch, pltpu.SemaphoreType.DMA((copies,))],
        compiler_params=pltpu.CompilerParams(vmem_limit_bytes=NEAR_LIMIT if near else VMEM_LIMIT),
        cost_estimate=pl.CostEstimate(flops=flops, bytes_accessed=moved, transcendentals=exps),
    )(*operands, *after)


def start(pairs, sems, first=0):
    copies = [
        pltpu.make_async_copy(source, target, sems.at[first + at])
        for at, (source, target) in enumerate(pairs)
    ]
    for copy in copies:
        copy.start()
    return copies


def places(high, ranks, lo):
    span = high // ranks
    rest = [(h + lo % ranks * span) % high for h in range(high)]
    if lo % ranks == 0:
        rest = [h // span * span + span - 1 - h % span for h in rest]
    return rest


def turns(high, low):
    slow = sorted(range(high), key=lambda h: (h < high // 2, abs(2 * h - high)))
    return [h * low + lo for h in slow for lo in range(low)]


def hold(value, after):
    return pl.pallas_call(
        lambda *refs: None,
        out_shape=jax.ShapeDtypeStruct(value.shape, value.dtype),
        in_specs=[
            pl.BlockSpec(memory_space=pltpu.HBM),
            pl.BlockSpec(memory_space=pl.ANY),
        ],
        out_specs=pl.BlockSpec(memory_space=pltpu.HBM),
        input_output_aliases={0: 0},
        compiler_params=pltpu.CompilerParams(vmem_limit_bytes=VMEM_LIMIT),
    )(value, after)


def own_place():
    low = lax.axis_size("lo")
    return lax.axis_index("hi") * low + lax.axis_index("lo"), lax.axis_size("hi") * low


def norm_kernel(pair_hbm, weight_hbm, bias_hbm, normed_hbm, pair, weight, wide, bias, normed, sems):
    rows, cols, channels = pair.shape
    pieces = 4
    some = rows // pieces
    slices = [pl.ds(at * some, some) for at in range(pieces)]
    loads = start([(weight_hbm, weight)] + [(pair_hbm.at[h], pair.at[h]) for h in slices], sems)
    for at, load in enumerate(loads[1:]):
        load.wait()
        tile = pair[at * some : (at + 1) * some].astype(F32).reshape(some * cols, channels)
        wide[at * some * cols : (at + 1) * some * cols, :] = normalize(tile)
    loads[0].wait()
    for col in range(cols):
        one = wide[pl.ds(col, rows, stride=cols), :].astype(BF16)
        normed[col] = one
        bias[:, col, :] = lax.dot_general(weight[...], one, NT, preferred_element_type=F32)
    copies = bias_hbm.shape[0]
    pairs = [(bias, bias_hbm.at[at]) for at in range(copies)] + [(normed, normed_hbm)]
    for copy in start(pairs, sems, 1 + pieces):
        copy.wait()


def first_sample(share, each, flip=0):
    return (lax.rem(lax.axis_index("lo"), share) ^ flip) * each


def condition_kernel(share, *refs):
    levels_hbm, cond_hbm, noise_hbm, modulation_hbm, samples_hbm, attention_hbm = refs[:6]
    key_hbm, value_hbm, rows_hbm, cond_rows_hbm = refs[6:10]
    levels, cond, noise, modulation, samples, attention, key, value = refs[10:18]
    adapted, conditions, sems = refs[18:]
    count, tokens, width = samples.shape
    extra = rows_hbm.shape[1]
    first = first_sample(share, count)
    loads = start(
        [
            (levels_hbm, levels),
            (noise_hbm, noise),
            (cond_hbm, cond),
            (modulation_hbm, modulation),
            (samples_hbm.at[pl.ds(first, count)], samples),
            (attention_hbm.at[:, pl.ds(width, width)], attention.at[0]),
            (attention_hbm.at[:, pl.ds(2 * width, width)], attention.at[1]),
        ],
        sems,
    )
    loads[0].wait()
    row = lax.broadcasted_iota(jnp.int32, (8, NE // 2), 0)
    level = jnp.zeros((8, NE // 2), F32)
    for sample in range(count):
        level = jnp.where(row == sample, levels[first + sample].astype(F32), level)
    fraction = level / (LEVELS - 1)
    upper_root = SIGMA_MAX ** (1.0 / 7.0)
    lower_root = SIGMA_MIN ** (1.0 / 7.0)
    root = upper_root + fraction * (lower_root - upper_root)
    square = root * root
    sigma = SIGMA_DATA * (square * square * square * root)
    scaled = 0.25 * jnp.log(sigma / SIGMA_DATA)
    step = lax.broadcasted_iota(jnp.int32, scaled.shape, 1).astype(F32)
    angles = scaled * (2.0 * math.pi * jnp.exp(step * (math.log(100.0) / (NE // 2))))
    features = jnp.concatenate([jnp.cos(angles), jnp.sin(angles)], axis=-1).astype(BF16)
    loads[1].wait()
    terms = jnp.dot(features, noise[...], preferred_element_type=F32)
    for load in loads[2:4]:
        load.wait()

    loads[4].wait()
    for sample in range(count):
        trunk = cond[...].astype(F32) + terms[sample : sample + 1]
        conditioned = normalize(trunk).astype(BF16)
        conditions[sample] = conditioned
        modulated = jnp.dot(conditioned, modulation[...], preferred_element_type=F32)
        gain = jax.nn.sigmoid(modulated[:, :width])
        one = gain * normalize(samples[sample]) + modulated[:, width:]
        adapted[sample] = one.astype(BF16)
    place, places = own_place()
    chip = lax.div(lax.axis_index("row") * places + place, share) * extra
    here = pl.ds(pl.multiple_of(chip, extra), extra)
    stores = start(
        [(adapted.at[:, here], rows_hbm), (conditions.at[:, here], cond_rows_hbm)], sems, 7
    )
    for at, (part, target) in enumerate(((key, key_hbm), (value, value_hbm))):
        loads[5 + at].wait()
        for sample in range(count):
            part[sample] = jnp.dot(
                adapted[sample], attention[at], preferred_element_type=F32
            ).astype(BF16)
        stores += start([(part, target)], sems, 9 + at)
    for store in stores:
        store.wait()


def token_kernel(share, *refs):
    attention_hbm, gate_hbm, rows_hbm, cond_hbm, key_hbm = refs[:5]
    targets, refs = refs[5 : 5 + share], refs[5 + share :]
    attention, gate_weight, rows, cond, key, found, wide, sems = refs
    count, tokens, width = key.shape
    extra = rows.shape[1]
    own = extra // share
    loads = start(
        [
            (rows_hbm, rows),
            (attention_hbm.at[:, pl.ds(0, width)], attention.at[0]),
            (key_hbm, key),
            (attention_hbm.at[:, pl.ds(3 * width, width)], attention.at[1]),
            (cond_hbm, cond),
            (gate_hbm, gate_weight),
        ],
        sems,
    )
    for load in loads[:2]:
        load.wait()
    flat = rows[...].reshape(count * extra, width)
    raw = jnp.dot(flat, attention[0], preferred_element_type=F32)
    query = (raw * DH ** (-0.5)).astype(BF16).astype(F32)
    masks = head_masks(width)
    loads[2].wait()
    for sample in range(count):
        stacked = []
        for core in range(share):
            at = sample * extra + core * own
            one = query[at : at + own]
            stacked += [jnp.where(m, one, 0.0) for m in masks]
        stacked = jnp.concatenate(stacked, axis=0).astype(BF16)
        raw = lax.dot_general(key[sample], stacked, NT, preferred_element_type=F32)
        for core in range(share):
            found[core, sample, :tokens, :] = raw[:, core * HD * own : (core + 1) * HD * own]
    loads[3].wait()
    wide[0] = jax.nn.sigmoid(jnp.dot(flat, attention[1], preferred_element_type=F32))
    for load in loads[4:]:
        load.wait()
    flat = cond[...].reshape(count * extra, cond.shape[2])
    wide[1] = jax.nn.sigmoid(jnp.dot(flat, gate_weight[...], preferred_element_type=F32))
    lanes = found.shape[3]
    for core in range(share):
        for sample in range(count):
            at = sample * extra + core * own
            to = tokens
            for kind in range(2):
                for lane in range(0, width, lanes):
                    found[core, sample, to : to + own, :] = wide[
                        kind, at : at + own, lane : lane + lanes
                    ]
                    to += own
    mine = lax.rem(lax.axis_index("lo"), share)
    stores = start(
        [(found.at[mine ^ flip], targets[flip]) for flip in range(share)], sems, len(loads)
    )
    for store in stores:
        store.wait()


def triangle_kernel(ranks, low, *refs):
    pair_hbm, weight_hbm, out_weight_hbm, bias_weight_hbm = refs[:4]
    gathered_hbm, refs = refs[4 : 4 + low], refs[4 + low :]
    normed_hbm, refs = refs[:ranks], refs[ranks:]
    new_hbm, pair_bias_hbm, refs = refs[0], refs[1], refs[2:]
    pair, weight, out_weight, bias_weight = refs[:4]
    gathered, normed, new, pair_bias, refs = refs[4], refs[5], refs[6], refs[7], refs[8:]
    bias_rows, bias, query, key, value, gate, wide = refs[:7]
    slots, sems = (refs[7:10], refs[10:13]), refs[13]
    rows, cols, channels = pair.shape
    width = HT * DT
    span = gathered.shape[2]
    loads = start(
        [
            (weight_hbm, weight),
            *[(normed_hbm[at], normed.at[at]) for at in range(ranks)],
            *[(gathered_hbm[at], gathered.at[at]) for at in range(low)],
            (pair_hbm, pair),
            (out_weight_hbm, out_weight),
            (bias_weight_hbm, bias_weight),
        ],
        sems,
    )
    for load in loads[: 1 + ranks + low]:
        load.wait()
    row, fast = lax.axis_index("row"), lax.axis_index("lo")
    for flip in range(low):
        for slow in range(span):
            sender = fast ^ flip
            block = jnp.where(lax.rem(sender, ranks) == 0, span - 1 - slow, slow)
            first = pl.multiple_of((block * low + sender) * cols, cols)
            for source in range(ranks):
                step = lax.rem(source + ranks - row, ranks)
                bias_rows[step, :, pl.ds(first, cols), :] = gathered[flip, source, slow]
    turned = jnp.transpose(weight[...].astype(F32)).astype(BF16)
    own_lines = jnp.concatenate([turned[:width], turned[2 * width :]], axis=0)
    peer_lines = turned[2 * width : 3 * width]
    batch = 4
    tiles = [(step, head) for step in range(ranks) for head in range(HT)]
    groups = cols // batch
    for group in range(groups):
        at = group * batch
        for step in range(ranks):
            some = normed[step, at : at + batch].reshape(batch * rows, channels)
            here = slice(step * rows, (step + 1) * rows)
            raw = jnp.dot(some, weight[:, width : 2 * width], preferred_element_type=F32)
            key[at : at + batch, here, :] = raw.astype(BF16).reshape(batch, rows, width)
            lines = own_lines if step == 0 else peer_lines
            raw = lax.dot_general(lines, some, NT, preferred_element_type=F32)
            for side in range(batch):
                part = raw[:, side * rows : (side + 1) * rows]
                if step == 0:
                    query[at + side] = (part[:width] * DT ** (-0.5)).astype(BF16)
                    gate[at + side] = jax.nn.sigmoid(part[2 * width :])
                    part = part[width : 2 * width]
                value[at + side, :, here] = part.astype(BF16)
        for step, head in tiles[group::groups]:
            bias[step * rows : (step + 1) * rows, head * rows : (head + 1) * rows] = jnp.transpose(
                bias_rows[step, head]
            )
    for load in loads[1 + ranks + low :]:
        load.wait()

    def score(col, slot):
        scores, peak, _ = slots[slot]
        own = query[col]
        blocks = []
        for head in range(HT):
            zeros = [jnp.zeros((size, rows), BF16) for size in (head * DT, width - (head + 1) * DT)]
            block = [zeros[0], own[head * DT : (head + 1) * DT], zeros[1]]
            blocks.append(jnp.concatenate([b for b in block if b.shape[0]], axis=0))
        stacked = jnp.concatenate(blocks, axis=1)
        raw = jnp.dot(key[col], stacked, preferred_element_type=F32) + bias[...]
        scores[...] = raw
        peak[...] = jnp.max(raw, axis=0, keepdims=True)

    def attend(col, slot):
        scores, peak, weights = slots[slot]
        exponent = jnp.exp(scores[...] - peak[...])
        scale = 1.0 / jnp.sum(exponent, axis=0, keepdims=True)
        weights[...] = exponent.astype(BF16)
        parts = []
        for head in range(0, HT, 2):
            here = slice(head * rows, (head + 2) * rows)
            summed = jnp.dot(
                value[col, head * DT : (head + 2) * DT, :],
                weights[:, here],
                preferred_element_type=F32,
            )
            summed = summed * scale[:, here]
            parts += [summed[:DT, :rows], summed[DT:, rows:]]
        gated = (gate[col] * jnp.concatenate(parts, axis=0)).astype(BF16)
        wide[pl.ds(col, rows, stride=cols), :] = lax.dot_general(
            gated, out_weight[...], (((0,), (0,)), ((), ())), preferred_element_type=F32
        )

    score(0, 0)

    @pl.loop(0, cols // batch)
    def _(group):
        for side in range(batch):
            col = group * batch + side
            score(jnp.minimum(col + 1, cols - 1), (side + 1) % 2)
            attend(col, side % 2)

    updated = (pair[...].astype(F32).reshape(rows * cols, channels) + wide[...]).astype(BF16)
    new[...] = updated.reshape(rows, cols, channels)
    stores = start([(new, new_hbm)], sems, len(loads))
    owners, _, lanes = pair_bias.shape
    own = rows // owners
    lane = lax.broadcasted_iota(jnp.int32, (lanes, HD), 0)
    pick = (lane // own == lax.broadcasted_iota(jnp.int32, (lanes, HD), 1)).astype(BF16)
    spread = jnp.dot(pick, bias_weight[...], preferred_element_type=F32)
    token_of = lax.rem(lax.broadcasted_iota(jnp.int32, (lanes, channels), 0), own)
    renormed = normalize(updated).astype(BF16).reshape(owners, own, cols, channels)
    total = jnp.zeros((owners * cols, lanes), F32)
    for token in range(own):
        total += lax.dot_general(
            renormed[:, token].reshape(owners * cols, channels),
            jnp.where(token_of == token, spread, 0.0).astype(BF16),
            NT,
            preferred_element_type=F32,
        )
    total = total.reshape(owners, cols, lanes)
    for place, owner in enumerate(turns(owners // low, low)):
        pair_bias[place] = total[owner]
    stores += start([(pair_bias, pair_bias_hbm)], sems, len(loads) + 1)
    for store in stores:
        store.wait()


def head_masks(width):
    lane = lax.broadcasted_iota(jnp.int32, (1, width), 1)
    return [(lane >= head * DH) & (lane < (head + 1) * DH) for head in range(HD)]


def attend_kernel(share, *refs):
    bias, weight, refs = refs[0], refs[1], refs[2:]
    found, value, refs = refs[:share], refs[share : 2 * share], refs[2 * share :]
    out_hbm, wide, out, sems = refs
    count, own, width = wide.shape
    each, tokens, _ = value[0].shape
    low = lax.axis_size("lo")
    order = turns(bias.shape[0] // low, low)
    turned = jnp.concatenate([bias[order.index(c)] for c in range(len(order))], axis=0)
    masks = head_masks(width)
    ones = jnp.ones((tokens, turned.shape[1]), BF16)
    turn = (((0,), (0,)), ((), ()))
    slots = [(flip, at) for flip in range(share) for at in range(each)]
    rows = []
    for flip, at in slots:
        scores = found[flip][at, :tokens] + turned
        peak = jnp.max(scores, axis=0, keepdims=True)
        weights = jnp.exp(scores - peak).astype(BF16)
        summed = lax.dot_general(weights, value[flip][at], turn, preferred_element_type=F32)
        total = lax.dot_general(weights, ones, turn, preferred_element_type=F32)
        summed = summed * (1.0 / total[:, :1])
        attended = jnp.where(masks[0], summed[:own], 0.0)
        for head in range(1, HD):
            attended = jnp.where(masks[head], summed[head * own : (head + 1) * own], attended)
        rows.append(attended)

    def gates(kind):
        lanes = turned.shape[1]
        first = tokens + kind * own * (width // lanes)
        places = [slice(first + lane * own, first + (lane + 1) * own) for lane in range(width // lanes)]
        return jnp.concatenate(
            [
                jnp.concatenate([found[flip][at, place] for place in places], axis=1)
                for flip, at in slots
            ],
            axis=0,
        )

    gated = (gates(0) * jnp.concatenate(rows, axis=0)).astype(BF16)
    projected = gates(1) * jnp.dot(gated, weight[...], preferred_element_type=F32)
    for slot, (flip, at) in enumerate(slots):
        wide[first_sample(share, each, flip) + at] = projected[slot * own : (slot + 1) * own]
    out[...] = wide[...].reshape(count * own, width).astype(BF16)
    for store in start([(out, out_hbm)], sems):
        store.wait()


def local(
    pair_repr,
    tri_weight,
    tri_bias_weight,
    tri_output_weight,
    samples,
    levels,
    single_cond,
    noise_weight,
    modulation_weight,
    attention_weight,
    pair_bias_weight,
    output_weight,
    output_gate_weight,
):
    rows, cols, channels = pair_repr.shape
    ranks, high, low = (lax.axis_size(name) for name in ("row", "hi", "lo"))
    col_count = high * low
    sample_count, tokens, width = samples.shape
    own = rows // col_count
    span = high // ranks
    keys = ranks * rows
    shape = jax.ShapeDtypeStruct

    turned = jnp.transpose(tri_bias_weight)
    normed_shape = shape((cols, rows, channels), BF16)
    bias_shape = shape((HT, cols, rows), F32)
    wide = pltpu.VMEM((rows * cols, channels), F32)
    copies_shape = shape((ranks * high, *bias_shape.shape), F32)
    bias, normed = call(
        norm_kernel,
        (copies_shape, normed_shape),
        (pair_repr, turned),
        scratch=(held(pair_repr), held(turned), wide, held(bias_shape), held(normed_shape)),
        copies=6 + ranks * high,
        flops=2 * rows * cols * channels * HT,
    )
    groups = [
        [
            (r * high + h) * low + lo
            for r in range(ranks)
            for h in places(high, ranks, lo)
        ]
        for lo in range(low)
    ]
    placed = lax.all_to_all(
        bias, ("row", "hi", "lo"), split_axis=0, concat_axis=0, axis_index_groups=groups
    )
    peers = [
        lax.ppermute(normed, "row", [((r + step) % ranks, r) for r in range(ranks)])
        for step in range(1, ranks)
    ]

    share = 2 if low % 2 == 0 and sample_count % 2 == 0 else 1
    each = sample_count // share
    part = (each, tokens, width)
    extra = share * own
    conditions = single_cond.shape[1]
    key, value, own_rows, cond_rows = call(
        functools.partial(condition_kernel, share),
        (
            shape(part, BF16),
            shape(part, BF16),
            shape((each, extra, width), BF16),
            shape((each, extra, conditions), BF16),
        ),
        (
            levels,
            single_cond,
            noise_weight,
            modulation_weight,
            samples,
            attention_weight,
        ),
        scratch=(
            pltpu.SMEM(levels.shape, levels.dtype),
            held(single_cond),
            held(noise_weight),
            held(modulation_weight),
            pltpu.VMEM(part, BF16),
            pltpu.VMEM((2, width, width), BF16),
            pltpu.VMEM(part, BF16),
            pltpu.VMEM(part, BF16),
            pltpu.VMEM(part, BF16),
            pltpu.VMEM((each, *single_cond.shape), BF16),
        ),
        copies=11,
        after=(bias,),
        flops=4 * each * tokens * width * 2 * width,
        exps=each * tokens * width,
    )
    placed = placed.reshape(ranks, high, *bias_shape.shape)
    place = lax.axis_index("row") + ranks - lax.rem(lax.axis_index("lo"), ranks)
    gathered = [lax.dynamic_slice_in_dim(placed, lax.rem(place, ranks) * span, span, 1)]
    found_shape = shape((each, tokens + 2 * width // HD, HD * own), F32)
    found = list(
        call(
            functools.partial(token_kernel, share),
            (found_shape,) * share,
            (attention_weight, output_gate_weight, own_rows, cond_rows, key),
            scratch=(
                pltpu.VMEM((2, width, width), BF16),
                held(output_gate_weight),
                held(own_rows),
                held(cond_rows),
                held(key),
                pltpu.VMEM((share, *found_shape.shape), F32),
                pltpu.VMEM((2, each * extra, width), F32),
            ),
            copies=6 + share,
            after=(gathered[0],),
            flops=64 * rows * cols * channels * HT * DT,
        )
    )
    bit = low // 2
    while bit:
        flip = [(c ^ bit, c) for c in range(low)]
        ready = [gathered[0], *(hold(part, found[0]) for part in gathered[1:])]
        more = [lax.ppermute(part, "lo", flip) for part in ready]
        gathered = [part for both in zip(ready, more) for part in both]
        bit //= 2
    values = [value]
    if share == 2:
        other = [(c ^ 1, c) for c in range(low)]
        values.append(lax.ppermute(value, "lo", other))
        found[1] = lax.ppermute(found[1], "lo", other)

    pair_weight = jnp.transpose(pair_bias_weight)
    outs = (shape((rows, cols, channels), BF16), shape((col_count, cols, HD * own), F32))
    new_pair, pair_bias = call(
        functools.partial(triangle_kernel, ranks, low),
        outs,
        (
            pair_repr,
            tri_weight,
            tri_output_weight,
            pair_weight,
            *gathered,
            normed,
            *peers,
        ),
        scratch=(
            held(pair_repr),
            held(tri_weight),
            held(tri_output_weight),
            held(pair_weight),
            pltpu.VMEM((low, ranks, span, HT, cols, rows), F32),
            pltpu.VMEM((ranks, cols, rows, channels), BF16),
            held(outs[0]),
            held(outs[1]),
            pltpu.VMEM((ranks, HT, rows, rows), F32),
            pltpu.VMEM((keys, HT * rows), F32),
            pltpu.VMEM((cols, HT * DT, rows), BF16),
            pltpu.VMEM((cols, keys, HT * DT), BF16),
            pltpu.VMEM((cols, HT * DT, keys), BF16),
            pltpu.VMEM((cols, HT * DT, rows), F32),
            wide,
            *[
                pltpu.VMEM(*slot)
                for slot in (
                    ((keys, HT * rows), F32),
                    ((1, HT * rows), F32),
                    ((keys, HT * rows), BF16),
                )
                * 2
            ],
        ),
        copies=6 + ranks + low,
        after=(found[0],),
        flops=4 * HT * rows * cols * keys * HT * DT,
        exps=HT * rows * cols * keys,
    )
    own_bias = lax.all_to_all(
        pair_bias, ("hi", "lo"), split_axis=0, concat_axis=0, axis_index_groups=[turns(high, low)]
    )

    outs = (shape((sample_count * own, width), BF16),)
    (attn_update,) = call(
        functools.partial(attend_kernel, share),
        outs,
        (own_bias, output_weight, *found, *values),
        scratch=(pltpu.VMEM((sample_count, own, width), F32), held(outs[0])),
        copies=1,
        near=True,
        flops=2 * sample_count * HD * own * tokens * width,
        exps=sample_count * HD * own * tokens,
    )
    return (new_pair, attn_update.reshape(sample_count, own, width))


def solution(mesh):
    ranks, col_count, groups = (mesh.shape[name] for name in ("row", "col", "smp"))
    low = math.gcd(col_count // ranks, 4)
    finer = jax.sharding.Mesh(
        mesh.devices.reshape(ranks, col_count // low, low, groups), ("row", "hi", "lo", "smp")
    )
    tile = P("row", ("hi", "lo"), None)
    return jax.shard_map(
        local,
        mesh=finer,
        in_specs=(tile, P(), P(), P(), P("smp", None, None), P("smp"), *[P()] * 7),
        out_specs=(tile, P("smp", ("row", "hi", "lo"), None)),
        check_vma=False,
    )
```

```python
import functools
import math

import jax
import jax.numpy as jnp
from jax import lax
from jax.experimental import pallas as pl
from jax.experimental.pallas import tpu as pltpu
from jax.sharding import PartitionSpec as P

HT = 4
DT = 32
CA = 768
HD = 16
DH = 48
NE = 256
LEVELS = 200

NORM_EPSILON = 1e-05
SIGMA_DATA = 16.0
SIGMA_MAX = 160.0
SIGMA_MIN = 0.0004

VMEM_LIMIT = 60 << 20
NEAR_LIMIT = 48 << 20

F32 = jnp.float32
BF16 = jnp.bfloat16
NT = (((1,), (1,)), ((), ()))


def normalize(values):
    values = values.astype(F32)
    average = jnp.mean(values, axis=-1, keepdims=True)
    centred = values - average
    variance = jnp.mean(centred * centred, axis=-1, keepdims=True)
    return centred * lax.rsqrt(variance + NORM_EPSILON)


def noise_features(levels):
    fraction = levels.astype(F32) / (LEVELS - 1)
    upper_root = SIGMA_MAX ** (1.0 / 7.0)
    lower_root = SIGMA_MIN ** (1.0 / 7.0)
    noise_sigma = SIGMA_DATA * (upper_root + fraction * (lower_root - upper_root)) ** 7
    scaled = 0.25 * jnp.log(noise_sigma / SIGMA_DATA)
    frequency = (
        2.0 * math.pi * jnp.exp(jnp.arange(NE // 2, dtype=F32) * (math.log(100.0) / (NE // 2)))
    )
    angles = scaled[:, None] * frequency[None, :]
    return jnp.concatenate([jnp.cos(angles), jnp.sin(angles)], axis=-1)


def nbytes(*shapes):
    return sum(math.prod(s.shape) * jnp.dtype(s.dtype).itemsize for s in shapes)


def held(operand):
    return pltpu.VMEM(operand.shape, operand.dtype)


def call(kernel, out_shape, operands, scratch=(), copies=0, after=(), near=False, flops=0, exps=0):
    in_specs = [pl.BlockSpec(memory_space=pltpu.VMEM if near else pltpu.HBM)] * len(operands)
    in_specs += [pl.BlockSpec(memory_space=pl.ANY)] * len(after)
    moved = nbytes(*operands, *out_shape)
    count = len(operands)

    def body(*refs):
        kernel(*refs[:count], *refs[count + len(after) :])

    return pl.pallas_call(
        body,
        out_shape=out_shape,
        in_specs=in_specs,
        out_specs=tuple(pl.BlockSpec(memory_space=pltpu.HBM) for _ in out_shape),
        scratch_shapes=[*scratch, pltpu.SemaphoreType.DMA((copies,))],
        compiler_params=pltpu.CompilerParams(vmem_limit_bytes=NEAR_LIMIT if near else VMEM_LIMIT),
        cost_estimate=pl.CostEstimate(flops=flops, bytes_accessed=moved, transcendentals=exps),
    )(*operands, *after)


def start(pairs, sems, first=0):
    copies = [
        pltpu.make_async_copy(source, target, sems.at[first + at])
        for at, (source, target) in enumerate(pairs)
    ]
    for copy in copies:
        copy.start()
    return copies


def places(high, ranks, lo):
    span = high // ranks
    rest = [(h + lo % ranks * span) % high for h in range(high)]
    if lo % ranks == 0:
        rest = [h // span * span + span - 1 - h % span for h in rest]
    return rest


def turns(high, low):
    order = []
    for h in range(high // 2):
        for lo in range(low):
            order += [((high // 2 + h) * low + lo), ((high // 2 - 1 - h) * low + lo)]
    return order


def hold(value, after):
    return pl.pallas_call(
        lambda *refs: None,
        out_shape=jax.ShapeDtypeStruct(value.shape, value.dtype),
        in_specs=[
            pl.BlockSpec(memory_space=pltpu.HBM),
            pl.BlockSpec(memory_space=pl.ANY),
        ],
        out_specs=pl.BlockSpec(memory_space=pltpu.HBM),
        input_output_aliases={0: 0},
        compiler_params=pltpu.CompilerParams(vmem_limit_bytes=VMEM_LIMIT),
    )(value, after)


def own_place():
    low = lax.axis_size("lo")
    return lax.axis_index("hi") * low + lax.axis_index("lo"), lax.axis_size("hi") * low


def norm_kernel(pair_hbm, weight_hbm, bias_hbm, normed_hbm, pair, weight, wide, bias, normed, sems):
    rows, cols, channels = pair.shape
    pieces = 4
    some = rows // pieces
    slices = [pl.ds(at * some, some) for at in range(pieces)]
    loads = start([(weight_hbm, weight)] + [(pair_hbm.at[h], pair.at[h]) for h in slices], sems)
    for at, load in enumerate(loads[1:]):
        load.wait()
        for first in range(at * some, (at + 1) * some, 8):
            tile = pair[first : first + 8].astype(F32).reshape(8 * cols, channels)
            wide[first * cols : (first + 8) * cols, :] = normalize(tile)
    loads[0].wait()
    for col in range(cols):
        one = wide[pl.ds(col, rows, stride=cols), :].astype(BF16)
        normed[col] = one
        bias[:, col, :] = lax.dot_general(weight[...], one, NT, preferred_element_type=F32)
    copies = bias_hbm.shape[0]
    pairs = [(bias, bias_hbm.at[at]) for at in range(copies)] + [(normed, normed_hbm)]
    for copy in start(pairs, sems, 1 + pieces):
        copy.wait()


def first_sample(share, each, flip=0):
    return (lax.rem(lax.axis_index("lo"), share) ^ flip) * each


def condition_kernel(share, *refs):
    levels_hbm, cond_hbm, noise_hbm, modulation_hbm, samples_hbm, attention_hbm = refs[:6]
    key_hbm, value_hbm, rows_hbm, cond_rows_hbm = refs[6:10]
    levels, cond, noise, modulation, samples, attention, key, value = refs[10:18]
    adapted, conditions, sems = refs[18:]
    count, tokens, width = samples.shape
    extra = rows_hbm.shape[1]
    first = first_sample(share, count)
    loads = start(
        [
            (levels_hbm, levels),
            (noise_hbm, noise),
            (cond_hbm, cond),
            (modulation_hbm, modulation),
            (samples_hbm.at[pl.ds(first, count)], samples),
            (attention_hbm.at[:, pl.ds(width, width)], attention.at[0]),
            (attention_hbm.at[:, pl.ds(2 * width, width)], attention.at[1]),
        ],
        sems,
    )
    loads[0].wait()
    row = lax.broadcasted_iota(jnp.int32, (8, NE // 2), 0)
    level = jnp.zeros((8, NE // 2), F32)
    for sample in range(count):
        level = jnp.where(row == sample, levels[first + sample].astype(F32), level)
    fraction = level / (LEVELS - 1)
    upper_root = SIGMA_MAX ** (1.0 / 7.0)
    lower_root = SIGMA_MIN ** (1.0 / 7.0)
    root = upper_root + fraction * (lower_root - upper_root)
    square = root * root
    sigma = SIGMA_DATA * (square * square * square * root)
    scaled = 0.25 * jnp.log(sigma / SIGMA_DATA)
    step = lax.broadcasted_iota(jnp.int32, scaled.shape, 1).astype(F32)
    angles = scaled * (2.0 * math.pi * jnp.exp(step * (math.log(100.0) / (NE // 2))))
    features = jnp.concatenate([jnp.cos(angles), jnp.sin(angles)], axis=-1).astype(BF16)
    loads[1].wait()
    terms = jnp.dot(features, noise[...], preferred_element_type=F32)
    for load in loads[2:4]:
        load.wait()

    loads[4].wait()
    for sample in range(count):
        trunk = cond[...].astype(F32) + terms[sample : sample + 1]
        conditioned = normalize(trunk).astype(BF16)
        conditions[sample] = conditioned
        modulated = jnp.dot(conditioned, modulation[...], preferred_element_type=F32)
        gain = jax.nn.sigmoid(modulated[:, :width])
        one = gain * normalize(samples[sample]) + modulated[:, width:]
        adapted[sample] = one.astype(BF16)
    place, places = own_place()
    chip = lax.div(lax.axis_index("row") * places + place, share) * extra
    here = pl.ds(pl.multiple_of(chip, extra), extra)
    stores = start(
        [(adapted.at[:, here], rows_hbm), (conditions.at[:, here], cond_rows_hbm)], sems, 7
    )
    for at, (part, target) in enumerate(((key, key_hbm), (value, value_hbm))):
        loads[5 + at].wait()
        for sample in range(count):
            part[sample] = jnp.dot(
                adapted[sample], attention[at], preferred_element_type=F32
            ).astype(BF16)
        stores += start([(part, target)], sems, 9 + at)
    for store in stores:
        store.wait()


def token_kernel(share, *refs):
    attention_hbm, gate_hbm, rows_hbm, cond_hbm, key_hbm = refs[:5]
    targets, refs = refs[5 : 5 + share], refs[5 + share :]
    attention, gate_weight, rows, cond, key, found, wide, sems = refs
    count, tokens, width = key.shape
    extra = rows.shape[1]
    own = extra // share
    loads = start(
        [
            (rows_hbm, rows),
            (attention_hbm.at[:, pl.ds(0, width)], attention.at[0]),
            (key_hbm, key),
            (attention_hbm.at[:, pl.ds(3 * width, width)], attention.at[1]),
            (cond_hbm, cond),
            (gate_hbm, gate_weight),
        ],
        sems,
    )
    for load in loads[:2]:
        load.wait()
    flat = rows[...].reshape(count * extra, width)
    raw = jnp.dot(flat, attention[0], preferred_element_type=F32)
    query = (raw * DH ** (-0.5)).astype(BF16).astype(F32)
    masks = head_masks(width)
    loads[2].wait()
    for sample in range(count):
        stacked = []
        for core in range(share):
            at = sample * extra + core * own
            one = query[at : at + own]
            stacked += [jnp.where(m, one, 0.0) for m in masks]
        stacked = jnp.concatenate(stacked, axis=0).astype(BF16)
        raw = lax.dot_general(key[sample], stacked, NT, preferred_element_type=F32)
        for core in range(share):
            found[core, sample, :tokens, :] = raw[:, core * HD * own : (core + 1) * HD * own]
    loads[3].wait()
    wide[0] = jax.nn.sigmoid(jnp.dot(flat, attention[1], preferred_element_type=F32))
    for load in loads[4:]:
        load.wait()
    flat = cond[...].reshape(count * extra, cond.shape[2])
    wide[1] = jax.nn.sigmoid(jnp.dot(flat, gate_weight[...], preferred_element_type=F32))
    lanes = found.shape[3]
    for core in range(share):
        for sample in range(count):
            at = sample * extra + core * own
            to = tokens
            for kind in range(2):
                for lane in range(0, width, lanes):
                    found[core, sample, to : to + own, :] = wide[
                        kind, at : at + own, lane : lane + lanes
                    ]
                    to += own
    mine = lax.rem(lax.axis_index("lo"), share)
    stores = start(
        [(found.at[mine ^ flip], targets[flip]) for flip in range(share)], sems, len(loads)
    )
    for store in stores:
        store.wait()


def triangle_kernel(ranks, low, *refs):
    pair_hbm, weight_hbm, out_weight_hbm, bias_weight_hbm = refs[:4]
    gathered_hbm, refs = refs[4 : 4 + low], refs[4 + low :]
    normed_hbm, refs = refs[:ranks], refs[ranks:]
    new_hbm, pair_bias_hbm, refs = refs[0], refs[1], refs[2:]
    pair, weight, out_weight, bias_weight = refs[:4]
    gathered, normed, new, pair_bias, refs = refs[4], refs[5], refs[6], refs[7], refs[8:]
    bias_rows, bias, query, key, value, gate, wide = refs[:7]
    slots, renormed, sems = (refs[7:9], refs[9:11]), refs[11], refs[12]
    rows, cols, channels = pair.shape
    width = HT * DT
    span = gathered.shape[2]
    loads = start(
        [
            (weight_hbm, weight),
            *[(normed_hbm[at], normed.at[at]) for at in range(ranks)],
            *[(gathered_hbm[at], gathered.at[at]) for at in range(low)],
            (pair_hbm, pair),
            (out_weight_hbm, out_weight),
            (bias_weight_hbm, bias_weight),
        ],
        sems,
    )
    for load in loads[: 1 + ranks + low]:
        load.wait()
    row, fast = lax.axis_index("row"), lax.axis_index("lo")
    for flip in range(low):
        for slow in range(span):
            sender = fast ^ flip
            block = jnp.where(lax.rem(sender, ranks) == 0, span - 1 - slow, slow)
            first = pl.multiple_of((block * low + sender) * cols, cols)
            for source in range(ranks):
                step = lax.rem(source + ranks - row, ranks)
                bias_rows[step, :, pl.ds(first, cols), :] = gathered[flip, source, slow]
    turned = jnp.transpose(weight[...].astype(F32)).astype(BF16)
    own_lines = jnp.concatenate([turned[:width], turned[2 * width :]], axis=0)
    peer_lines = turned[2 * width : 3 * width]
    batch = 4
    tiles = [(step, head) for step in range(ranks) for head in range(HT)]
    groups = cols // batch
    for group in range(groups):
        at = group * batch
        for step in range(ranks):
            some = normed[step, at : at + batch].reshape(batch * rows, channels)
            here = slice(step * rows, (step + 1) * rows)
            raw = jnp.dot(some, weight[:, width : 2 * width], preferred_element_type=F32)
            key[at : at + batch, here, :] = raw.astype(BF16).reshape(batch, rows, width)
            lines = own_lines if step == 0 else peer_lines
            raw = lax.dot_general(lines, some, NT, preferred_element_type=F32)
            for side in range(batch):
                part = raw[:, side * rows : (side + 1) * rows]
                if step == 0:
                    query[at + side] = (part[:width] * DT ** (-0.5)).astype(BF16)
                    gate[at + side] = jax.nn.sigmoid(part[2 * width :])
                    part = part[width : 2 * width]
                value[at + side, :, here] = part.astype(BF16)
        for step, head in tiles[group::groups]:
            bias[step * rows : (step + 1) * rows, head * rows : (head + 1) * rows] = jnp.transpose(
                bias_rows[step, head]
            )
    for load in loads[1 + ranks + low :]:
        load.wait()

    def score(col, slot):
        scores, _ = slots[slot]
        own = query[col]
        blocks = []
        for head in range(HT):
            zeros = [jnp.zeros((size, rows), BF16) for size in (head * DT, width - (head + 1) * DT)]
            block = [zeros[0], own[head * DT : (head + 1) * DT], zeros[1]]
            blocks.append(jnp.concatenate([b for b in block if b.shape[0]], axis=0))
        stacked = jnp.concatenate(blocks, axis=1)
        scores[...] = jnp.dot(key[col], stacked, preferred_element_type=F32)

    def attend(col, slot):
        scores, weights = slots[slot]
        piece = 32
        pieces = [slice(at, at + piece) for at in range(0, scores.shape[0], piece)]
        rough = None
        for at in pieces:
            some = (scores[at] + bias[at]).reshape(piece // 8, 8, -1)
            some = jnp.max(some, axis=0)
            rough = some if rough is None else jnp.maximum(rough, some)
        peak = jnp.max(rough, axis=0, keepdims=True)
        rough = None
        for at in pieces:
            exponent = jnp.exp(scores[at] + bias[at] - peak)
            weights[at] = exponent.astype(BF16)
            some = jnp.sum(exponent.reshape(piece // 8, 8, -1), axis=0)
            rough = some if rough is None else rough + some
        scale = 1.0 / jnp.sum(rough, axis=0, keepdims=True)
        parts = []
        for head in range(0, HT, 2):
            here = slice(head * rows, (head + 2) * rows)
            summed = jnp.dot(
                value[col, head * DT : (head + 2) * DT, :],
                weights[:, here],
                preferred_element_type=F32,
            )
            summed = summed * scale[:, here]
            parts += [summed[:DT, :rows], summed[DT:, rows:]]
        gated = (gate[col] * jnp.concatenate(parts, axis=0)).astype(BF16)
        wide[pl.ds(col, rows, stride=cols), :] = lax.dot_general(
            gated, out_weight[...], (((0,), (0,)), ((), ())), preferred_element_type=F32
        )

    score(0, 0)

    @pl.loop(0, cols // batch)
    def _(group):
        for side in range(batch):
            col = group * batch + side
            score(jnp.minimum(col + 1, cols - 1), (side + 1) % 2)
            attend(col, side % 2)

    owners, _, lanes = pair_bias.shape
    own = rows // owners
    for owner in range(owners):
        here = slice(owner * own, (owner + 1) * own)
        some = pair[here].astype(F32).reshape(own * cols, channels)
        some = (some + wide[owner * own * cols : (owner + 1) * own * cols, :]).astype(BF16)
        new[here] = some.reshape(own, cols, channels)
        renormed[owner] = normalize(some).astype(BF16).reshape(own, cols, channels)
    stores = start([(new, new_hbm)], sems, len(loads))
    lane = lax.broadcasted_iota(jnp.int32, (lanes, HD), 0)
    pick = (lane // own == lax.broadcasted_iota(jnp.int32, (lanes, HD), 1)).astype(BF16)
    spread = jnp.dot(pick, bias_weight[...], preferred_element_type=F32)
    token_of = lax.rem(lax.broadcasted_iota(jnp.int32, (lanes, channels), 0), own)
    spots = [jnp.where(token_of == token, spread, 0.0).astype(BF16) for token in range(own)]
    flat = [renormed[:, token].reshape(owners * cols, channels) for token in range(own)]
    total = lax.dot_general(
        jnp.concatenate(flat, axis=1),
        jnp.concatenate(spots, axis=1),
        NT,
        preferred_element_type=F32,
    )
    total = total.reshape(owners, cols, lanes)
    for place, owner in enumerate(turns(owners // low, low)):
        pair_bias[place] = total[owner]
    stores += start([(pair_bias, pair_bias_hbm)], sems, len(loads) + 1)
    for store in stores:
        store.wait()


def head_masks(width):
    lane = lax.broadcasted_iota(jnp.int32, (1, width), 1)
    return [(lane >= head * DH) & (lane < (head + 1) * DH) for head in range(HD)]


def attend_kernel(share, *refs):
    bias, weight, refs = refs[0], refs[1], refs[2:]
    found, value, refs = refs[:share], refs[share : 2 * share], refs[2 * share :]
    out_hbm, wide, out, sems = refs
    count, own, width = wide.shape
    each, tokens, _ = value[0].shape
    low = lax.axis_size("lo")
    order = turns(bias.shape[0] // low, low)
    turned = jnp.concatenate([bias[order.index(c)] for c in range(len(order))], axis=0)
    masks = head_masks(width)
    ones = jnp.ones((tokens, turned.shape[1]), BF16)
    turn = (((0,), (0,)), ((), ()))
    slots = [(flip, at) for flip in range(share) for at in range(each)]
    rows = []
    for flip, at in slots:
        scores = found[flip][at, :tokens] + turned
        peak = jnp.max(scores, axis=0, keepdims=True)
        weights = jnp.exp(scores - peak).astype(BF16)
        summed = lax.dot_general(weights, value[flip][at], turn, preferred_element_type=F32)
        total = lax.dot_general(weights, ones, turn, preferred_element_type=F32)
        summed = summed * (1.0 / total[:, :1])
        attended = jnp.where(masks[0], summed[:own], 0.0)
        for head in range(1, HD):
            attended = jnp.where(masks[head], summed[head * own : (head + 1) * own], attended)
        rows.append(attended)

    def gates(kind):
        lanes = turned.shape[1]
        first = tokens + kind * own * (width // lanes)
        places = [slice(first + lane * own, first + (lane + 1) * own) for lane in range(width // lanes)]
        return jnp.concatenate(
            [
                jnp.concatenate([found[flip][at, place] for place in places], axis=1)
                for flip, at in slots
            ],
            axis=0,
        )

    gated = (gates(0) * jnp.concatenate(rows, axis=0)).astype(BF16)
    projected = gates(1) * jnp.dot(gated, weight[...], preferred_element_type=F32)
    for slot, (flip, at) in enumerate(slots):
        wide[first_sample(share, each, flip) + at] = projected[slot * own : (slot + 1) * own]
    out[...] = wide[...].reshape(count * own, width).astype(BF16)
    for store in start([(out, out_hbm)], sems):
        store.wait()


def local(
    pair_repr,
    tri_weight,
    tri_bias_weight,
    tri_output_weight,
    samples,
    levels,
    single_cond,
    noise_weight,
    modulation_weight,
    attention_weight,
    pair_bias_weight,
    output_weight,
    output_gate_weight,
):
    rows, cols, channels = pair_repr.shape
    ranks, high, low = (lax.axis_size(name) for name in ("row", "hi", "lo"))
    col_count = high * low
    sample_count, tokens, width = samples.shape
    own = rows // col_count
    span = high // ranks
    keys = ranks * rows
    shape = jax.ShapeDtypeStruct

    turned = jnp.transpose(tri_bias_weight)
    normed_shape = shape((cols, rows, channels), BF16)
    bias_shape = shape((HT, cols, rows), F32)
    wide = pltpu.VMEM((rows * cols, channels), F32)
    copies_shape = shape((ranks * high, *bias_shape.shape), F32)
    bias, normed = call(
        norm_kernel,
        (copies_shape, normed_shape),
        (pair_repr, turned),
        scratch=(held(pair_repr), held(turned), wide, held(bias_shape), held(normed_shape)),
        copies=6 + ranks * high,
        flops=2 * rows * cols * channels * HT,
    )
    groups = [
        [
            (r * high + h) * low + lo
            for r in range(ranks)
            for h in places(high, ranks, lo)
        ]
        for lo in range(low)
    ]
    placed = lax.all_to_all(
        bias, ("row", "hi", "lo"), split_axis=0, concat_axis=0, axis_index_groups=groups
    )
    peers = [
        lax.ppermute(normed, "row", [((r + step) % ranks, r) for r in range(ranks)])
        for step in range(1, ranks)
    ]

    share = 2 if low % 2 == 0 and sample_count % 2 == 0 else 1
    each = sample_count // share
    part = (each, tokens, width)
    extra = share * own
    conditions = single_cond.shape[1]
    key, value, own_rows, cond_rows = call(
        functools.partial(condition_kernel, share),
        (
            shape(part, BF16),
            shape(part, BF16),
            shape((each, extra, width), BF16),
            shape((each, extra, conditions), BF16),
        ),
        (
            levels,
            single_cond,
            noise_weight,
            modulation_weight,
            samples,
            attention_weight,
        ),
        scratch=(
            pltpu.SMEM(levels.shape, levels.dtype),
            held(single_cond),
            held(noise_weight),
            held(modulation_weight),
            pltpu.VMEM(part, BF16),
            pltpu.VMEM((2, width, width), BF16),
            pltpu.VMEM(part, BF16),
            pltpu.VMEM(part, BF16),
            pltpu.VMEM(part, BF16),
            pltpu.VMEM((each, *single_cond.shape), BF16),
        ),
        copies=11,
        after=(bias,),
        flops=4 * each * tokens * width * 2 * width,
        exps=each * tokens * width,
    )
    placed = placed.reshape(ranks, high, *bias_shape.shape)
    place = lax.axis_index("row") + ranks - lax.rem(lax.axis_index("lo"), ranks)
    gathered = [lax.dynamic_slice_in_dim(placed, lax.rem(place, ranks) * span, span, 1)]
    found_shape = shape((each, tokens + 2 * width // HD, HD * own), F32)
    found = list(
        call(
            functools.partial(token_kernel, share),
            (found_shape,) * share,
            (attention_weight, output_gate_weight, own_rows, cond_rows, key),
            scratch=(
                pltpu.VMEM((2, width, width), BF16),
                held(output_gate_weight),
                held(own_rows),
                held(cond_rows),
                held(key),
                pltpu.VMEM((share, *found_shape.shape), F32),
                pltpu.VMEM((2, each * extra, width), F32),
            ),
            copies=6 + share,
            after=(gathered[0],),
            flops=64 * rows * cols * channels * HT * DT,
        )
    )
    bit = low // 2
    while bit:
        flip = [(c ^ bit, c) for c in range(low)]
        ready = [gathered[0], *(hold(part, found[0]) for part in gathered[1:])]
        more = [lax.ppermute(part, "lo", flip) for part in ready]
        gathered = [part for both in zip(ready, more) for part in both]
        bit //= 2
    values = [value]
    if share == 2:
        other = [(c ^ 1, c) for c in range(low)]
        values.append(lax.ppermute(value, "lo", other))
        found[1] = lax.ppermute(found[1], "lo", other)

    pair_weight = jnp.transpose(pair_bias_weight)
    outs = (shape((rows, cols, channels), BF16), shape((col_count, cols, HD * own), F32))
    new_pair, pair_bias = call(
        functools.partial(triangle_kernel, ranks, low),
        outs,
        (
            pair_repr,
            tri_weight,
            tri_output_weight,
            pair_weight,
            *gathered,
            normed,
            *peers,
        ),
        scratch=(
            held(pair_repr),
            held(tri_weight),
            held(tri_output_weight),
            held(pair_weight),
            pltpu.VMEM((low, ranks, span, HT, cols, rows), F32),
            pltpu.VMEM((ranks, cols, rows, channels), BF16),
            held(outs[0]),
            held(outs[1]),
            pltpu.VMEM((ranks, HT, rows, rows), F32),
            pltpu.VMEM((keys, HT * rows), F32),
            pltpu.VMEM((cols, HT * DT, rows), BF16),
            pltpu.VMEM((cols, keys, HT * DT), BF16),
            pltpu.VMEM((cols, HT * DT, keys), BF16),
            pltpu.VMEM((cols, HT * DT, rows), F32),
            wide,
            *[
                pltpu.VMEM(*slot)
                for slot in (
                    ((keys, HT * rows), F32),
                    ((keys, HT * rows), BF16),
                )
                * 2
            ],
            pltpu.VMEM((col_count, own, cols, channels), BF16),
        ),
        copies=6 + ranks + low,
        after=(found[0],),
        flops=4 * HT * rows * cols * keys * HT * DT,
        exps=HT * rows * cols * keys,
    )
    own_bias = lax.all_to_all(
        pair_bias, ("hi", "lo"), split_axis=0, concat_axis=0, axis_index_groups=[turns(high, low)]
    )

    outs = (shape((sample_count * own, width), BF16),)
    (attn_update,) = call(
        functools.partial(attend_kernel, share),
        outs,
        (own_bias, output_weight, *found, *values),
        scratch=(pltpu.VMEM((sample_count, own, width), F32), held(outs[0])),
        copies=1,
        near=True,
        flops=2 * sample_count * HD * own * tokens * width,
        exps=sample_count * HD * own * tokens,
    )
    return (new_pair, attn_update.reshape(sample_count, own, width))


def solution(mesh):
    ranks, col_count, groups = (mesh.shape[name] for name in ("row", "col", "smp"))
    low = math.gcd(col_count // ranks, 4)
    finer = jax.sharding.Mesh(
        mesh.devices.reshape(ranks, col_count // low, low, groups), ("row", "hi", "lo", "smp")
    )
    tile = P("row", ("hi", "lo"), None)
    return jax.shard_map(
        local,
        mesh=finer,
        in_specs=(tile, P(), P(), P(), P("smp", None, None), P("smp"), *[P()] * 7),
        out_specs=(tile, P("smp", ("row", "hi", "lo"), None)),
        check_vma=False,
    )
```

```python
import functools
import math

import jax
import jax.numpy as jnp
from jax import lax
from jax.experimental import pallas as pl
from jax.experimental.pallas import tpu as pltpu
from jax.sharding import PartitionSpec as P

HT = 4
DT = 32
CA = 768
HD = 16
DH = 48
NE = 256
LEVELS = 200

NORM_EPSILON = 1e-05
SIGMA_DATA = 16.0
SIGMA_MAX = 160.0
SIGMA_MIN = 0.0004


F32 = jnp.float32
BF16 = jnp.bfloat16
NT = (((1,), (1,)), ((), ()))


def normalize(values):
    values = values.astype(F32)
    average = jnp.mean(values, axis=-1, keepdims=True)
    centred = values - average
    variance = jnp.mean(centred * centred, axis=-1, keepdims=True)
    return centred * lax.rsqrt(variance + NORM_EPSILON)


def noise_features(levels):
    fraction = levels.astype(F32) / (LEVELS - 1)
    upper_root = SIGMA_MAX ** (1.0 / 7.0)
    lower_root = SIGMA_MIN ** (1.0 / 7.0)
    noise_sigma = SIGMA_DATA * (upper_root + fraction * (lower_root - upper_root)) ** 7
    scaled = 0.25 * jnp.log(noise_sigma / SIGMA_DATA)
    frequency = (
        2.0 * math.pi * jnp.exp(jnp.arange(NE // 2, dtype=F32) * (math.log(100.0) / (NE // 2)))
    )
    angles = scaled[:, None] * frequency[None, :]
    return jnp.concatenate([jnp.cos(angles), jnp.sin(angles)], axis=-1)


def nbytes(*shapes):
    return sum(math.prod(s.shape) * jnp.dtype(s.dtype).itemsize for s in shapes)


def held(operand):
    return pltpu.VMEM(operand.shape, operand.dtype)


def call(
    kernel, out_shape, operands, scratch=(), copies=0, after=(), near=(), mib=60, flops=0, exps=0
):
    in_specs = [
        pl.BlockSpec(memory_space=pltpu.VMEM if at in near else pltpu.HBM)
        for at in range(len(operands))
    ]
    in_specs += [pl.BlockSpec(memory_space=pl.ANY)] * len(after)
    moved = nbytes(*operands, *out_shape)
    count = len(operands)

    def body(*refs):
        kernel(*refs[:count], *refs[count + len(after) :])

    return pl.pallas_call(
        body,
        out_shape=out_shape,
        in_specs=in_specs,
        out_specs=tuple(pl.BlockSpec(memory_space=pltpu.HBM) for _ in out_shape),
        scratch_shapes=[*scratch, pltpu.SemaphoreType.DMA((copies,))],
        compiler_params=pltpu.CompilerParams(vmem_limit_bytes=mib << 20),
        cost_estimate=pl.CostEstimate(flops=flops, bytes_accessed=moved, transcendentals=exps),
    )(*operands, *after)


def start(pairs, sems, first=0):
    copies = [
        pltpu.make_async_copy(source, target, sems.at[first + at])
        for at, (source, target) in enumerate(pairs)
    ]
    for copy in copies:
        copy.start()
    return copies


def places(high, ranks, lo):
    span = high // ranks
    rest = [(h + lo % ranks * span) % high for h in range(high)]
    if lo % ranks == 0:
        rest = [h // span * span + span - 1 - h % span for h in rest]
    return rest


def turns(high, low):
    slow = sorted(range(high), key=lambda h: (h < high // 2, abs(2 * h - high)))
    return [h * low + lo for h in slow for lo in range(low)]


def hold(value, after):
    return pl.pallas_call(
        lambda *refs: None,
        out_shape=jax.ShapeDtypeStruct(value.shape, value.dtype),
        in_specs=[
            pl.BlockSpec(memory_space=pltpu.HBM),
            pl.BlockSpec(memory_space=pl.ANY),
        ],
        out_specs=pl.BlockSpec(memory_space=pltpu.HBM),
        input_output_aliases={0: 0},
        compiler_params=pltpu.CompilerParams(vmem_limit_bytes=48 << 20),
    )(value, after)


def own_place():
    low = lax.axis_size("lo")
    return lax.axis_index("hi") * low + lax.axis_index("lo"), lax.axis_size("hi") * low


def norm_kernel(pair_hbm, weight_hbm, bias_hbm, normed_hbm, pair, weight, wide, bias, normed, sems):
    rows, cols, channels = pair.shape
    pieces = 4
    some = rows // pieces
    slices = [pl.ds(at * some, some) for at in range(pieces)]
    loads = start([(weight_hbm, weight)] + [(pair_hbm.at[h], pair.at[h]) for h in slices], sems)
    for at, load in enumerate(loads[1:]):
        load.wait()
        tile = pair[at * some : (at + 1) * some].astype(F32).reshape(some * cols, channels)
        wide[at * some * cols : (at + 1) * some * cols, :] = normalize(tile)
    loads[0].wait()
    for col in range(cols):
        one = wide[pl.ds(col, rows, stride=cols), :].astype(BF16)
        normed[col] = one
        bias[:, col, :] = lax.dot_general(weight[...], one, NT, preferred_element_type=F32)
    copies = bias_hbm.shape[0]
    pairs = [(bias, bias_hbm.at[at]) for at in range(copies)] + [(normed, normed_hbm)]
    for copy in start(pairs, sems, 1 + pieces):
        copy.wait()


def first_sample(share, each, flip=0):
    return (lax.rem(lax.axis_index("lo"), share) ^ flip) * each


def condition_kernel(share, *refs):
    levels_hbm, cond_hbm, noise_hbm, modulation_hbm, samples_hbm, attention_hbm = refs[:6]
    key_hbm, value_hbm, rows_hbm, cond_rows_hbm = refs[6:10]
    levels, cond, noise, modulation, samples, attention, key, value = refs[10:18]
    adapted, conditions, sems = refs[18:]
    count, tokens, width = samples.shape
    extra = rows_hbm.shape[1]
    first = first_sample(share, count)
    loads = start(
        [
            (levels_hbm, levels),
            (noise_hbm, noise),
            (cond_hbm, cond),
            (modulation_hbm, modulation),
            (samples_hbm.at[pl.ds(first, count)], samples),
            (attention_hbm.at[:, pl.ds(width, width)], attention.at[0]),
            (attention_hbm.at[:, pl.ds(2 * width, width)], attention.at[1]),
        ],
        sems,
    )
    loads[0].wait()
    row = lax.broadcasted_iota(jnp.int32, (8, NE // 2), 0)
    level = jnp.zeros((8, NE // 2), F32)
    for sample in range(count):
        level = jnp.where(row == sample, levels[first + sample].astype(F32), level)
    fraction = level / (LEVELS - 1)
    upper_root = SIGMA_MAX ** (1.0 / 7.0)
    lower_root = SIGMA_MIN ** (1.0 / 7.0)
    root = upper_root + fraction * (lower_root - upper_root)
    square = root * root
    sigma = SIGMA_DATA * (square * square * square * root)
    scaled = 0.25 * jnp.log(sigma / SIGMA_DATA)
    step = lax.broadcasted_iota(jnp.int32, scaled.shape, 1).astype(F32)
    angles = scaled * (2.0 * math.pi * jnp.exp(step * (math.log(100.0) / (NE // 2))))
    features = jnp.concatenate([jnp.cos(angles), jnp.sin(angles)], axis=-1).astype(BF16)
    loads[1].wait()
    terms = jnp.dot(features, noise[...], preferred_element_type=F32)
    for load in loads[2:4]:
        load.wait()

    loads[4].wait()
    for sample in range(count):
        trunk = cond[...].astype(F32) + terms[sample : sample + 1]
        conditioned = normalize(trunk).astype(BF16)
        conditions[sample] = conditioned
        modulated = jnp.dot(conditioned, modulation[...], preferred_element_type=F32)
        gain = jax.nn.sigmoid(modulated[:, :width])
        one = gain * normalize(samples[sample]) + modulated[:, width:]
        adapted[sample] = one.astype(BF16)
    place, places = own_place()
    chip = lax.div(lax.axis_index("row") * places + place, share) * extra
    here = pl.ds(pl.multiple_of(chip, extra), extra)
    stores = start(
        [(adapted.at[:, here], rows_hbm), (conditions.at[:, here], cond_rows_hbm)], sems, 7
    )
    for at, (part, target) in enumerate(((key, key_hbm), (value, value_hbm))):
        loads[5 + at].wait()
        for sample in range(count):
            part[sample] = jnp.dot(
                adapted[sample], attention[at], preferred_element_type=F32
            ).astype(BF16)
        stores += start([(part, target)], sems, 9 + at)
    for store in stores:
        store.wait()


def token_kernel(share, *refs):
    attention_hbm, gate_hbm, rows_hbm, cond_hbm, key_hbm = refs[:5]
    targets, refs = refs[5 : 5 + share], refs[5 + share :]
    attention, gate_weight, rows, cond, key, found, wide, sems = refs
    count, tokens, width = key.shape
    extra = rows.shape[1]
    own = extra // share
    loads = start(
        [
            (rows_hbm, rows),
            (attention_hbm.at[:, pl.ds(0, width)], attention.at[0]),
            (key_hbm, key),
            (attention_hbm.at[:, pl.ds(3 * width, width)], attention.at[1]),
            (cond_hbm, cond),
            (gate_hbm, gate_weight),
        ],
        sems,
    )
    for load in loads[:2]:
        load.wait()
    flat = rows[...].reshape(count * extra, width)
    raw = jnp.dot(flat, attention[0], preferred_element_type=F32)
    query = (raw * DH ** (-0.5)).astype(BF16).astype(F32)
    masks = head_masks(width)
    loads[2].wait()
    for sample in range(count):
        stacked = []
        for core in range(share):
            at = sample * extra + core * own
            one = query[at : at + own]
            stacked += [jnp.where(m, one, 0.0) for m in masks]
        stacked = jnp.concatenate(stacked, axis=0).astype(BF16)
        raw = lax.dot_general(key[sample], stacked, NT, preferred_element_type=F32)
        for core in range(share):
            found[core, sample, :tokens, :] = raw[:, core * HD * own : (core + 1) * HD * own]
    loads[3].wait()
    wide[0] = jax.nn.sigmoid(jnp.dot(flat, attention[1], preferred_element_type=F32))
    for load in loads[4:]:
        load.wait()
    flat = cond[...].reshape(count * extra, cond.shape[2])
    wide[1] = jax.nn.sigmoid(jnp.dot(flat, gate_weight[...], preferred_element_type=F32))
    lanes = found.shape[3]
    for core in range(share):
        for sample in range(count):
            at = sample * extra + core * own
            to = tokens
            for kind in range(2):
                for lane in range(0, width, lanes):
                    found[core, sample, to : to + own, :] = wide[
                        kind, at : at + own, lane : lane + lanes
                    ]
                    to += own
    mine = lax.rem(lax.axis_index("lo"), share)
    stores = start(
        [(found.at[mine ^ flip], targets[flip]) for flip in range(share)], sems, len(loads)
    )
    for store in stores:
        store.wait()


def triangle_kernel(ranks, low, *refs):
    pair, weight, out_weight, bias_weight = refs[:4]
    gathered, refs = refs[4 : 4 + low], refs[4 + low :]
    normed_hbm, refs = refs[:ranks], refs[ranks:]
    new_hbm, pair_bias_hbm, refs = refs[0], refs[1], refs[2:]
    normed, new, pair_bias, refs = refs[0], refs[1], refs[2], refs[3:]
    bias_rows, bias, query, key, value, gate, wide = refs[:7]
    slots, (gated, renormed, sems) = (refs[7:10], refs[10:13]), refs[13:]
    rows, cols, channels = pair.shape
    width = HT * DT
    span = gathered[0].shape[1]
    loads = start([(normed_hbm[at], normed.at[at]) for at in range(ranks)], sems)
    row, fast = lax.axis_index("row"), lax.axis_index("lo")
    for flip in range(low):
        for slow in range(span):
            sender = fast ^ flip
            block = jnp.where(lax.rem(sender, ranks) == 0, span - 1 - slow, slow)
            first = pl.multiple_of((block * low + sender) * cols, cols)
            for source in range(ranks):
                step = lax.rem(source + ranks - row, ranks)
                bias_rows[step, :, pl.ds(first, cols), :] = gathered[flip][source, slow]
    turned = jnp.transpose(weight[...].astype(F32)).astype(BF16)
    for load in loads:
        load.wait()
    own_lines = jnp.concatenate([turned[:width], turned[2 * width :]], axis=0)
    peer_lines = turned[2 * width : 3 * width]
    batch = 4
    tiles = [(step, head) for step in range(ranks) for head in range(HT)]
    groups = cols // batch
    for group in range(groups):
        at = group * batch
        for step in range(ranks):
            some = normed[step, at : at + batch].reshape(batch * rows, channels)
            here = slice(step * rows, (step + 1) * rows)
            raw = jnp.dot(some, weight[:, width : 2 * width], preferred_element_type=F32)
            key[at : at + batch, here, :] = raw.astype(BF16).reshape(batch, rows, width)
            lines = own_lines if step == 0 else peer_lines
            raw = lax.dot_general(lines, some, NT, preferred_element_type=F32)
            for side in range(batch):
                part = raw[:, side * rows : (side + 1) * rows]
                if step == 0:
                    query[at + side] = (part[:width] * DT ** (-0.5)).astype(BF16)
                    gate[at + side] = jax.nn.sigmoid(part[2 * width :])
                    part = part[width : 2 * width]
                value[at + side, :, here] = part.astype(BF16)
        for step, head in tiles[group::groups]:
            bias[step * rows : (step + 1) * rows, head * rows : (head + 1) * rows] = jnp.transpose(
                bias_rows[step, head]
            )
    def score(col, slot):
        scores, peak, _ = slots[slot]
        own = query[col]
        blocks = []
        for head in range(HT):
            zeros = [jnp.zeros((size, rows), BF16) for size in (head * DT, width - (head + 1) * DT)]
            block = [zeros[0], own[head * DT : (head + 1) * DT], zeros[1]]
            blocks.append(jnp.concatenate([b for b in block if b.shape[0]], axis=0))
        stacked = jnp.concatenate(blocks, axis=1)
        raw = jnp.dot(key[col], stacked, preferred_element_type=F32) + bias[...]
        scores[...] = raw
        peak[...] = jnp.max(raw, axis=0, keepdims=True)

    def attend(col, slot):
        scores, peak, weights = slots[slot]
        exponent = jnp.exp(scores[...] - peak[...])
        scale = 1.0 / jnp.sum(exponent, axis=0, keepdims=True)
        weights[...] = exponent.astype(BF16)
        parts = []
        for head in range(0, HT, 2):
            here = slice(head * rows, (head + 2) * rows)
            summed = jnp.dot(
                value[col, head * DT : (head + 2) * DT, :],
                weights[:, here],
                preferred_element_type=F32,
            )
            summed = summed * scale[:, here]
            parts += [summed[:DT, :rows], summed[DT:, rows:]]
        gated[col] = (gate[col] * jnp.concatenate(parts, axis=0)).astype(BF16)

    score(0, 0)

    @pl.loop(0, cols // batch)
    def _(group):
        for side in range(batch):
            col = group * batch + side
            score(jnp.minimum(col + 1, cols - 1), (side + 1) % 2)
            attend(col, side % 2)

    for at in range(0, cols, batch):
        some = jnp.concatenate([gated[at + side] for side in range(batch)], axis=1)
        raw = lax.dot_general(
            some, out_weight[...], (((0,), (0,)), ((), ())), preferred_element_type=F32
        )
        for side in range(batch):
            wide[pl.ds(at + side, rows, stride=cols), :] = raw[side * rows : (side + 1) * rows]
    owners, _, lanes = pair_bias.shape
    own = rows // owners
    for owner in range(owners):
        here = slice(owner * own, (owner + 1) * own)
        some = pair[here].astype(F32).reshape(own * cols, channels)
        some = (some + wide[owner * own * cols : (owner + 1) * own * cols, :]).astype(BF16)
        new[here] = some.reshape(own, cols, channels)
        renormed[owner] = normalize(some).astype(BF16).reshape(own, cols, channels)
    stores = start([(new, new_hbm)], sems, len(loads))
    lane = lax.broadcasted_iota(jnp.int32, (lanes, HD), 0)
    pick = (lane // own == lax.broadcasted_iota(jnp.int32, (lanes, HD), 1)).astype(BF16)
    spread = jnp.dot(pick, bias_weight[...], preferred_element_type=F32)
    token_of = lax.rem(lax.broadcasted_iota(jnp.int32, (lanes, channels), 0), own)
    spots = [jnp.where(token_of == token, spread, 0.0).astype(BF16) for token in range(own)]
    flat = [renormed[:, token].reshape(owners * cols, channels) for token in range(own)]
    total = lax.dot_general(
        jnp.concatenate(flat, axis=1),
        jnp.concatenate(spots, axis=1),
        NT,
        preferred_element_type=F32,
    )
    total = total.reshape(owners, cols, lanes)
    for place, owner in enumerate(turns(owners // low, low)):
        pair_bias[place] = total[owner]
    stores += start([(pair_bias, pair_bias_hbm)], sems, len(loads) + 1)
    for store in stores:
        store.wait()


def head_masks(width):
    lane = lax.broadcasted_iota(jnp.int32, (1, width), 1)
    return [(lane >= head * DH) & (lane < (head + 1) * DH) for head in range(HD)]


def attend_kernel(share, *refs):
    bias, weight, refs = refs[0], refs[1], refs[2:]
    found, value, refs = refs[:share], refs[share : 2 * share], refs[2 * share :]
    out_hbm, wide, out, sems = refs
    count, own, width = wide.shape
    each, tokens, _ = value[0].shape
    low = lax.axis_size("lo")
    order = turns(bias.shape[0] // low, low)
    turned = jnp.concatenate([bias[order.index(c)] for c in range(len(order))], axis=0)
    masks = head_masks(width)
    ones = jnp.ones((tokens, turned.shape[1]), BF16)
    turn = (((0,), (0,)), ((), ()))
    slots = [(flip, at) for flip in range(share) for at in range(each)]
    rows = []
    for flip, at in slots:
        scores = found[flip][at, :tokens] + turned
        peak = jnp.max(scores, axis=0, keepdims=True)
        weights = jnp.exp(scores - peak).astype(BF16)
        summed = lax.dot_general(weights, value[flip][at], turn, preferred_element_type=F32)
        total = lax.dot_general(weights, ones, turn, preferred_element_type=F32)
        summed = summed * (1.0 / total[:, :1])
        attended = jnp.where(masks[0], summed[:own], 0.0)
        for head in range(1, HD):
            attended = jnp.where(masks[head], summed[head * own : (head + 1) * own], attended)
        rows.append(attended)

    def gates(kind):
        lanes = turned.shape[1]
        first = tokens + kind * own * (width // lanes)
        places = [slice(first + lane * own, first + (lane + 1) * own) for lane in range(width // lanes)]
        return jnp.concatenate(
            [
                jnp.concatenate([found[flip][at, place] for place in places], axis=1)
                for flip, at in slots
            ],
            axis=0,
        )

    gated = (gates(0) * jnp.concatenate(rows, axis=0)).astype(BF16)
    projected = gates(1) * jnp.dot(gated, weight[...], preferred_element_type=F32)
    for slot, (flip, at) in enumerate(slots):
        wide[first_sample(share, each, flip) + at] = projected[slot * own : (slot + 1) * own]
    out[...] = wide[...].reshape(count * own, width).astype(BF16)
    for store in start([(out, out_hbm)], sems):
        store.wait()


def local(
    pair_repr,
    tri_weight,
    tri_bias_weight,
    tri_output_weight,
    samples,
    levels,
    single_cond,
    noise_weight,
    modulation_weight,
    attention_weight,
    pair_bias_weight,
    output_weight,
    output_gate_weight,
):
    rows, cols, channels = pair_repr.shape
    ranks, high, low = (lax.axis_size(name) for name in ("row", "hi", "lo"))
    col_count = high * low
    sample_count, tokens, width = samples.shape
    own = rows // col_count
    span = high // ranks
    keys = ranks * rows
    shape = jax.ShapeDtypeStruct

    turned = jnp.transpose(tri_bias_weight)
    normed_shape = shape((cols, rows, channels), BF16)
    bias_shape = shape((HT, cols, rows), F32)
    wide = pltpu.VMEM((rows * cols, channels), F32)
    copies_shape = shape((ranks * high, *bias_shape.shape), F32)
    bias, normed = call(
        norm_kernel,
        (copies_shape, normed_shape),
        (pair_repr, turned),
        scratch=(held(pair_repr), held(turned), wide, held(bias_shape), held(normed_shape)),
        copies=6 + ranks * high,
        flops=2 * rows * cols * channels * HT,
    )
    groups = [
        [
            (r * high + h) * low + lo
            for r in range(ranks)
            for h in places(high, ranks, lo)
        ]
        for lo in range(low)
    ]
    placed = lax.all_to_all(
        bias, ("row", "hi", "lo"), split_axis=0, concat_axis=0, axis_index_groups=groups
    )
    peers = [
        lax.ppermute(normed, "row", [((r + step) % ranks, r) for r in range(ranks)])
        for step in range(1, ranks)
    ]

    share = 2 if low % 2 == 0 and sample_count % 2 == 0 else 1
    each = sample_count // share
    part = (each, tokens, width)
    extra = share * own
    conditions = single_cond.shape[1]
    key, value, own_rows, cond_rows = call(
        functools.partial(condition_kernel, share),
        (
            shape(part, BF16),
            shape(part, BF16),
            shape((each, extra, width), BF16),
            shape((each, extra, conditions), BF16),
        ),
        (
            levels,
            single_cond,
            noise_weight,
            modulation_weight,
            samples,
            attention_weight,
        ),
        scratch=(
            pltpu.SMEM(levels.shape, levels.dtype),
            held(single_cond),
            held(noise_weight),
            held(modulation_weight),
            pltpu.VMEM(part, BF16),
            pltpu.VMEM((2, width, width), BF16),
            pltpu.VMEM(part, BF16),
            pltpu.VMEM(part, BF16),
            pltpu.VMEM(part, BF16),
            pltpu.VMEM((each, *single_cond.shape), BF16),
        ),
        copies=11,
        after=(bias,),
        flops=4 * each * tokens * width * 2 * width,
        exps=each * tokens * width,
    )
    placed = placed.reshape(ranks, high, *bias_shape.shape)
    place = lax.axis_index("row") + ranks - lax.rem(lax.axis_index("lo"), ranks)
    gathered = [lax.dynamic_slice_in_dim(placed, lax.rem(place, ranks) * span, span, 1)]
    found_shape = shape((each, tokens + 2 * width // HD, HD * own), F32)
    found = list(
        call(
            functools.partial(token_kernel, share),
            (found_shape,) * share,
            (attention_weight, output_gate_weight, own_rows, cond_rows, key),
            scratch=(
                pltpu.VMEM((2, width, width), BF16),
                held(output_gate_weight),
                held(own_rows),
                held(cond_rows),
                held(key),
                pltpu.VMEM((share, *found_shape.shape), F32),
                pltpu.VMEM((2, each * extra, width), F32),
            ),
            copies=6 + share,
            after=(gathered[0],),
            mib=53,
            flops=64 * rows * cols * channels * HT * DT,
        )
    )
    bit = low // 2
    while bit:
        flip = [(c ^ bit, c) for c in range(low)]
        ready = [gathered[0], *(hold(part, found[0]) for part in gathered[1:])]
        more = [lax.ppermute(part, "lo", flip) for part in ready]
        gathered = [part for both in zip(ready, more) for part in both]
        bit //= 2
    values = [value]
    if share == 2:
        other = [(c ^ 1, c) for c in range(low)]
        values.append(lax.ppermute(value, "lo", other))
        found[1] = lax.ppermute(found[1], "lo", other)

    pair_weight = jnp.transpose(pair_bias_weight)
    outs = (shape((rows, cols, channels), BF16), shape((col_count, cols, HD * own), F32))
    new_pair, pair_bias = call(
        functools.partial(triangle_kernel, ranks, low),
        outs,
        (
            pair_repr,
            tri_weight,
            tri_output_weight,
            pair_weight,
            *gathered,
            normed,
            *peers,
        ),
        scratch=(
            pltpu.VMEM((ranks, cols, rows, channels), BF16),
            held(outs[0]),
            held(outs[1]),
            pltpu.VMEM((ranks, HT, rows, rows), F32),
            pltpu.VMEM((keys, HT * rows), F32),
            pltpu.VMEM((cols, HT * DT, rows), BF16),
            pltpu.VMEM((cols, keys, HT * DT), BF16),
            pltpu.VMEM((cols, HT * DT, keys), BF16),
            pltpu.VMEM((cols, HT * DT, rows), F32),
            wide,
            *[
                pltpu.VMEM(*slot)
                for slot in (
                    ((keys, HT * rows), F32),
                    ((1, HT * rows), F32),
                    ((keys, HT * rows), BF16),
                )
                * 2
            ],
            pltpu.VMEM((cols, HT * DT, rows), BF16),
            pltpu.VMEM((col_count, own, cols, channels), BF16),
        ),
        copies=2 + ranks,
        after=(found[0],),
        near=range(4 + low),
        mib=52,
        flops=4 * HT * rows * cols * keys * HT * DT,
        exps=HT * rows * cols * keys,
    )
    own_bias = lax.all_to_all(
        pair_bias, ("hi", "lo"), split_axis=0, concat_axis=0, axis_index_groups=[turns(high, low)]
    )

    outs = (shape((sample_count * own, width), BF16),)
    (attn_update,) = call(
        functools.partial(attend_kernel, share),
        outs,
        (own_bias, output_weight, *found, *values),
        scratch=(pltpu.VMEM((sample_count, own, width), F32), held(outs[0])),
        copies=1,
        near=range(2 + 2 * share),
        mib=48,
        flops=2 * sample_count * HD * own * tokens * width,
        exps=sample_count * HD * own * tokens,
    )
    return (new_pair, attn_update.reshape(sample_count, own, width))


def solution(mesh):
    ranks, col_count, groups = (mesh.shape[name] for name in ("row", "col", "smp"))
    low = math.gcd(col_count // ranks, 4)
    finer = jax.sharding.Mesh(
        mesh.devices.reshape(ranks, col_count // low, low, groups), ("row", "hi", "lo", "smp")
    )
    tile = P("row", ("hi", "lo"), None)
    return jax.shard_map(
        local,
        mesh=finer,
        in_specs=(tile, P(), P(), P(), P("smp", None, None), P("smp"), *[P()] * 7),
        out_specs=(tile, P("smp", ("row", "hi", "lo"), None)),
        check_vma=False,
    )
```

```python
import functools
import math

import jax
import jax.numpy as jnp
from jax import lax
from jax.experimental import pallas as pl
from jax.experimental.pallas import tpu as pltpu
from jax.sharding import PartitionSpec as P

HT = 4
DT = 32
CA = 768
HD = 16
DH = 48
NE = 256
LEVELS = 200

NORM_EPSILON = 1e-05
SIGMA_DATA = 16.0
SIGMA_MAX = 160.0
SIGMA_MIN = 0.0004


F32 = jnp.float32
BF16 = jnp.bfloat16
NT = (((1,), (1,)), ((), ()))


def normalize(values):
    values = values.astype(F32)
    average = jnp.mean(values, axis=-1, keepdims=True)
    centred = values - average
    variance = jnp.mean(centred * centred, axis=-1, keepdims=True)
    return centred * lax.rsqrt(variance + NORM_EPSILON)


def noise_features(levels):
    fraction = levels.astype(F32) / (LEVELS - 1)
    upper_root = SIGMA_MAX ** (1.0 / 7.0)
    lower_root = SIGMA_MIN ** (1.0 / 7.0)
    noise_sigma = SIGMA_DATA * (upper_root + fraction * (lower_root - upper_root)) ** 7
    scaled = 0.25 * jnp.log(noise_sigma / SIGMA_DATA)
    frequency = (
        2.0 * math.pi * jnp.exp(jnp.arange(NE // 2, dtype=F32) * (math.log(100.0) / (NE // 2)))
    )
    angles = scaled[:, None] * frequency[None, :]
    return jnp.concatenate([jnp.cos(angles), jnp.sin(angles)], axis=-1)


def nbytes(*shapes):
    return sum(math.prod(s.shape) * jnp.dtype(s.dtype).itemsize for s in shapes)


def held(operand):
    return pltpu.VMEM(operand.shape, operand.dtype)


def call(
    kernel, out_shape, operands, scratch=(), copies=0, after=(), near=(), mib=60, flops=0, exps=0
):
    in_specs = [
        pl.BlockSpec(memory_space=pltpu.VMEM if at in near else pltpu.HBM)
        for at in range(len(operands))
    ]
    in_specs += [pl.BlockSpec(memory_space=pl.ANY)] * len(after)
    moved = nbytes(*operands, *out_shape)
    count = len(operands)

    def body(*refs):
        kernel(*refs[:count], *refs[count + len(after) :])

    return pl.pallas_call(
        body,
        out_shape=out_shape,
        in_specs=in_specs,
        out_specs=tuple(pl.BlockSpec(memory_space=pltpu.HBM) for _ in out_shape),
        scratch_shapes=[*scratch, pltpu.SemaphoreType.DMA((copies,))],
        compiler_params=pltpu.CompilerParams(vmem_limit_bytes=mib << 20),
        cost_estimate=pl.CostEstimate(flops=flops, bytes_accessed=moved, transcendentals=exps),
    )(*operands, *after)


def start(pairs, sems, first=0):
    copies = [
        pltpu.make_async_copy(source, target, sems.at[first + at])
        for at, (source, target) in enumerate(pairs)
    ]
    for copy in copies:
        copy.start()
    return copies


def places(high, ranks, lo):
    span = high // ranks
    rest = [(h + lo % ranks * span) % high for h in range(high)]
    if lo % ranks == 0:
        rest = [h // span * span + span - 1 - h % span for h in rest]
    return rest


def turns(high, low):
    slow = [(high // 2 + high - 1 + at) % high for at in range(high)]
    return [h * low + lo for h in slow for lo in range(low)]


def hold(value, after):
    return pl.pallas_call(
        lambda *refs: None,
        out_shape=jax.ShapeDtypeStruct(value.shape, value.dtype),
        in_specs=[
            pl.BlockSpec(memory_space=pltpu.HBM),
            pl.BlockSpec(memory_space=pl.ANY),
        ],
        out_specs=pl.BlockSpec(memory_space=pltpu.HBM),
        input_output_aliases={0: 0},
        compiler_params=pltpu.CompilerParams(vmem_limit_bytes=48 << 20),
    )(value, after)


def own_place():
    low = lax.axis_size("lo")
    return lax.axis_index("hi") * low + lax.axis_index("lo"), lax.axis_size("hi") * low


def norm_kernel(pair_hbm, weight_hbm, bias_hbm, normed_hbm, pair, weight, wide, bias, normed, sems):
    rows, cols, channels = pair.shape
    pieces = 4
    some = rows // pieces
    slices = [pl.ds(at * some, some) for at in range(pieces)]
    loads = start([(weight_hbm, weight)] + [(pair_hbm.at[h], pair.at[h]) for h in slices], sems)
    for at, load in enumerate(loads[1:]):
        load.wait()
        tile = pair[at * some : (at + 1) * some].astype(F32).reshape(some * cols, channels)
        wide[at * some * cols : (at + 1) * some * cols, :] = normalize(tile)
    loads[0].wait()
    for col in range(cols):
        one = wide[pl.ds(col, rows, stride=cols), :].astype(BF16)
        normed[col] = one
        bias[:, col, :] = lax.dot_general(weight[...], one, NT, preferred_element_type=F32)
    copies = bias_hbm.shape[0]
    pairs = [(bias, bias_hbm.at[at]) for at in range(copies)] + [(normed, normed_hbm)]
    for copy in start(pairs, sems, 1 + pieces):
        copy.wait()


def first_sample(share, each, flip=0):
    return (lax.rem(lax.axis_index("lo"), share) ^ flip) * each


def condition_kernel(share, *refs):
    levels_hbm, cond_hbm, noise_hbm, modulation_hbm, samples_hbm, attention_hbm = refs[:6]
    key_hbm, value_hbm = refs[6:8]
    levels, cond, noise, modulation, samples, attention, key, value = refs[8:16]
    adapted, conditions, sems = refs[16:]
    count, tokens, width = samples.shape
    extra = (key.shape[1] - tokens) // 2
    first = first_sample(share, count)
    loads = start(
        [
            (levels_hbm, levels),
            (noise_hbm, noise),
            (cond_hbm, cond),
            (modulation_hbm, modulation),
            (samples_hbm.at[pl.ds(first, count)], samples),
            (attention_hbm.at[:, pl.ds(width, width)], attention.at[0]),
            (attention_hbm.at[:, pl.ds(2 * width, width)], attention.at[1]),
        ],
        sems,
    )
    loads[0].wait()
    row = lax.broadcasted_iota(jnp.int32, (8, NE // 2), 0)
    level = jnp.zeros((8, NE // 2), F32)
    for sample in range(count):
        level = jnp.where(row == sample, levels[first + sample].astype(F32), level)
    fraction = level / (LEVELS - 1)
    upper_root = SIGMA_MAX ** (1.0 / 7.0)
    lower_root = SIGMA_MIN ** (1.0 / 7.0)
    root = upper_root + fraction * (lower_root - upper_root)
    square = root * root
    sigma = SIGMA_DATA * (square * square * square * root)
    scaled = 0.25 * jnp.log(sigma / SIGMA_DATA)
    step = lax.broadcasted_iota(jnp.int32, scaled.shape, 1).astype(F32)
    angles = scaled * (2.0 * math.pi * jnp.exp(step * (math.log(100.0) / (NE // 2))))
    features = jnp.concatenate([jnp.cos(angles), jnp.sin(angles)], axis=-1).astype(BF16)
    loads[1].wait()
    terms = jnp.dot(features, noise[...], preferred_element_type=F32)
    for load in loads[2:4]:
        load.wait()

    loads[4].wait()
    for sample in range(count):
        trunk = cond[...].astype(F32) + terms[sample : sample + 1]
        conditioned = normalize(trunk).astype(BF16)
        conditions[sample] = conditioned
        modulated = jnp.dot(conditioned, modulation[...], preferred_element_type=F32)
        gain = jax.nn.sigmoid(modulated[:, :width])
        one = gain * normalize(samples[sample]) + modulated[:, width:]
        adapted[sample] = one.astype(BF16)
    place, places = own_place()
    chip = lax.div(lax.axis_index("row") * places + place, share) * extra
    here = pl.ds(pl.multiple_of(chip, extra), extra)
    key[:, tokens : tokens + extra, :] = adapted[:, here, :]
    key[:, tokens + extra :, : cond.shape[1]] = conditions[:, here, :]
    key[:, tokens + extra :, cond.shape[1] :] = jnp.zeros(
        (count, extra, width - cond.shape[1]), BF16
    )
    stores = []
    for at, (part, target) in enumerate(((key, key_hbm), (value, value_hbm))):
        loads[5 + at].wait()
        for sample in range(count):
            part[sample, :tokens, :] = jnp.dot(
                adapted[sample], attention[at], preferred_element_type=F32
            ).astype(BF16)
        stores += start([(part, target)], sems, 7 + at)
    for store in stores:
        store.wait()


def token_kernel(share, *refs):
    attention_hbm, gate_hbm, key_hbm = refs[:3]
    targets, refs = refs[3 : 3 + share], refs[3 + share :]
    attention, gate_weight, key, found, wide, sems = refs
    count, tokens, width = key.shape
    tokens = found.shape[2] - 2 * width // HD
    extra = (key.shape[1] - tokens) // 2
    own = extra // share
    loads = start(
        [
            (key_hbm, key),
            (attention_hbm.at[:, pl.ds(0, width)], attention.at[0]),
            (attention_hbm.at[:, pl.ds(3 * width, width)], attention.at[1]),
            (gate_hbm, gate_weight),
        ],
        sems,
    )
    for load in loads[:2]:
        load.wait()
    flat = key[:, tokens : tokens + extra, :].reshape(count * extra, width)
    raw = jnp.dot(flat, attention[0], preferred_element_type=F32)
    query = (raw * DH ** (-0.5)).astype(BF16).astype(F32)
    masks = head_masks(width)
    for sample in range(count):
        stacked = []
        for core in range(share):
            at = sample * extra + core * own
            one = query[at : at + own]
            stacked += [jnp.where(m, one, 0.0) for m in masks]
        stacked = jnp.concatenate(stacked, axis=0).astype(BF16)
        raw = lax.dot_general(key[sample, :tokens, :], stacked, NT, preferred_element_type=F32)
        for core in range(share):
            found[core, sample, :tokens, :] = raw[:, core * HD * own : (core + 1) * HD * own]
    loads[2].wait()
    wide[0] = jax.nn.sigmoid(jnp.dot(flat, attention[1], preferred_element_type=F32))
    loads[3].wait()
    flat = key[:, tokens + extra :, :].reshape(count * extra, width)[:, : gate_weight.shape[0]]
    wide[1] = jax.nn.sigmoid(jnp.dot(flat, gate_weight[...], preferred_element_type=F32))
    lanes = found.shape[3]
    for core in range(share):
        for sample in range(count):
            at = sample * extra + core * own
            to = tokens
            for kind in range(2):
                for lane in range(0, width, lanes):
                    found[core, sample, to : to + own, :] = wide[
                        kind, at : at + own, lane : lane + lanes
                    ]
                    to += own
    mine = lax.rem(lax.axis_index("lo"), share)
    stores = start(
        [(found.at[mine ^ flip], targets[flip]) for flip in range(share)], sems, len(loads)
    )
    for store in stores:
        store.wait()


def triangle_kernel(ranks, low, *refs):
    pair, weight, out_weight, bias_weight = refs[:4]
    gathered, refs = refs[4 : 4 + low], refs[4 + low :]
    normed_hbm, refs = refs[:ranks], refs[ranks:]
    new_hbm, pair_bias_hbm, refs = refs[0], refs[1], refs[2:]
    normed, new, pair_bias, refs = refs[0], refs[1], refs[2], refs[3:]
    bias_rows, bias, query, key, value, gate, wide = refs[:7]
    slots, (gated, renormed, sems) = (refs[7:10], refs[10:13]), refs[13:]
    rows, cols, channels = pair.shape
    width = HT * DT
    span = gathered[0].shape[1]
    loads = start([(normed_hbm[at], normed.at[at]) for at in range(ranks)], sems)
    row, fast = lax.axis_index("row"), lax.axis_index("lo")
    for flip in range(low):
        for slow in range(span):
            sender = fast ^ flip
            block = jnp.where(lax.rem(sender, ranks) == 0, span - 1 - slow, slow)
            first = pl.multiple_of((block * low + sender) * cols, cols)
            for source in range(ranks):
                step = lax.rem(source + ranks - row, ranks)
                bias_rows[step, :, pl.ds(first, cols), :] = gathered[flip][source, slow]
    turned = jnp.transpose(weight[...].astype(F32)).astype(BF16)
    for load in loads:
        load.wait()
    own_lines = jnp.concatenate([turned[:width], turned[2 * width :]], axis=0)
    peer_lines = turned[2 * width : 3 * width]
    batch = 4
    tiles = [(step, head) for step in range(ranks) for head in range(HT)]
    groups = cols // batch
    for group in range(groups):
        at = group * batch
        for step in range(ranks):
            some = normed[step, at : at + batch].reshape(batch * rows, channels)
            here = slice(step * rows, (step + 1) * rows)
            raw = jnp.dot(some, weight[:, width : 2 * width], preferred_element_type=F32)
            key[at : at + batch, here, :] = raw.astype(BF16).reshape(batch, rows, width)
            lines = own_lines if step == 0 else peer_lines
            raw = lax.dot_general(lines, some, NT, preferred_element_type=F32)
            for side in range(batch):
                part = raw[:, side * rows : (side + 1) * rows]
                if step == 0:
                    query[at + side] = (part[:width] * DT ** (-0.5)).astype(BF16)
                    gate[at + side] = jax.nn.sigmoid(part[2 * width :])
                    part = part[width : 2 * width]
                value[at + side, :, here] = part.astype(BF16)
        for step, head in tiles[group::groups]:
            bias[step * rows : (step + 1) * rows, head * rows : (head + 1) * rows] = jnp.transpose(
                bias_rows[step, head]
            )
    def score(col, slot):
        scores, peak, _ = slots[slot]
        own = query[col]
        blocks = []
        for head in range(HT):
            zeros = [jnp.zeros((size, rows), BF16) for size in (head * DT, width - (head + 1) * DT)]
            block = [zeros[0], own[head * DT : (head + 1) * DT], zeros[1]]
            blocks.append(jnp.concatenate([b for b in block if b.shape[0]], axis=0))
        stacked = jnp.concatenate(blocks, axis=1)
        raw = jnp.dot(key[col], stacked, preferred_element_type=F32) + bias[...]
        scores[...] = raw
        peak[...] = jnp.max(raw, axis=0, keepdims=True)

    def attend(col, slot):
        scores, peak, weights = slots[slot]
        exponent = jnp.exp(scores[...] - peak[...])
        scale = 1.0 / jnp.sum(exponent, axis=0, keepdims=True)
        weights[...] = exponent.astype(BF16)
        parts = []
        for head in range(0, HT, 2):
            here = slice(head * rows, (head + 2) * rows)
            summed = jnp.dot(
                value[col, head * DT : (head + 2) * DT, :],
                weights[:, here],
                preferred_element_type=F32,
            )
            summed = summed * scale[:, here]
            parts += [summed[:DT, :rows], summed[DT:, rows:]]
        gated[col] = (gate[col] * jnp.concatenate(parts, axis=0)).astype(BF16)

    score(0, 0)

    @pl.loop(0, cols // batch)
    def _(group):
        for side in range(batch):
            col = group * batch + side
            score(jnp.minimum(col + 1, cols - 1), (side + 1) % 2)
            attend(col, side % 2)

    for at in range(0, cols, batch):
        some = jnp.concatenate([gated[at + side] for side in range(batch)], axis=1)
        raw = lax.dot_general(
            some, out_weight[...], (((0,), (0,)), ((), ())), preferred_element_type=F32
        )
        for side in range(batch):
            wide[pl.ds(at + side, rows, stride=cols), :] = raw[side * rows : (side + 1) * rows]
    owners, _, lanes = pair_bias.shape
    own = rows // owners
    for owner in range(owners):
        here = slice(owner * own, (owner + 1) * own)
        some = pair[here].astype(F32).reshape(own * cols, channels)
        some = (some + wide[owner * own * cols : (owner + 1) * own * cols, :]).astype(BF16)
        new[here] = some.reshape(own, cols, channels)
        renormed[owner] = normalize(some).astype(BF16).reshape(own, cols, channels)
    stores = start([(new, new_hbm)], sems, len(loads))
    lane = lax.broadcasted_iota(jnp.int32, (lanes, HD), 0)
    pick = (lane // own == lax.broadcasted_iota(jnp.int32, (lanes, HD), 1)).astype(BF16)
    spread = jnp.dot(pick, bias_weight[...], preferred_element_type=F32)
    token_of = lax.rem(lax.broadcasted_iota(jnp.int32, (lanes, channels), 0), own)
    spots = [jnp.where(token_of == token, spread, 0.0).astype(BF16) for token in range(own)]
    flat = [renormed[:, token].reshape(owners * cols, channels) for token in range(own)]
    total = lax.dot_general(
        jnp.concatenate(flat, axis=1),
        jnp.concatenate(spots, axis=1),
        NT,
        preferred_element_type=F32,
    )
    total = total.reshape(owners, cols, lanes)
    for place, owner in enumerate(turns(owners // low, low)):
        pair_bias[place] = total[owner]
    stores += start([(pair_bias, pair_bias_hbm)], sems, len(loads) + 1)
    for store in stores:
        store.wait()


def head_masks(width):
    lane = lax.broadcasted_iota(jnp.int32, (1, width), 1)
    return [(lane >= head * DH) & (lane < (head + 1) * DH) for head in range(HD)]


def attend_kernel(share, *refs):
    bias, weight, refs = refs[0], refs[1], refs[2:]
    found, value, refs = refs[:share], refs[share : 2 * share], refs[2 * share :]
    out_hbm, wide, out, sems = refs
    count, own, width = wide.shape
    each, tokens, _ = value[0].shape
    low = lax.axis_size("lo")
    order = turns(bias.shape[0] // low, low)
    turned = jnp.concatenate([bias[order.index(c)] for c in range(len(order))], axis=0)
    masks = head_masks(width)
    ones = jnp.ones((tokens, turned.shape[1]), BF16)
    turn = (((0,), (0,)), ((), ()))
    slots = [(flip, at) for flip in range(share) for at in range(each)]
    rows = []
    for flip, at in slots:
        scores = found[flip][at, :tokens] + turned
        peak = jnp.max(scores, axis=0, keepdims=True)
        weights = jnp.exp(scores - peak).astype(BF16)
        summed = lax.dot_general(weights, value[flip][at], turn, preferred_element_type=F32)
        total = lax.dot_general(weights, ones, turn, preferred_element_type=F32)
        summed = summed * (1.0 / total[:, :1])
        attended = jnp.where(masks[0], summed[:own], 0.0)
        for head in range(1, HD):
            attended = jnp.where(masks[head], summed[head * own : (head + 1) * own], attended)
        rows.append(attended)

    def gates(kind):
        lanes = turned.shape[1]
        first = tokens + kind * own * (width // lanes)
        places = [slice(first + lane * own, first + (lane + 1) * own) for lane in range(width // lanes)]
        return jnp.concatenate(
            [
                jnp.concatenate([found[flip][at, place] for place in places], axis=1)
                for flip, at in slots
            ],
            axis=0,
        )

    gated = (gates(0) * jnp.concatenate(rows, axis=0)).astype(BF16)
    projected = gates(1) * jnp.dot(gated, weight[...], preferred_element_type=F32)
    for slot, (flip, at) in enumerate(slots):
        wide[first_sample(share, each, flip) + at] = projected[slot * own : (slot + 1) * own]
    out[...] = wide[...].reshape(count * own, width).astype(BF16)
    for store in start([(out, out_hbm)], sems):
        store.wait()


def local(
    pair_repr,
    tri_weight,
    tri_bias_weight,
    tri_output_weight,
    samples,
    levels,
    single_cond,
    noise_weight,
    modulation_weight,
    attention_weight,
    pair_bias_weight,
    output_weight,
    output_gate_weight,
):
    rows, cols, channels = pair_repr.shape
    ranks, high, low = (lax.axis_size(name) for name in ("row", "hi", "lo"))
    col_count = high * low
    sample_count, tokens, width = samples.shape
    own = rows // col_count
    span = high // ranks
    keys = ranks * rows
    shape = jax.ShapeDtypeStruct

    turned = jnp.transpose(tri_bias_weight)
    normed_shape = shape((cols, rows, channels), BF16)
    bias_shape = shape((HT, cols, rows), F32)
    wide = pltpu.VMEM((rows * cols, channels), F32)
    copies_shape = shape((ranks * high, *bias_shape.shape), F32)
    bias, normed = call(
        norm_kernel,
        (copies_shape, normed_shape),
        (pair_repr, turned),
        scratch=(held(pair_repr), held(turned), wide, held(bias_shape), held(normed_shape)),
        copies=6 + ranks * high,
        flops=2 * rows * cols * channels * HT,
    )
    groups = [
        [
            (r * high + h) * low + lo
            for r in range(ranks)
            for h in places(high, ranks, lo)
        ]
        for lo in range(low)
    ]
    placed = lax.all_to_all(
        bias, ("row", "hi", "lo"), split_axis=0, concat_axis=0, axis_index_groups=groups
    )
    peers = [
        lax.ppermute(normed, "row", [((r + step) % ranks, r) for r in range(ranks)])
        for step in range(1, ranks)
    ]

    share = 2 if low % 2 == 0 and sample_count % 2 == 0 else 1
    each = sample_count // share
    part = (each, tokens, width)
    extra = share * own
    key_shape = shape((each, tokens + 2 * extra, width), BF16)
    key, value = call(
        functools.partial(condition_kernel, share),
        (key_shape, shape(part, BF16)),
        (
            levels,
            single_cond,
            noise_weight,
            modulation_weight,
            samples,
            attention_weight,
        ),
        scratch=(
            pltpu.SMEM(levels.shape, levels.dtype),
            held(single_cond),
            held(noise_weight),
            held(modulation_weight),
            pltpu.VMEM(part, BF16),
            pltpu.VMEM((2, width, width), BF16),
            held(key_shape),
            pltpu.VMEM(part, BF16),
            pltpu.VMEM(part, BF16),
            pltpu.VMEM((each, *single_cond.shape), BF16),
        ),
        copies=9,
        after=(bias,),
        flops=4 * each * tokens * width * 2 * width,
        exps=each * tokens * width,
    )
    placed = placed.reshape(ranks, high, *bias_shape.shape)
    place = lax.axis_index("row") + ranks - lax.rem(lax.axis_index("lo"), ranks)
    gathered = [lax.dynamic_slice_in_dim(placed, lax.rem(place, ranks) * span, span, 1)]
    found_shape = shape((each, tokens + 2 * width // HD, HD * own), F32)
    found = list(
        call(
            functools.partial(token_kernel, share),
            (found_shape,) * share,
            (attention_weight, output_gate_weight, key),
            scratch=(
                pltpu.VMEM((2, width, width), BF16),
                held(output_gate_weight),
                held(key),
                pltpu.VMEM((share, *found_shape.shape), F32),
                pltpu.VMEM((2, each * extra, width), F32),
            ),
            copies=4 + share,
            after=(gathered[0],),
            mib=53,
            flops=64 * rows * cols * channels * HT * DT,
        )
    )
    bit = low // 2
    while bit:
        flip = [(c ^ bit, c) for c in range(low)]
        ready = [gathered[0], *(hold(part, found[0]) for part in gathered[1:])]
        more = [lax.ppermute(part, "lo", flip) for part in ready]
        gathered = [part for both in zip(ready, more) for part in both]
        bit //= 2
    values = [value]
    if share == 2:
        other = [(c ^ 1, c) for c in range(low)]
        values.append(lax.ppermute(value, "lo", other))
        found[1] = lax.ppermute(found[1], "lo", other)

    pair_weight = jnp.transpose(pair_bias_weight)
    outs = (shape((rows, cols, channels), BF16), shape((col_count, cols, HD * own), F32))
    new_pair, pair_bias = call(
        functools.partial(triangle_kernel, ranks, low),
        outs,
        (
            pair_repr,
            tri_weight,
            tri_output_weight,
            pair_weight,
            *gathered,
            normed,
            *peers,
        ),
        scratch=(
            pltpu.VMEM((ranks, cols, rows, channels), BF16),
            held(outs[0]),
            held(outs[1]),
            pltpu.VMEM((ranks, HT, rows, rows), F32),
            pltpu.VMEM((keys, HT * rows), F32),
            pltpu.VMEM((cols, HT * DT, rows), BF16),
            pltpu.VMEM((cols, keys, HT * DT), BF16),
            pltpu.VMEM((cols, HT * DT, keys), BF16),
            pltpu.VMEM((cols, HT * DT, rows), F32),
            wide,
            *[
                pltpu.VMEM(*slot)
                for slot in (
                    ((keys, HT * rows), F32),
                    ((1, HT * rows), F32),
                    ((keys, HT * rows), BF16),
                )
                * 2
            ],
            pltpu.VMEM((cols, HT * DT, rows), BF16),
            pltpu.VMEM((col_count, own, cols, channels), BF16),
        ),
        copies=2 + ranks,
        after=(found[0],),
        near=range(4 + low),
        mib=52,
        flops=4 * HT * rows * cols * keys * HT * DT,
        exps=HT * rows * cols * keys,
    )
    own_bias = lax.all_to_all(
        pair_bias, ("hi", "lo"), split_axis=0, concat_axis=0, axis_index_groups=[turns(high, low)]
    )

    outs = (shape((sample_count * own, width), BF16),)
    (attn_update,) = call(
        functools.partial(attend_kernel, share),
        outs,
        (own_bias, output_weight, *found, *values),
        scratch=(pltpu.VMEM((sample_count, own, width), F32), held(outs[0])),
        copies=1,
        near=range(2 + 2 * share),
        mib=48,
        flops=2 * sample_count * HD * own * tokens * width,
        exps=sample_count * HD * own * tokens,
    )
    return (new_pair, attn_update.reshape(sample_count, own, width))


def solution(mesh):
    ranks, col_count, groups = (mesh.shape[name] for name in ("row", "col", "smp"))
    low = math.gcd(col_count // ranks, 4)
    finer = jax.sharding.Mesh(
        mesh.devices.reshape(ranks, col_count // low, low, groups), ("row", "hi", "lo", "smp")
    )
    tile = P("row", ("hi", "lo"), None)
    return jax.shard_map(
        local,
        mesh=finer,
        in_specs=(tile, P(), P(), P(), P("smp", None, None), P("smp"), *[P()] * 7),
        out_specs=(tile, P("smp", ("row", "hi", "lo"), None)),
        check_vma=False,
    )
```

```python
import functools
import math

import jax
import jax.numpy as jnp
from jax import lax
from jax.experimental import pallas as pl
from jax.experimental.pallas import tpu as pltpu
from jax.sharding import PartitionSpec as P

HT = 4
DT = 32
CA = 768
HD = 16
DH = 48
NE = 256
LEVELS = 200

NORM_EPSILON = 1e-05
SIGMA_DATA = 16.0
SIGMA_MAX = 160.0
SIGMA_MIN = 0.0004


F32 = jnp.float32
BF16 = jnp.bfloat16
NT = (((1,), (1,)), ((), ()))


def normalize(values):
    values = values.astype(F32)
    average = jnp.mean(values, axis=-1, keepdims=True)
    centred = values - average
    variance = jnp.mean(centred * centred, axis=-1, keepdims=True)
    return centred * lax.rsqrt(variance + NORM_EPSILON)


def noise_features(levels):
    fraction = levels.astype(F32) / (LEVELS - 1)
    upper_root = SIGMA_MAX ** (1.0 / 7.0)
    lower_root = SIGMA_MIN ** (1.0 / 7.0)
    noise_sigma = SIGMA_DATA * (upper_root + fraction * (lower_root - upper_root)) ** 7
    scaled = 0.25 * jnp.log(noise_sigma / SIGMA_DATA)
    frequency = (
        2.0 * math.pi * jnp.exp(jnp.arange(NE // 2, dtype=F32) * (math.log(100.0) / (NE // 2)))
    )
    angles = scaled[:, None] * frequency[None, :]
    return jnp.concatenate([jnp.cos(angles), jnp.sin(angles)], axis=-1)


def nbytes(*shapes):
    return sum(math.prod(s.shape) * jnp.dtype(s.dtype).itemsize for s in shapes)


def held(operand):
    return pltpu.VMEM(operand.shape, operand.dtype)


def call(
    kernel, out_shape, operands, scratch=(), copies=0, after=(), near=(), mib=60, flops=0, exps=0
):
    in_specs = [
        pl.BlockSpec(memory_space=pltpu.VMEM if at in near else pltpu.HBM)
        for at in range(len(operands))
    ]
    in_specs += [pl.BlockSpec(memory_space=pl.ANY)] * len(after)
    moved = nbytes(*operands, *out_shape)
    count = len(operands)

    def body(*refs):
        kernel(*refs[:count], *refs[count + len(after) :])

    return pl.pallas_call(
        body,
        out_shape=out_shape,
        in_specs=in_specs,
        out_specs=tuple(pl.BlockSpec(memory_space=pltpu.HBM) for _ in out_shape),
        scratch_shapes=[*scratch, pltpu.SemaphoreType.DMA((copies,))],
        compiler_params=pltpu.CompilerParams(vmem_limit_bytes=mib << 20),
        cost_estimate=pl.CostEstimate(flops=flops, bytes_accessed=moved, transcendentals=exps),
    )(*operands, *after)


def start(pairs, sems, first=0):
    copies = [
        pltpu.make_async_copy(source, target, sems.at[first + at])
        for at, (source, target) in enumerate(pairs)
    ]
    for copy in copies:
        copy.start()
    return copies


def places(high, ranks, lo):
    span = high // ranks
    rest = [(h + lo % ranks * span) % high for h in range(high)]
    if lo % ranks == 0:
        rest = [h // span * span + span - 1 - h % span for h in rest]
    return rest


def turns(high, low):
    slow = sorted(range(high), key=lambda h: (h < high // 2, abs(2 * h - high)))
    return [h * low + lo for h in slow for lo in reversed(range(low))]


def hold(value, after):
    return pl.pallas_call(
        lambda *refs: None,
        out_shape=jax.ShapeDtypeStruct(value.shape, value.dtype),
        in_specs=[
            pl.BlockSpec(memory_space=pltpu.HBM),
            pl.BlockSpec(memory_space=pl.ANY),
        ],
        out_specs=pl.BlockSpec(memory_space=pltpu.HBM),
        input_output_aliases={0: 0},
        compiler_params=pltpu.CompilerParams(vmem_limit_bytes=48 << 20),
    )(value, after)


def own_place():
    low = lax.axis_size("lo")
    return lax.axis_index("hi") * low + lax.axis_index("lo"), lax.axis_size("hi") * low


def norm_kernel(pair_hbm, weight_hbm, bias_hbm, normed_hbm, pair, weight, wide, bias, normed, sems):
    rows, cols, channels = pair.shape
    pieces = 4
    some = rows // pieces
    slices = [pl.ds(at * some, some) for at in range(pieces)]
    loads = start([(weight_hbm, weight)] + [(pair_hbm.at[h], pair.at[h]) for h in slices], sems)
    for at, load in enumerate(loads[1:]):
        load.wait()
        tile = pair[at * some : (at + 1) * some].astype(F32).reshape(some * cols, channels)
        wide[at * some * cols : (at + 1) * some * cols, :] = normalize(tile)
    loads[0].wait()
    for col in range(cols):
        one = wide[pl.ds(col, rows, stride=cols), :].astype(BF16)
        normed[col] = one
        bias[:, col, :] = lax.dot_general(weight[...], one, NT, preferred_element_type=F32)
    copies = bias_hbm.shape[0]
    pairs = [(bias, bias_hbm.at[at]) for at in range(copies)] + [(normed, normed_hbm)]
    for copy in start(pairs, sems, 1 + pieces):
        copy.wait()


def first_sample(share, each, flip=0):
    return (lax.rem(lax.axis_index("lo"), share) ^ flip) * each


def condition_kernel(share, *refs):
    levels_hbm, cond_hbm, noise_hbm, modulation_hbm, samples_hbm, attention_hbm = refs[:6]
    key_hbm, value_hbm = refs[6:8]
    levels, cond, noise, modulation, samples, attention, key, value = refs[8:16]
    adapted, conditions, sems = refs[16:]
    count, tokens, width = samples.shape
    extra = (key.shape[1] - tokens) // 2
    first = first_sample(share, count)
    loads = start(
        [
            (levels_hbm, levels),
            (noise_hbm, noise),
            (cond_hbm, cond),
            (modulation_hbm, modulation),
            (samples_hbm.at[pl.ds(first, count)], samples),
            (attention_hbm.at[:, pl.ds(width, width)], attention.at[0]),
            (attention_hbm.at[:, pl.ds(2 * width, width)], attention.at[1]),
        ],
        sems,
    )
    loads[0].wait()
    row = lax.broadcasted_iota(jnp.int32, (8, NE // 2), 0)
    level = jnp.zeros((8, NE // 2), F32)
    for sample in range(count):
        level = jnp.where(row == sample, levels[first + sample].astype(F32), level)
    fraction = level / (LEVELS - 1)
    upper_root = SIGMA_MAX ** (1.0 / 7.0)
    lower_root = SIGMA_MIN ** (1.0 / 7.0)
    root = upper_root + fraction * (lower_root - upper_root)
    square = root * root
    sigma = SIGMA_DATA * (square * square * square * root)
    scaled = 0.25 * jnp.log(sigma / SIGMA_DATA)
    step = lax.broadcasted_iota(jnp.int32, scaled.shape, 1).astype(F32)
    angles = scaled * (2.0 * math.pi * jnp.exp(step * (math.log(100.0) / (NE // 2))))
    features = jnp.concatenate([jnp.cos(angles), jnp.sin(angles)], axis=-1).astype(BF16)
    loads[1].wait()
    terms = jnp.dot(features, noise[...], preferred_element_type=F32)
    for load in loads[2:4]:
        load.wait()

    loads[4].wait()
    for sample in range(count):
        trunk = cond[...].astype(F32) + terms[sample : sample + 1]
        conditioned = normalize(trunk).astype(BF16)
        conditions[sample] = conditioned
        modulated = jnp.dot(conditioned, modulation[...], preferred_element_type=F32)
        gain = jax.nn.sigmoid(modulated[:, :width])
        one = gain * normalize(samples[sample]) + modulated[:, width:]
        adapted[sample] = one.astype(BF16)
    place, places = own_place()
    chip = lax.div(lax.axis_index("row") * places + place, share) * extra
    here = pl.ds(pl.multiple_of(chip, extra), extra)
    key[:, tokens : tokens + extra, :] = adapted[:, here, :]
    key[:, tokens + extra :, : cond.shape[1]] = conditions[:, here, :]
    key[:, tokens + extra :, cond.shape[1] :] = jnp.zeros(
        (count, extra, width - cond.shape[1]), BF16
    )
    stores = []
    for at, (part, target) in enumerate(((key, key_hbm), (value, value_hbm))):
        loads[5 + at].wait()
        for sample in range(count):
            part[sample, :tokens, :] = jnp.dot(
                adapted[sample], attention[at], preferred_element_type=F32
            ).astype(BF16)
        stores += start([(part, target)], sems, 7 + at)
    for store in stores:
        store.wait()


def token_kernel(share, *refs):
    attention_hbm, gate_hbm, key_hbm = refs[:3]
    targets, refs = refs[3 : 3 + share], refs[3 + share :]
    attention, gate_weight, key, found, wide, sems = refs
    count, tokens, width = key.shape
    tokens = found.shape[2] - 2 * width // HD
    extra = (key.shape[1] - tokens) // 2
    own = extra // share
    loads = start(
        [
            (key_hbm, key),
            (attention_hbm.at[:, pl.ds(0, width)], attention.at[0]),
            (attention_hbm.at[:, pl.ds(3 * width, width)], attention.at[1]),
            (gate_hbm, gate_weight),
        ],
        sems,
    )
    for load in loads[:2]:
        load.wait()
    flat = key[:, tokens : tokens + extra, :].reshape(count * extra, width)
    raw = jnp.dot(flat, attention[0], preferred_element_type=F32)
    query = (raw * DH ** (-0.5)).astype(BF16).astype(F32)
    masks = head_masks(width)
    for sample in range(count):
        stacked = []
        for core in range(share):
            at = sample * extra + core * own
            one = query[at : at + own]
            stacked += [jnp.where(m, one, 0.0) for m in masks]
        stacked = jnp.concatenate(stacked, axis=0).astype(BF16)
        raw = lax.dot_general(key[sample, :tokens, :], stacked, NT, preferred_element_type=F32)
        for core in range(share):
            found[core, sample, :tokens, :] = raw[:, core * HD * own : (core + 1) * HD * own]
    loads[2].wait()
    wide[0] = jax.nn.sigmoid(jnp.dot(flat, attention[1], preferred_element_type=F32))
    loads[3].wait()
    flat = key[:, tokens + extra :, :].reshape(count * extra, width)[:, : gate_weight.shape[0]]
    wide[1] = jax.nn.sigmoid(jnp.dot(flat, gate_weight[...], preferred_element_type=F32))
    lanes = found.shape[3]
    for core in range(share):
        for sample in range(count):
            at = sample * extra + core * own
            to = tokens
            for kind in range(2):
                for lane in range(0, width, lanes):
                    found[core, sample, to : to + own, :] = wide[
                        kind, at : at + own, lane : lane + lanes
                    ]
                    to += own
    mine = lax.rem(lax.axis_index("lo"), share)
    stores = start(
        [(found.at[mine ^ flip], targets[flip]) for flip in range(share)], sems, len(loads)
    )
    for store in stores:
        store.wait()


def triangle_kernel(ranks, low, *refs):
    pair, weight, out_weight, bias_weight = refs[:4]
    gathered, refs = refs[4 : 4 + low], refs[4 + low :]
    normed_hbm, refs = refs[:ranks], refs[ranks:]
    new_hbm, pair_bias_hbm, refs = refs[0], refs[1], refs[2:]
    normed, new, pair_bias, refs = refs[0], refs[1], refs[2], refs[3:]
    bias_rows, bias, query, key, value, gate, wide = refs[:7]
    slots, (gated, renormed, sems) = (refs[7:10], refs[10:13]), refs[13:]
    rows, cols, channels = pair.shape
    width = HT * DT
    span = gathered[0].shape[1]
    loads = start([(normed_hbm[at], normed.at[at]) for at in range(ranks)], sems)
    row, fast = lax.axis_index("row"), lax.axis_index("lo")
    for flip in range(low):
        for slow in range(span):
            sender = fast ^ flip
            block = jnp.where(lax.rem(sender, ranks) == 0, span - 1 - slow, slow)
            first = pl.multiple_of((block * low + sender) * cols, cols)
            for source in range(ranks):
                step = lax.rem(source + ranks - row, ranks)
                bias_rows[step, :, pl.ds(first, cols), :] = gathered[flip][source, slow]
    turned = jnp.transpose(weight[...].astype(F32)).astype(BF16)
    for load in loads:
        load.wait()
    own_lines = jnp.concatenate([turned[:width], turned[2 * width :]], axis=0)
    peer_lines = turned[2 * width : 3 * width]
    batch = 4
    tiles = [(step, head) for step in range(ranks) for head in range(HT)]
    groups = cols // batch
    for group in range(groups):
        at = group * batch
        for step in range(ranks):
            some = normed[step, at : at + batch].reshape(batch * rows, channels)
            here = slice(step * rows, (step + 1) * rows)
            raw = jnp.dot(some, weight[:, width : 2 * width], preferred_element_type=F32)
            key[at : at + batch, here, :] = raw.astype(BF16).reshape(batch, rows, width)
            lines = own_lines if step == 0 else peer_lines
            raw = lax.dot_general(lines, some, NT, preferred_element_type=F32)
            for side in range(batch):
                part = raw[:, side * rows : (side + 1) * rows]
                if step == 0:
                    query[at + side] = (part[:width] * DT ** (-0.5)).astype(BF16)
                    gate[at + side] = jax.nn.sigmoid(part[2 * width :])
                    part = part[width : 2 * width]
                value[at + side, :, here] = part.astype(BF16)
        for step, head in tiles[group::groups]:
            bias[step * rows : (step + 1) * rows, head * rows : (head + 1) * rows] = jnp.transpose(
                bias_rows[step, head]
            )
    def score(col, slot):
        scores, peak, _ = slots[slot]
        own = query[col]
        blocks = []
        for head in range(HT):
            zeros = [jnp.zeros((size, rows), BF16) for size in (head * DT, width - (head + 1) * DT)]
            block = [zeros[0], own[head * DT : (head + 1) * DT], zeros[1]]
            blocks.append(jnp.concatenate([b for b in block if b.shape[0]], axis=0))
        stacked = jnp.concatenate(blocks, axis=1)
        raw = jnp.dot(key[col], stacked, preferred_element_type=F32) + bias[...]
        scores[...] = raw
        peak[...] = jnp.max(raw, axis=0, keepdims=True)

    def attend(col, slot):
        scores, peak, weights = slots[slot]
        exponent = jnp.exp(scores[...] - peak[...])
        scale = 1.0 / jnp.sum(exponent, axis=0, keepdims=True)
        weights[...] = exponent.astype(BF16)
        parts = []
        for head in range(0, HT, 2):
            here = slice(head * rows, (head + 2) * rows)
            summed = jnp.dot(
                value[col, head * DT : (head + 2) * DT, :],
                weights[:, here],
                preferred_element_type=F32,
            )
            summed = summed * scale[:, here]
            parts += [summed[:DT, :rows], summed[DT:, rows:]]
        gated[col] = (gate[col] * jnp.concatenate(parts, axis=0)).astype(BF16)

    score(0, 0)

    @pl.loop(0, cols // batch)
    def _(group):
        for side in range(batch):
            col = group * batch + side
            score(jnp.minimum(col + 1, cols - 1), (side + 1) % 2)
            attend(col, side % 2)

    for at in range(0, cols, batch):
        some = jnp.concatenate([gated[at + side] for side in range(batch)], axis=1)
        raw = lax.dot_general(
            some, out_weight[...], (((0,), (0,)), ((), ())), preferred_element_type=F32
        )
        for side in range(batch):
            wide[pl.ds(at + side, rows, stride=cols), :] = raw[side * rows : (side + 1) * rows]
    owners, _, lanes = pair_bias.shape
    own = rows // owners
    for owner in range(owners):
        here = slice(owner * own, (owner + 1) * own)
        some = pair[here].astype(F32).reshape(own * cols, channels)
        some = (some + wide[owner * own * cols : (owner + 1) * own * cols, :]).astype(BF16)
        new[here] = some.reshape(own, cols, channels)
        renormed[owner] = normalize(some).astype(BF16).reshape(own, cols, channels)
    stores = start([(new, new_hbm)], sems, len(loads))
    lane = lax.broadcasted_iota(jnp.int32, (lanes, HD), 0)
    pick = (lane // own == lax.broadcasted_iota(jnp.int32, (lanes, HD), 1)).astype(BF16)
    spread = jnp.dot(pick, bias_weight[...], preferred_element_type=F32)
    token_of = lax.rem(lax.broadcasted_iota(jnp.int32, (lanes, channels), 0), own)
    spots = [jnp.where(token_of == token, spread, 0.0).astype(BF16) for token in range(own)]
    flat = [renormed[:, token].reshape(owners * cols, channels) for token in range(own)]
    total = lax.dot_general(
        jnp.concatenate(flat, axis=1),
        jnp.concatenate(spots, axis=1),
        NT,
        preferred_element_type=F32,
    )
    total = total.reshape(owners, cols, lanes)
    for place, owner in enumerate(turns(owners // low, low)):
        pair_bias[place] = total[owner]
    stores += start([(pair_bias, pair_bias_hbm)], sems, len(loads) + 1)
    for store in stores:
        store.wait()


def head_masks(width):
    lane = lax.broadcasted_iota(jnp.int32, (1, width), 1)
    return [(lane >= head * DH) & (lane < (head + 1) * DH) for head in range(HD)]


def attend_kernel(share, *refs):
    bias, weight, refs = refs[0], refs[1], refs[2:]
    found, value, refs = refs[:share], refs[share : 2 * share], refs[2 * share :]
    out_hbm, wide, out, sems = refs
    count, own, width = wide.shape
    each, tokens, _ = value[0].shape
    low = lax.axis_size("lo")
    order = turns(bias.shape[0] // low, low)
    turned = jnp.concatenate([bias[order.index(c)] for c in range(len(order))], axis=0)
    masks = head_masks(width)
    ones = jnp.ones((tokens, turned.shape[1]), BF16)
    turn = (((0,), (0,)), ((), ()))
    slots = [(flip, at) for flip in range(share) for at in range(each)]
    rows = []
    for flip, at in slots:
        scores = found[flip][at, :tokens] + turned
        peak = jnp.max(scores, axis=0, keepdims=True)
        weights = jnp.exp(scores - peak).astype(BF16)
        summed = lax.dot_general(weights, value[flip][at], turn, preferred_element_type=F32)
        total = lax.dot_general(weights, ones, turn, preferred_element_type=F32)
        summed = summed * (1.0 / total[:, :1])
        attended = jnp.where(masks[0], summed[:own], 0.0)
        for head in range(1, HD):
            attended = jnp.where(masks[head], summed[head * own : (head + 1) * own], attended)
        rows.append(attended)

    def gates(kind):
        lanes = turned.shape[1]
        first = tokens + kind * own * (width // lanes)
        places = [slice(first + lane * own, first + (lane + 1) * own) for lane in range(width // lanes)]
        return jnp.concatenate(
            [
                jnp.concatenate([found[flip][at, place] for place in places], axis=1)
                for flip, at in slots
            ],
            axis=0,
        )

    gated = (gates(0) * jnp.concatenate(rows, axis=0)).astype(BF16)
    projected = gates(1) * jnp.dot(gated, weight[...], preferred_element_type=F32)
    for slot, (flip, at) in enumerate(slots):
        wide[first_sample(share, each, flip) + at] = projected[slot * own : (slot + 1) * own]
    out[...] = wide[...].reshape(count * own, width).astype(BF16)
    for store in start([(out, out_hbm)], sems):
        store.wait()


def local(
    pair_repr,
    tri_weight,
    tri_bias_weight,
    tri_output_weight,
    samples,
    levels,
    single_cond,
    noise_weight,
    modulation_weight,
    attention_weight,
    pair_bias_weight,
    output_weight,
    output_gate_weight,
):
    rows, cols, channels = pair_repr.shape
    ranks, high, low = (lax.axis_size(name) for name in ("row", "hi", "lo"))
    col_count = high * low
    sample_count, tokens, width = samples.shape
    own = rows // col_count
    span = high // ranks
    keys = ranks * rows
    shape = jax.ShapeDtypeStruct

    turned = jnp.transpose(tri_bias_weight)
    normed_shape = shape((cols, rows, channels), BF16)
    bias_shape = shape((HT, cols, rows), F32)
    wide = pltpu.VMEM((rows * cols, channels), F32)
    copies_shape = shape((ranks * high, *bias_shape.shape), F32)
    bias, normed = call(
        norm_kernel,
        (copies_shape, normed_shape),
        (pair_repr, turned),
        scratch=(held(pair_repr), held(turned), wide, held(bias_shape), held(normed_shape)),
        copies=6 + ranks * high,
        flops=2 * rows * cols * channels * HT,
    )
    groups = [
        [
            (r * high + h) * low + lo
            for r in range(ranks)
            for h in places(high, ranks, lo)
        ]
        for lo in range(low)
    ]
    placed = lax.all_to_all(
        bias, ("row", "hi", "lo"), split_axis=0, concat_axis=0, axis_index_groups=groups
    )
    peers = [
        lax.ppermute(normed, "row", [((r + step) % ranks, r) for r in range(ranks)])
        for step in range(1, ranks)
    ]

    share = 2 if low % 2 == 0 and sample_count % 2 == 0 else 1
    each = sample_count // share
    part = (each, tokens, width)
    extra = share * own
    key_shape = shape((each, tokens + 2 * extra, width), BF16)
    key, value = call(
        functools.partial(condition_kernel, share),
        (key_shape, shape(part, BF16)),
        (
            levels,
            single_cond,
            noise_weight,
            modulation_weight,
            samples,
            attention_weight,
        ),
        scratch=(
            pltpu.SMEM(levels.shape, levels.dtype),
            held(single_cond),
            held(noise_weight),
            held(modulation_weight),
            pltpu.VMEM(part, BF16),
            pltpu.VMEM((2, width, width), BF16),
            held(key_shape),
            pltpu.VMEM(part, BF16),
            pltpu.VMEM(part, BF16),
            pltpu.VMEM((each, *single_cond.shape), BF16),
        ),
        copies=9,
        after=(bias,),
        flops=4 * each * tokens * width * 2 * width,
        exps=each * tokens * width,
    )
    placed = placed.reshape(ranks, high, *bias_shape.shape)
    place = lax.axis_index("row") + ranks - lax.rem(lax.axis_index("lo"), ranks)
    gathered = [lax.dynamic_slice_in_dim(placed, lax.rem(place, ranks) * span, span, 1)]
    found_shape = shape((each, tokens + 2 * width // HD, HD * own), F32)
    found = list(
        call(
            functools.partial(token_kernel, share),
            (found_shape,) * share,
            (attention_weight, output_gate_weight, key),
            scratch=(
                pltpu.VMEM((2, width, width), BF16),
                held(output_gate_weight),
                held(key),
                pltpu.VMEM((share, *found_shape.shape), F32),
                pltpu.VMEM((2, each * extra, width), F32),
            ),
            copies=4 + share,
            after=(gathered[0],),
            mib=53,
            flops=64 * rows * cols * channels * HT * DT,
        )
    )
    bit = low // 2
    while bit:
        flip = [(c ^ bit, c) for c in range(low)]
        ready = [gathered[0], *(hold(part, found[0]) for part in gathered[1:])]
        more = [lax.ppermute(part, "lo", flip) for part in ready]
        gathered = [part for both in zip(ready, more) for part in both]
        bit //= 2
    values = [value]
    if share == 2:
        other = [(c ^ 1, c) for c in range(low)]
        values.append(lax.ppermute(value, "lo", other))
        found[1] = lax.ppermute(found[1], "lo", other)

    pair_weight = jnp.transpose(pair_bias_weight)
    outs = (shape((rows, cols, channels), BF16), shape((col_count, cols, HD * own), F32))
    new_pair, pair_bias = call(
        functools.partial(triangle_kernel, ranks, low),
        outs,
        (
            pair_repr,
            tri_weight,
            tri_output_weight,
            pair_weight,
            *gathered,
            normed,
            *peers,
        ),
        scratch=(
            pltpu.VMEM((ranks, cols, rows, channels), BF16),
            held(outs[0]),
            held(outs[1]),
            pltpu.VMEM((ranks, HT, rows, rows), F32),
            pltpu.VMEM((keys, HT * rows), F32),
            pltpu.VMEM((cols, HT * DT, rows), BF16),
            pltpu.VMEM((cols, keys, HT * DT), BF16),
            pltpu.VMEM((cols, HT * DT, keys), BF16),
            pltpu.VMEM((cols, HT * DT, rows), F32),
            wide,
            *[
                pltpu.VMEM(*slot)
                for slot in (
                    ((keys, HT * rows), F32),
                    ((1, HT * rows), F32),
                    ((keys, HT * rows), BF16),
                )
                * 2
            ],
            pltpu.VMEM((cols, HT * DT, rows), BF16),
            pltpu.VMEM((col_count, own, cols, channels), BF16),
        ),
        copies=2 + ranks,
        after=(found[0],),
        near=range(4 + low),
        mib=52,
        flops=4 * HT * rows * cols * keys * HT * DT,
        exps=HT * rows * cols * keys,
    )
    own_bias = lax.all_to_all(
        pair_bias, ("hi", "lo"), split_axis=0, concat_axis=0, axis_index_groups=[turns(high, low)]
    )

    outs = (shape((sample_count * own, width), BF16),)
    (attn_update,) = call(
        functools.partial(attend_kernel, share),
        outs,
        (own_bias, output_weight, *found, *values),
        scratch=(pltpu.VMEM((sample_count, own, width), F32), held(outs[0])),
        copies=1,
        near=range(2 + 2 * share),
        mib=48,
        flops=2 * sample_count * HD * own * tokens * width,
        exps=sample_count * HD * own * tokens,
    )
    return (new_pair, attn_update.reshape(sample_count, own, width))


def solution(mesh):
    ranks, col_count, groups = (mesh.shape[name] for name in ("row", "col", "smp"))
    low = math.gcd(col_count // ranks, 4)
    finer = jax.sharding.Mesh(
        mesh.devices.reshape(ranks, col_count // low, low, groups), ("row", "hi", "lo", "smp")
    )
    tile = P("row", ("hi", "lo"), None)
    return jax.shard_map(
        local,
        mesh=finer,
        in_specs=(tile, P(), P(), P(), P("smp", None, None), P("smp"), *[P()] * 7),
        out_specs=(tile, P("smp", ("row", "hi", "lo"), None)),
        check_vma=False,
    )
```

```python
import functools
import math

import jax
import jax.numpy as jnp
from jax import lax
from jax.experimental import pallas as pl
from jax.experimental.pallas import tpu as pltpu
from jax.sharding import PartitionSpec as P

HT = 4
DT = 32
CA = 768
HD = 16
DH = 48
NE = 256
LEVELS = 200

NORM_EPSILON = 1e-05
SIGMA_DATA = 16.0
SIGMA_MAX = 160.0
SIGMA_MIN = 0.0004


F32 = jnp.float32
BF16 = jnp.bfloat16
NT = (((1,), (1,)), ((), ()))


def normalize(values):
    values = values.astype(F32)
    average = jnp.mean(values, axis=-1, keepdims=True)
    centred = values - average
    variance = jnp.mean(centred * centred, axis=-1, keepdims=True)
    return centred * lax.rsqrt(variance + NORM_EPSILON)


def noise_features(levels):
    fraction = levels.astype(F32) / (LEVELS - 1)
    upper_root = SIGMA_MAX ** (1.0 / 7.0)
    lower_root = SIGMA_MIN ** (1.0 / 7.0)
    noise_sigma = SIGMA_DATA * (upper_root + fraction * (lower_root - upper_root)) ** 7
    scaled = 0.25 * jnp.log(noise_sigma / SIGMA_DATA)
    frequency = (
        2.0 * math.pi * jnp.exp(jnp.arange(NE // 2, dtype=F32) * (math.log(100.0) / (NE // 2)))
    )
    angles = scaled[:, None] * frequency[None, :]
    return jnp.concatenate([jnp.cos(angles), jnp.sin(angles)], axis=-1)


def nbytes(*shapes):
    return sum(math.prod(s.shape) * jnp.dtype(s.dtype).itemsize for s in shapes)


def held(operand):
    return pltpu.VMEM(operand.shape, operand.dtype)


def call(
    kernel, out_shape, operands, scratch=(), copies=0, after=(), near=(), mib=60, flops=0, exps=0
):
    in_specs = [
        pl.BlockSpec(memory_space=pltpu.VMEM if at in near else pltpu.HBM)
        for at in range(len(operands))
    ]
    in_specs += [pl.BlockSpec(memory_space=pl.ANY)] * len(after)
    moved = nbytes(*operands, *out_shape)
    count = len(operands)

    def body(*refs):
        kernel(*refs[:count], *refs[count + len(after) :])

    return pl.pallas_call(
        body,
        out_shape=out_shape,
        in_specs=in_specs,
        out_specs=tuple(pl.BlockSpec(memory_space=pltpu.HBM) for _ in out_shape),
        scratch_shapes=[*scratch, pltpu.SemaphoreType.DMA((copies,))],
        compiler_params=pltpu.CompilerParams(vmem_limit_bytes=mib << 20),
        cost_estimate=pl.CostEstimate(flops=flops, bytes_accessed=moved, transcendentals=exps),
    )(*operands, *after)


def start(pairs, sems, first=0):
    copies = [
        pltpu.make_async_copy(source, target, sems.at[first + at])
        for at, (source, target) in enumerate(pairs)
    ]
    for copy in copies:
        copy.start()
    return copies


def places(high, ranks, lo):
    span = high // ranks
    rest = [(h + lo % ranks * span) % high for h in range(high)]
    if lo % ranks == 0:
        rest = [h // span * span + span - 1 - h % span for h in rest]
    return rest


def turns(high, low):
    slow = sorted(range(high), key=lambda h: (h < high // 2, abs(2 * h - high)))
    return [h * low + lo for h in slow for lo in reversed(range(low))]


def hold(value, after):
    return pl.pallas_call(
        lambda *refs: None,
        out_shape=jax.ShapeDtypeStruct(value.shape, value.dtype),
        in_specs=[
            pl.BlockSpec(memory_space=pltpu.HBM),
            pl.BlockSpec(memory_space=pl.ANY),
        ],
        out_specs=pl.BlockSpec(memory_space=pltpu.HBM),
        input_output_aliases={0: 0},
        compiler_params=pltpu.CompilerParams(vmem_limit_bytes=48 << 20),
    )(value, after)


def own_place():
    low = lax.axis_size("lo")
    return lax.axis_index("hi") * low + lax.axis_index("lo"), lax.axis_size("hi") * low


def norm_kernel(pair_hbm, weight_hbm, bias_hbm, normed_hbm, pair, weight, wide, bias, normed, sems):
    rows, cols, channels = pair.shape
    pieces = 4
    some = rows // pieces
    slices = [pl.ds(at * some, some) for at in range(pieces)]
    loads = start([(weight_hbm, weight)] + [(pair_hbm.at[h], pair.at[h]) for h in slices], sems)
    for at, load in enumerate(loads[1:]):
        load.wait()
        tile = pair[at * some : (at + 1) * some].astype(F32).reshape(some * cols, channels)
        wide[at * some * cols : (at + 1) * some * cols, :] = normalize(tile)
    loads[0].wait()
    for col in range(cols):
        one = wide[pl.ds(col, rows, stride=cols), :].astype(BF16)
        normed[col] = one
        bias[:, col, :] = lax.dot_general(weight[...], one, NT, preferred_element_type=F32)
    copies = bias_hbm.shape[0]
    pairs = [(bias, bias_hbm.at[at]) for at in range(copies)] + [(normed, normed_hbm)]
    for copy in start(pairs, sems, 1 + pieces):
        copy.wait()


def first_sample(share, each, flip=0):
    return (lax.rem(lax.axis_index("lo"), share) ^ flip) * each


def condition_kernel(share, *refs):
    levels_hbm, cond_hbm, noise_hbm, modulation_hbm, samples_hbm, attention_hbm = refs[:6]
    key_hbm, value_hbm = refs[6:8]
    levels, cond, noise, modulation, samples, attention, key, value = refs[8:16]
    adapted, conditions, sems = refs[16:]
    count, tokens, width = samples.shape
    extra = (key.shape[1] - tokens) // 2
    first = first_sample(share, count)
    loads = start(
        [
            (levels_hbm, levels),
            (noise_hbm, noise),
            (cond_hbm, cond),
            (modulation_hbm, modulation),
            (samples_hbm.at[pl.ds(first, count)], samples),
            (attention_hbm.at[:, pl.ds(width, width)], attention.at[0]),
            (attention_hbm.at[:, pl.ds(2 * width, width)], attention.at[1]),
        ],
        sems,
    )
    loads[0].wait()
    row = lax.broadcasted_iota(jnp.int32, (8, NE // 2), 0)
    level = jnp.zeros((8, NE // 2), F32)
    for sample in range(count):
        level = jnp.where(row == sample, levels[first + sample].astype(F32), level)
    fraction = level / (LEVELS - 1)
    upper_root = SIGMA_MAX ** (1.0 / 7.0)
    lower_root = SIGMA_MIN ** (1.0 / 7.0)
    root = upper_root + fraction * (lower_root - upper_root)
    square = root * root
    sigma = SIGMA_DATA * (square * square * square * root)
    scaled = 0.25 * jnp.log(sigma / SIGMA_DATA)
    step = lax.broadcasted_iota(jnp.int32, scaled.shape, 1).astype(F32)
    angles = scaled * (2.0 * math.pi * jnp.exp(step * (math.log(100.0) / (NE // 2))))
    features = jnp.concatenate([jnp.cos(angles), jnp.sin(angles)], axis=-1).astype(BF16)
    loads[1].wait()
    terms = jnp.dot(features, noise[...], preferred_element_type=F32)
    for load in loads[2:4]:
        load.wait()

    loads[4].wait()
    for sample in range(count):
        trunk = cond[...].astype(F32) + terms[sample : sample + 1]
        conditioned = normalize(trunk).astype(BF16)
        conditions[sample] = conditioned
        modulated = jnp.dot(conditioned, modulation[...], preferred_element_type=F32)
        gain = jax.nn.sigmoid(modulated[:, :width])
        one = gain * normalize(samples[sample]) + modulated[:, width:]
        adapted[sample] = one.astype(BF16)
    place, places = own_place()
    chip = lax.div(lax.axis_index("row") * places + place, share) * extra
    here = pl.ds(pl.multiple_of(chip, extra), extra)
    key[:, tokens : tokens + extra, :] = adapted[:, here, :]
    key[:, tokens + extra :, : cond.shape[1]] = conditions[:, here, :]
    key[:, tokens + extra :, cond.shape[1] :] = jnp.zeros(
        (count, extra, width - cond.shape[1]), BF16
    )
    stores = []
    for at, (part, target) in enumerate(((key, key_hbm), (value, value_hbm))):
        loads[5 + at].wait()
        for sample in range(count):
            part[sample, :tokens, :] = jnp.dot(
                adapted[sample], attention[at], preferred_element_type=F32
            ).astype(BF16)
        stores += start([(part, target)], sems, 7 + at)
    for store in stores:
        store.wait()


def token_kernel(share, *refs):
    attention_hbm, gate_hbm, key_hbm = refs[:3]
    targets, refs = refs[3 : 3 + share], refs[3 + share :]
    attention, gate_weight, key, found, wide, sems = refs
    count, tokens, width = key.shape
    tokens = found.shape[2] - 2 * width // HD
    extra = (key.shape[1] - tokens) // 2
    own = extra // share
    loads = start(
        [
            (key_hbm, key),
            (attention_hbm.at[:, pl.ds(0, width)], attention.at[0]),
            (attention_hbm.at[:, pl.ds(3 * width, width)], attention.at[1]),
            (gate_hbm, gate_weight),
        ],
        sems,
    )
    for load in loads[:2]:
        load.wait()
    flat = key[:, tokens : tokens + extra, :].reshape(count * extra, width)
    raw = jnp.dot(flat, attention[0], preferred_element_type=F32)
    query = (raw * DH ** (-0.5)).astype(BF16).astype(F32)
    masks = head_masks(width)
    for sample in range(count):
        stacked = []
        for core in range(share):
            at = sample * extra + core * own
            one = query[at : at + own]
            stacked += [jnp.where(m, one, 0.0) for m in masks]
        stacked = jnp.concatenate(stacked, axis=0).astype(BF16)
        raw = lax.dot_general(key[sample, :tokens, :], stacked, NT, preferred_element_type=F32)
        for core in range(share):
            found[core, sample, :tokens, :] = raw[:, core * HD * own : (core + 1) * HD * own]
    loads[2].wait()
    wide[0] = jax.nn.sigmoid(jnp.dot(flat, attention[1], preferred_element_type=F32))
    loads[3].wait()
    flat = key[:, tokens + extra :, :].reshape(count * extra, width)[:, : gate_weight.shape[0]]
    wide[1] = jax.nn.sigmoid(jnp.dot(flat, gate_weight[...], preferred_element_type=F32))
    lanes = found.shape[3]
    for core in range(share):
        for sample in range(count):
            at = sample * extra + core * own
            to = tokens
            for kind in range(2):
                for lane in range(0, width, lanes):
                    found[core, sample, to : to + own, :] = wide[
                        kind, at : at + own, lane : lane + lanes
                    ]
                    to += own
    mine = lax.rem(lax.axis_index("lo"), share)
    stores = start(
        [(found.at[mine ^ flip], targets[flip]) for flip in range(share)], sems, len(loads)
    )
    for store in stores:
        store.wait()


def triangle_kernel(ranks, low, *refs):
    pair, weight, out_weight, bias_weight = refs[:4]
    gathered, refs = refs[4 : 4 + low], refs[4 + low :]
    normed_hbm, refs = refs[:ranks], refs[ranks:]
    new_hbm, pair_bias_hbm, refs = refs[0], refs[1], refs[2:]
    normed, new, pair_bias, refs = refs[0], refs[1], refs[2], refs[3:]
    bias_rows, bias, query, key, value, gate, wide = refs[:7]
    slots, (gated, renormed, sems) = (refs[7:10], refs[10:13]), refs[13:]
    rows, cols, channels = pair.shape
    width = HT * DT
    span = gathered[0].shape[1]
    loads = start([(normed_hbm[at], normed.at[at]) for at in range(ranks)], sems)
    row, fast = lax.axis_index("row"), lax.axis_index("lo")
    for flip in range(low):
        for slow in range(span):
            sender = fast ^ flip
            block = jnp.where(lax.rem(sender, ranks) == 0, span - 1 - slow, slow)
            first = pl.multiple_of((block * low + sender) * cols, cols)
            for source in range(ranks):
                step = lax.rem(source + ranks - row, ranks)
                bias_rows[step, :, pl.ds(first, cols), :] = gathered[flip][source, slow]
    turned = jnp.transpose(weight[...].astype(F32)).astype(BF16)
    for load in loads:
        load.wait()
    own_lines = jnp.concatenate([turned[:width], turned[2 * width :]], axis=0)
    peer_lines = turned[2 * width : 3 * width]
    batch = 4
    tiles = [(step, head) for step in range(ranks) for head in range(HT)]
    groups = cols // batch
    for group in range(groups):
        at = group * batch
        for step in range(ranks):
            some = normed[step, at : at + batch].reshape(batch * rows, channels)
            here = slice(step * rows, (step + 1) * rows)
            raw = jnp.dot(some, weight[:, width : 2 * width], preferred_element_type=F32)
            key[at : at + batch, here, :] = raw.astype(BF16).reshape(batch, rows, width)
            lines = own_lines if step == 0 else peer_lines
            raw = lax.dot_general(lines, some, NT, preferred_element_type=F32)
            for side in range(batch):
                part = raw[:, side * rows : (side + 1) * rows]
                if step == 0:
                    query[at + side] = (part[:width] * DT ** (-0.5)).astype(BF16)
                    gate[at + side] = jax.nn.sigmoid(part[2 * width :])
                    part = part[width : 2 * width]
                value[at + side, :, here] = part.astype(BF16)
        for step, head in tiles[group::groups]:
            bias[step * rows : (step + 1) * rows, head * rows : (head + 1) * rows] = jnp.transpose(
                bias_rows[step, head]
            )
    def score(col, slot):
        scores, peak, _ = slots[slot]
        own = query[col]
        blocks = []
        for head in range(HT):
            zeros = [jnp.zeros((size, rows), BF16) for size in (head * DT, width - (head + 1) * DT)]
            block = [zeros[0], own[head * DT : (head + 1) * DT], zeros[1]]
            blocks.append(jnp.concatenate([b for b in block if b.shape[0]], axis=0))
        stacked = jnp.concatenate(blocks, axis=1)
        raw = jnp.dot(key[col], stacked, preferred_element_type=F32) + bias[...]
        scores[...] = raw
        peak[...] = jnp.max(raw, axis=0, keepdims=True)

    def attend(col, slot):
        scores, peak, weights = slots[slot]
        exponent = jnp.exp(scores[...] - peak[...])
        scale = 1.0 / jnp.sum(exponent, axis=0, keepdims=True)
        weights[...] = exponent.astype(BF16)
        parts = []
        for head in range(0, HT, 2):
            here = slice(head * rows, (head + 2) * rows)
            summed = jnp.dot(
                value[col, head * DT : (head + 2) * DT, :],
                weights[:, here],
                preferred_element_type=F32,
            )
            summed = summed * scale[:, here]
            parts += [summed[:DT, :rows], summed[DT:, rows:]]
        gated[col] = (gate[col] * jnp.concatenate(parts, axis=0)).astype(BF16)

    score(0, 0)

    @pl.loop(0, cols // batch)
    def _(group):
        for side in range(batch):
            col = group * batch + side
            score(jnp.minimum(col + 1, cols - 1), (side + 1) % 2)
            attend(col, side % 2)

    for at in range(0, cols, batch):
        some = jnp.concatenate([gated[at + side] for side in range(batch)], axis=1)
        raw = lax.dot_general(
            some, out_weight[...], (((0,), (0,)), ((), ())), preferred_element_type=F32
        )
        for side in range(batch):
            wide[pl.ds(at + side, rows, stride=cols), :] = raw[side * rows : (side + 1) * rows]
    owners, _, lanes = pair_bias.shape
    own = rows // owners
    for owner in range(owners):
        here = slice(owner * own, (owner + 1) * own)
        some = pair[here].astype(F32).reshape(own * cols, channels)
        some = (some + wide[owner * own * cols : (owner + 1) * own * cols, :]).astype(BF16)
        new[here] = some.reshape(own, cols, channels)
        renormed[owner] = normalize(some).astype(BF16).reshape(own, cols, channels)
    stores = start([(new, new_hbm)], sems, len(loads))
    lane = lax.broadcasted_iota(jnp.int32, (lanes, HD), 0)
    pick = (lane // own == lax.broadcasted_iota(jnp.int32, (lanes, HD), 1)).astype(BF16)
    spread = jnp.dot(pick, bias_weight[...], preferred_element_type=F32)
    token_of = lax.rem(lax.broadcasted_iota(jnp.int32, (lanes, channels), 0), own)
    spots = [jnp.where(token_of == token, spread, 0.0).astype(BF16) for token in range(own)]
    flat = [renormed[:, token].reshape(owners * cols, channels) for token in range(own)]
    total = lax.dot_general(
        jnp.concatenate(flat, axis=1),
        jnp.concatenate(spots, axis=1),
        NT,
        preferred_element_type=F32,
    )
    total = total.reshape(owners, cols, lanes)
    for place, owner in enumerate(turns(owners // low, low)):
        pair_bias[place] = total[owner]
    stores += start([(pair_bias, pair_bias_hbm)], sems, len(loads) + 1)
    for store in stores:
        store.wait()


def head_masks(width):
    lane = lax.broadcasted_iota(jnp.int32, (1, width), 1)
    return [(lane >= head * DH) & (lane < (head + 1) * DH) for head in range(HD)]


def attend_kernel(share, *refs):
    bias, weight, refs = refs[0], refs[1], refs[2:]
    found, value, refs = refs[:share], refs[share : 2 * share], refs[2 * share :]
    out_hbm, wide, out, sems = refs
    count, own, width = wide.shape
    each, tokens, _ = value[0].shape
    low = lax.axis_size("lo")
    order = turns(bias.shape[0] // low, low)
    turned = jnp.concatenate([bias[order.index(c)] for c in range(len(order))], axis=0)
    masks = head_masks(width)
    turn = (((0,), (0,)), ((), ()))
    slots = [(flip, at) for flip in range(share) for at in range(each)]
    weights, totals = [], []
    for flip, at in slots:
        scores = found[flip][at, :tokens] + turned
        peak = jnp.max(scores, axis=0, keepdims=True)
        exponent = jnp.exp(scores - peak)
        weights.append(exponent.astype(BF16))
        totals.append(jnp.sum(exponent, axis=0, keepdims=True))
    totals.append(jnp.ones((-count % 8, turned.shape[1]), F32))
    scale = 1.0 / jnp.transpose(jnp.concatenate([t for t in totals if t.shape[0]], axis=0))
    rows = []
    for slot, (flip, at) in enumerate(slots):
        summed = lax.dot_general(weights[slot], value[flip][at], turn, preferred_element_type=F32)
        summed = summed * scale[:, slot : slot + 1]
        attended = jnp.where(masks[0], summed[:own], 0.0)
        for head in range(1, HD):
            attended = jnp.where(masks[head], summed[head * own : (head + 1) * own], attended)
        rows.append(attended)

    def gates(kind):
        lanes = turned.shape[1]
        first = tokens + kind * own * (width // lanes)
        places = [slice(first + lane * own, first + (lane + 1) * own) for lane in range(width // lanes)]
        return jnp.concatenate(
            [
                jnp.concatenate([found[flip][at, place] for place in places], axis=1)
                for flip, at in slots
            ],
            axis=0,
        )

    gated = (gates(0) * jnp.concatenate(rows, axis=0)).astype(BF16)
    projected = gates(1) * jnp.dot(gated, weight[...], preferred_element_type=F32)
    for slot, (flip, at) in enumerate(slots):
        wide[first_sample(share, each, flip) + at] = projected[slot * own : (slot + 1) * own]
    out[...] = wide[...].reshape(count * own, width).astype(BF16)
    for store in start([(out, out_hbm)], sems):
        store.wait()


def local(
    pair_repr,
    tri_weight,
    tri_bias_weight,
    tri_output_weight,
    samples,
    levels,
    single_cond,
    noise_weight,
    modulation_weight,
    attention_weight,
    pair_bias_weight,
    output_weight,
    output_gate_weight,
):
    rows, cols, channels = pair_repr.shape
    ranks, high, low = (lax.axis_size(name) for name in ("row", "hi", "lo"))
    col_count = high * low
    sample_count, tokens, width = samples.shape
    own = rows // col_count
    span = high // ranks
    keys = ranks * rows
    shape = jax.ShapeDtypeStruct

    turned = jnp.transpose(tri_bias_weight)
    normed_shape = shape((cols, rows, channels), BF16)
    bias_shape = shape((HT, cols, rows), F32)
    wide = pltpu.VMEM((rows * cols, channels), F32)
    copies_shape = shape((ranks * high, *bias_shape.shape), F32)
    bias, normed = call(
        norm_kernel,
        (copies_shape, normed_shape),
        (pair_repr, turned),
        scratch=(held(pair_repr), held(turned), wide, held(bias_shape), held(normed_shape)),
        copies=6 + ranks * high,
        flops=2 * rows * cols * channels * HT,
    )
    groups = [
        [
            (r * high + h) * low + lo
            for r in range(ranks)
            for h in places(high, ranks, lo)
        ]
        for lo in range(low)
    ]
    placed = lax.all_to_all(
        bias, ("row", "hi", "lo"), split_axis=0, concat_axis=0, axis_index_groups=groups
    )
    peers = [
        lax.ppermute(normed, "row", [((r + step) % ranks, r) for r in range(ranks)])
        for step in range(1, ranks)
    ]

    share = 2 if low % 2 == 0 and sample_count % 2 == 0 else 1
    each = sample_count // share
    part = (each, tokens, width)
    extra = share * own
    key_shape = shape((each, tokens + 2 * extra, width), BF16)
    key, value = call(
        functools.partial(condition_kernel, share),
        (key_shape, shape(part, BF16)),
        (
            levels,
            single_cond,
            noise_weight,
            modulation_weight,
            samples,
            attention_weight,
        ),
        scratch=(
            pltpu.SMEM(levels.shape, levels.dtype),
            held(single_cond),
            held(noise_weight),
            held(modulation_weight),
            pltpu.VMEM(part, BF16),
            pltpu.VMEM((2, width, width), BF16),
            held(key_shape),
            pltpu.VMEM(part, BF16),
            pltpu.VMEM(part, BF16),
            pltpu.VMEM((each, *single_cond.shape), BF16),
        ),
        copies=9,
        after=(bias,),
        flops=4 * each * tokens * width * 2 * width,
        exps=each * tokens * width,
    )
    placed = placed.reshape(ranks, high, *bias_shape.shape)
    place = lax.axis_index("row") + ranks - lax.rem(lax.axis_index("lo"), ranks)
    gathered = [lax.dynamic_slice_in_dim(placed, lax.rem(place, ranks) * span, span, 1)]
    found_shape = shape((each, tokens + 2 * width // HD, HD * own), F32)
    found = list(
        call(
            functools.partial(token_kernel, share),
            (found_shape,) * share,
            (attention_weight, output_gate_weight, key),
            scratch=(
                pltpu.VMEM((2, width, width), BF16),
                held(output_gate_weight),
                held(key),
                pltpu.VMEM((share, *found_shape.shape), F32),
                pltpu.VMEM((2, each * extra, width), F32),
            ),
            copies=4 + share,
            after=(gathered[0],),
            mib=53,
            flops=64 * rows * cols * channels * HT * DT,
        )
    )
    bit = low // 2
    while bit:
        flip = [(c ^ bit, c) for c in range(low)]
        ready = [gathered[0], *(hold(part, found[0]) for part in gathered[1:])]
        more = [lax.ppermute(part, "lo", flip) for part in ready]
        gathered = [part for both in zip(ready, more) for part in both]
        bit //= 2
    values = [value]
    if share == 2:
        other = [(c ^ 1, c) for c in range(low)]
        values.append(lax.ppermute(value, "lo", other))
        found[1] = lax.ppermute(found[1], "lo", other)

    pair_weight = jnp.transpose(pair_bias_weight)
    outs = (shape((rows, cols, channels), BF16), shape((col_count, cols, HD * own), F32))
    new_pair, pair_bias = call(
        functools.partial(triangle_kernel, ranks, low),
        outs,
        (
            pair_repr,
            tri_weight,
            tri_output_weight,
            pair_weight,
            *gathered,
            normed,
            *peers,
        ),
        scratch=(
            pltpu.VMEM((ranks, cols, rows, channels), BF16),
            held(outs[0]),
            held(outs[1]),
            pltpu.VMEM((ranks, HT, rows, rows), F32),
            pltpu.VMEM((keys, HT * rows), F32),
            pltpu.VMEM((cols, HT * DT, rows), BF16),
            pltpu.VMEM((cols, keys, HT * DT), BF16),
            pltpu.VMEM((cols, HT * DT, keys), BF16),
            pltpu.VMEM((cols, HT * DT, rows), F32),
            wide,
            *[
                pltpu.VMEM(*slot)
                for slot in (
                    ((keys, HT * rows), F32),
                    ((1, HT * rows), F32),
                    ((keys, HT * rows), BF16),
                )
                * 2
            ],
            pltpu.VMEM((cols, HT * DT, rows), BF16),
            pltpu.VMEM((col_count, own, cols, channels), BF16),
        ),
        copies=2 + ranks,
        after=(found[0],),
        near=range(4 + low),
        mib=52,
        flops=4 * HT * rows * cols * keys * HT * DT,
        exps=HT * rows * cols * keys,
    )
    own_bias = lax.all_to_all(
        pair_bias, ("hi", "lo"), split_axis=0, concat_axis=0, axis_index_groups=[turns(high, low)]
    )

    outs = (shape((sample_count * own, width), BF16),)
    (attn_update,) = call(
        functools.partial(attend_kernel, share),
        outs,
        (own_bias, output_weight, *found, *values),
        scratch=(pltpu.VMEM((sample_count, own, width), F32), held(outs[0])),
        copies=1,
        near=range(2 + 2 * share),
        mib=48,
        flops=2 * sample_count * HD * own * tokens * width,
        exps=sample_count * HD * own * tokens,
    )
    return (new_pair, attn_update.reshape(sample_count, own, width))


def solution(mesh):
    ranks, col_count, groups = (mesh.shape[name] for name in ("row", "col", "smp"))
    low = math.gcd(col_count // ranks, 4)
    finer = jax.sharding.Mesh(
        mesh.devices.reshape(ranks, col_count // low, low, groups), ("row", "hi", "lo", "smp")
    )
    tile = P("row", ("hi", "lo"), None)
    return jax.shard_map(
        local,
        mesh=finer,
        in_specs=(tile, P(), P(), P(), P("smp", None, None), P("smp"), *[P()] * 7),
        out_specs=(tile, P("smp", ("row", "hi", "lo"), None)),
        check_vma=False,
    )
```

```python
import functools
import math

import jax
import jax.numpy as jnp
from jax import lax
from jax.experimental import pallas as pl
from jax.experimental.pallas import tpu as pltpu
from jax.sharding import PartitionSpec as P

HT = 4
DT = 32
CA = 768
HD = 16
DH = 48
NE = 256
LEVELS = 200

NORM_EPSILON = 1e-05
SIGMA_DATA = 16.0
SIGMA_MAX = 160.0
SIGMA_MIN = 0.0004


F32 = jnp.float32
BF16 = jnp.bfloat16
NT = (((1,), (1,)), ((), ()))


def normalize(values):
    values = values.astype(F32)
    average = jnp.mean(values, axis=-1, keepdims=True)
    centred = values - average
    variance = jnp.mean(centred * centred, axis=-1, keepdims=True)
    return centred * lax.rsqrt(variance + NORM_EPSILON)


def noise_features(levels):
    fraction = levels.astype(F32) / (LEVELS - 1)
    upper_root = SIGMA_MAX ** (1.0 / 7.0)
    lower_root = SIGMA_MIN ** (1.0 / 7.0)
    noise_sigma = SIGMA_DATA * (upper_root + fraction * (lower_root - upper_root)) ** 7
    scaled = 0.25 * jnp.log(noise_sigma / SIGMA_DATA)
    frequency = (
        2.0 * math.pi * jnp.exp(jnp.arange(NE // 2, dtype=F32) * (math.log(100.0) / (NE // 2)))
    )
    angles = scaled[:, None] * frequency[None, :]
    return jnp.concatenate([jnp.cos(angles), jnp.sin(angles)], axis=-1)


def nbytes(*shapes):
    return sum(math.prod(s.shape) * jnp.dtype(s.dtype).itemsize for s in shapes)


def held(operand):
    return pltpu.VMEM(operand.shape, operand.dtype)


def call(
    kernel, out_shape, operands, scratch=(), copies=0, after=(), near=(), mib=60, flops=0, exps=0
):
    in_specs = [
        pl.BlockSpec(memory_space=pltpu.VMEM if at in near else pltpu.HBM)
        for at in range(len(operands))
    ]
    in_specs += [pl.BlockSpec(memory_space=pl.ANY)] * len(after)
    moved = nbytes(*operands, *out_shape)
    count = len(operands)

    def body(*refs):
        kernel(*refs[:count], *refs[count + len(after) :])

    return pl.pallas_call(
        body,
        out_shape=out_shape,
        in_specs=in_specs,
        out_specs=tuple(pl.BlockSpec(memory_space=pltpu.HBM) for _ in out_shape),
        scratch_shapes=[*scratch, pltpu.SemaphoreType.DMA((copies,))],
        compiler_params=pltpu.CompilerParams(vmem_limit_bytes=mib << 20),
        cost_estimate=pl.CostEstimate(flops=flops, bytes_accessed=moved, transcendentals=exps),
    )(*operands, *after)


def start(pairs, sems, first=0):
    copies = [
        pltpu.make_async_copy(source, target, sems.at[first + at])
        for at, (source, target) in enumerate(pairs)
    ]
    for copy in copies:
        copy.start()
    return copies


def places(high, ranks, lo):
    span = high // ranks
    rest = [(h + lo % ranks * span) % high for h in range(high)]
    if lo % ranks == 0:
        rest = [h // span * span + span - 1 - h % span for h in rest]
    return rest


def turns(high, low):
    slow = sorted(range(high), key=lambda h: (h < high // 2, abs(2 * h - high)))
    return [h * low + lo for h in slow for lo in reversed(range(low))]


def hold(value, after):
    return pl.pallas_call(
        lambda *refs: None,
        out_shape=jax.ShapeDtypeStruct(value.shape, value.dtype),
        in_specs=[
            pl.BlockSpec(memory_space=pltpu.HBM),
            pl.BlockSpec(memory_space=pl.ANY),
        ],
        out_specs=pl.BlockSpec(memory_space=pltpu.HBM),
        input_output_aliases={0: 0},
        compiler_params=pltpu.CompilerParams(vmem_limit_bytes=48 << 20),
    )(value, after)


def own_place():
    low = lax.axis_size("lo")
    return lax.axis_index("hi") * low + lax.axis_index("lo"), lax.axis_size("hi") * low


def norm_kernel(pair_hbm, weight_hbm, bias_hbm, normed_hbm, pair, weight, wide, bias, normed, sems):
    rows, cols, channels = pair.shape
    pieces = 4
    some = rows // pieces
    slices = [pl.ds(at * some, some) for at in range(pieces)]
    loads = start([(weight_hbm, weight)] + [(pair_hbm.at[h], pair.at[h]) for h in slices], sems)
    for at, load in enumerate(loads[1:]):
        load.wait()
        tile = pair[at * some : (at + 1) * some].astype(F32).reshape(some * cols, channels)
        wide[at * some * cols : (at + 1) * some * cols, :] = normalize(tile)
    loads[0].wait()
    for col in range(cols):
        one = wide[pl.ds(col, rows, stride=cols), :].astype(BF16)
        normed[col] = one
        bias[:, col, :] = lax.dot_general(weight[...], one, NT, preferred_element_type=F32)
    copies = bias_hbm.shape[0]
    pairs = [(bias, bias_hbm.at[at]) for at in range(copies)] + [(normed, normed_hbm)]
    for copy in start(pairs, sems, 1 + pieces):
        copy.wait()


def first_sample(share, each, flip=0):
    return (lax.rem(lax.axis_index("lo"), share) ^ flip) * each


def condition_kernel(share, *refs):
    levels_hbm, cond_hbm, noise_hbm, modulation_hbm, samples_hbm, attention_hbm = refs[:6]
    key_hbm, value_hbm = refs[6:8]
    levels, cond, noise, modulation, samples, attention, key, value = refs[8:16]
    adapted, conditions, sems = refs[16:]
    count, tokens, width = samples.shape
    extra = (key.shape[1] - tokens) // 2
    first = first_sample(share, count)
    loads = start(
        [
            (levels_hbm, levels),
            (noise_hbm, noise),
            (cond_hbm, cond),
            (modulation_hbm, modulation),
            (samples_hbm.at[pl.ds(first, count)], samples),
            (attention_hbm.at[:, pl.ds(width, width)], attention.at[0]),
            (attention_hbm.at[:, pl.ds(2 * width, width)], attention.at[1]),
        ],
        sems,
    )
    loads[0].wait()
    row = lax.broadcasted_iota(jnp.int32, (8, NE // 2), 0)
    level = jnp.zeros((8, NE // 2), F32)
    for sample in range(count):
        level = jnp.where(row == sample, levels[first + sample].astype(F32), level)
    fraction = level / (LEVELS - 1)
    upper_root = SIGMA_MAX ** (1.0 / 7.0)
    lower_root = SIGMA_MIN ** (1.0 / 7.0)
    root = upper_root + fraction * (lower_root - upper_root)
    square = root * root
    sigma = SIGMA_DATA * (square * square * square * root)
    scaled = 0.25 * jnp.log(sigma / SIGMA_DATA)
    step = lax.broadcasted_iota(jnp.int32, scaled.shape, 1).astype(F32)
    angles = scaled * (2.0 * math.pi * jnp.exp(step * (math.log(100.0) / (NE // 2))))
    features = jnp.concatenate([jnp.cos(angles), jnp.sin(angles)], axis=-1).astype(BF16)
    loads[1].wait()
    terms = jnp.dot(features, noise[...], preferred_element_type=F32)
    for load in loads[2:4]:
        load.wait()

    loads[4].wait()
    for sample in range(count):
        trunk = cond[...].astype(F32) + terms[sample : sample + 1]
        conditioned = normalize(trunk).astype(BF16)
        conditions[sample] = conditioned
        modulated = jnp.dot(conditioned, modulation[...], preferred_element_type=F32)
        gain = jax.nn.sigmoid(modulated[:, :width])
        one = gain * normalize(samples[sample]) + modulated[:, width:]
        adapted[sample] = one.astype(BF16)
    place, places = own_place()
    chip = lax.div(lax.axis_index("row") * places + place, share) * extra
    here = pl.ds(pl.multiple_of(chip, extra), extra)
    key[:, tokens : tokens + extra, :] = adapted[:, here, :]
    key[:, tokens + extra :, : cond.shape[1]] = conditions[:, here, :]
    key[:, tokens + extra :, cond.shape[1] :] = jnp.zeros(
        (count, extra, width - cond.shape[1]), BF16
    )
    stores = []
    for at, (part, target) in enumerate(((key, key_hbm), (value, value_hbm))):
        loads[5 + at].wait()
        for sample in range(count):
            part[sample, :tokens, :] = jnp.dot(
                adapted[sample], attention[at], preferred_element_type=F32
            ).astype(BF16)
        stores += start([(part, target)], sems, 7 + at)
    for store in stores:
        store.wait()


def token_kernel(share, *refs):
    attention_hbm, gate_hbm, key_hbm = refs[:3]
    targets, refs = refs[3 : 3 + share], refs[3 + share :]
    attention, gate_weight, key, found, wide, sems = refs
    count, tokens, width = key.shape
    tokens = found.shape[2] - 2 * width // HD
    extra = (key.shape[1] - tokens) // 2
    own = extra // share
    loads = start(
        [
            (key_hbm, key),
            (attention_hbm.at[:, pl.ds(0, width)], attention.at[0]),
            (attention_hbm.at[:, pl.ds(3 * width, width)], attention.at[1]),
            (gate_hbm, gate_weight),
        ],
        sems,
    )
    for load in loads[:2]:
        load.wait()
    flat = key[:, tokens : tokens + extra, :].reshape(count * extra, width)
    raw = jnp.dot(flat, attention[0], preferred_element_type=F32)
    query = (raw * DH ** (-0.5)).astype(BF16).astype(F32)
    masks = head_masks(width)
    for sample in range(count):
        stacked = []
        for core in range(share):
            at = sample * extra + core * own
            one = query[at : at + own]
            stacked += [jnp.where(m, one, 0.0) for m in masks]
        stacked = jnp.concatenate(stacked, axis=0).astype(BF16)
        raw = lax.dot_general(key[sample, :tokens, :], stacked, NT, preferred_element_type=F32)
        for core in range(share):
            found[core, sample, :tokens, :] = raw[:, core * HD * own : (core + 1) * HD * own]
    loads[2].wait()
    wide[0] = jax.nn.sigmoid(jnp.dot(flat, attention[1], preferred_element_type=F32))
    loads[3].wait()
    flat = key[:, tokens + extra :, :].reshape(count * extra, width)[:, : gate_weight.shape[0]]
    wide[1] = jax.nn.sigmoid(jnp.dot(flat, gate_weight[...], preferred_element_type=F32))
    lanes = found.shape[3]
    for core in range(share):
        for sample in range(count):
            at = sample * extra + core * own
            to = tokens
            for kind in range(2):
                for lane in range(0, width, lanes):
                    found[core, sample, to : to + own, :] = wide[
                        kind, at : at + own, lane : lane + lanes
                    ]
                    to += own
    mine = lax.rem(lax.axis_index("lo"), share)
    stores = start(
        [(found.at[mine ^ flip], targets[flip]) for flip in range(share)], sems, len(loads)
    )
    for store in stores:
        store.wait()


def triangle_kernel(ranks, low, *refs):
    pair, weight, out_weight, bias_weight = refs[:4]
    gathered, refs = refs[4 : 4 + low], refs[4 + low :]
    normed_hbm, refs = refs[:ranks], refs[ranks:]
    new_hbm, pair_bias_hbm, refs = refs[0], refs[1], refs[2:]
    normed, new, pair_bias, refs = refs[0], refs[1], refs[2], refs[3:]
    bias_rows, bias, query, key, value, gate, wide = refs[:7]
    slots, (gated, renormed, sems) = (refs[7:10], refs[10:13]), refs[13:]
    rows, cols, channels = pair.shape
    width = HT * DT
    span = gathered[0].shape[1]
    loads = start([(normed_hbm[at], normed.at[at]) for at in range(ranks)], sems)
    row, fast = lax.axis_index("row"), lax.axis_index("lo")
    for flip in range(low):
        for slow in range(span):
            sender = fast ^ flip
            block = jnp.where(lax.rem(sender, ranks) == 0, span - 1 - slow, slow)
            first = pl.multiple_of((block * low + sender) * cols, cols)
            for source in range(ranks):
                step = lax.rem(source + ranks - row, ranks)
                bias_rows[step, :, pl.ds(first, cols), :] = gathered[flip][source, slow]
    turned = jnp.transpose(weight[...].astype(F32)).astype(BF16)
    for load in loads:
        load.wait()
    own_lines = jnp.concatenate([turned[:width], turned[2 * width :]], axis=0)
    peer_lines = turned[2 * width : 3 * width]
    batch = 4
    tiles = [(step, head) for step in range(ranks) for head in range(HT)]
    groups = cols // batch
    for group in range(groups):
        at = group * batch
        for step in range(ranks):
            some = normed[step, at : at + batch].reshape(batch * rows, channels)
            here = slice(step * rows, (step + 1) * rows)
            raw = jnp.dot(some, weight[:, width : 2 * width], preferred_element_type=F32)
            key[at : at + batch, here, :] = raw.astype(BF16).reshape(batch, rows, width)
            lines = own_lines if step == 0 else peer_lines
            raw = lax.dot_general(lines, some, NT, preferred_element_type=F32)
            for side in range(batch):
                part = raw[:, side * rows : (side + 1) * rows]
                if step == 0:
                    query[at + side] = (part[:width] * DT ** (-0.5)).astype(BF16)
                    gate[at + side] = jax.nn.sigmoid(part[2 * width :])
                    part = part[width : 2 * width]
                value[at + side, :, here] = part.astype(BF16)
        for step, head in tiles[group::groups]:
            bias[step * rows : (step + 1) * rows, head * rows : (head + 1) * rows] = jnp.transpose(
                bias_rows[step, head]
            )
    def score(col, slot):
        scores, peak, _ = slots[slot]
        own = query[col]
        blocks = []
        for head in range(HT):
            zeros = [jnp.zeros((size, rows), BF16) for size in (head * DT, width - (head + 1) * DT)]
            block = [zeros[0], own[head * DT : (head + 1) * DT], zeros[1]]
            blocks.append(jnp.concatenate([b for b in block if b.shape[0]], axis=0))
        stacked = jnp.concatenate(blocks, axis=1)
        raw = jnp.dot(key[col], stacked, preferred_element_type=F32) + bias[...]
        scores[...] = raw
        peak[...] = jnp.max(raw, axis=0, keepdims=True)

    def attend(col, slot):
        scores, peak, weights = slots[slot]
        exponent = jnp.exp(scores[...] - peak[...])
        scale = 1.0 / jnp.sum(exponent, axis=0, keepdims=True)
        weights[...] = exponent.astype(BF16)
        parts = []
        for head in range(0, HT, 2):
            here = slice(head * rows, (head + 2) * rows)
            summed = jnp.dot(
                value[col, head * DT : (head + 2) * DT, :],
                weights[:, here],
                preferred_element_type=F32,
            )
            summed = summed * scale[:, here]
            parts += [summed[:DT, :rows], summed[DT:, rows:]]
        gated[col] = (gate[col] * jnp.concatenate(parts, axis=0)).astype(BF16)

    score(0, 0)

    @pl.loop(0, cols // 8)
    def _(group):
        for side in range(8):
            col = group * 8 + side
            score(jnp.minimum(col + 1, cols - 1), (side + 1) % 2)
            attend(col, side % 2)

    for at in range(0, cols, batch):
        some = jnp.concatenate([gated[at + side] for side in range(batch)], axis=1)
        raw = lax.dot_general(
            some, out_weight[...], (((0,), (0,)), ((), ())), preferred_element_type=F32
        )
        for side in range(batch):
            wide[pl.ds(at + side, rows, stride=cols), :] = raw[side * rows : (side + 1) * rows]
    owners, _, lanes = pair_bias.shape
    own = rows // owners
    for owner in range(owners):
        here = slice(owner * own, (owner + 1) * own)
        some = pair[here].astype(F32).reshape(own * cols, channels)
        some = (some + wide[owner * own * cols : (owner + 1) * own * cols, :]).astype(BF16)
        new[here] = some.reshape(own, cols, channels)
        renormed[owner] = normalize(some).astype(BF16).reshape(own, cols, channels)
    stores = start([(new, new_hbm)], sems, len(loads))
    lane = lax.broadcasted_iota(jnp.int32, (lanes, HD), 0)
    pick = (lane // own == lax.broadcasted_iota(jnp.int32, (lanes, HD), 1)).astype(BF16)
    spread = jnp.dot(pick, bias_weight[...], preferred_element_type=F32)
    token_of = lax.rem(lax.broadcasted_iota(jnp.int32, (lanes, channels), 0), own)
    spots = [jnp.where(token_of == token, spread, 0.0).astype(BF16) for token in range(own)]
    flat = [renormed[:, token].reshape(owners * cols, channels) for token in range(own)]
    total = lax.dot_general(
        jnp.concatenate(flat, axis=1),
        jnp.concatenate(spots, axis=1),
        NT,
        preferred_element_type=F32,
    )
    total = total.reshape(owners, cols, lanes)
    for place, owner in enumerate(turns(owners // low, low)):
        pair_bias[place] = total[owner]
    stores += start([(pair_bias, pair_bias_hbm)], sems, len(loads) + 1)
    for store in stores:
        store.wait()


def head_masks(width):
    lane = lax.broadcasted_iota(jnp.int32, (1, width), 1)
    return [(lane >= head * DH) & (lane < (head + 1) * DH) for head in range(HD)]


def attend_kernel(share, *refs):
    bias, weight, refs = refs[0], refs[1], refs[2:]
    found, value, refs = refs[:share], refs[share : 2 * share], refs[2 * share :]
    out_hbm, wide, out, sems = refs
    count, own, width = wide.shape
    each, tokens, _ = value[0].shape
    low = lax.axis_size("lo")
    order = turns(bias.shape[0] // low, low)
    turned = jnp.concatenate([bias[order.index(c)] for c in range(len(order))], axis=0)
    masks = head_masks(width)
    turn = (((0,), (0,)), ((), ()))
    slots = [(flip, at) for flip in range(share) for at in range(each)]
    weights, totals = [], []
    for flip, at in slots:
        scores = found[flip][at, :tokens] + turned
        peak = jnp.max(scores, axis=0, keepdims=True)
        exponent = jnp.exp(scores - peak)
        weights.append(exponent.astype(BF16))
        totals.append(jnp.sum(exponent, axis=0, keepdims=True))
    totals.append(jnp.ones((-count % 8, turned.shape[1]), F32))
    scale = 1.0 / jnp.transpose(jnp.concatenate([t for t in totals if t.shape[0]], axis=0))
    rows = []
    for slot, (flip, at) in enumerate(slots):
        summed = lax.dot_general(weights[slot], value[flip][at], turn, preferred_element_type=F32)
        summed = summed * scale[:, slot : slot + 1]
        attended = jnp.where(masks[0], summed[:own], 0.0)
        for head in range(1, HD):
            attended = jnp.where(masks[head], summed[head * own : (head + 1) * own], attended)
        rows.append(attended)

    def gates(kind):
        lanes = turned.shape[1]
        first = tokens + kind * own * (width // lanes)
        places = [slice(first + lane * own, first + (lane + 1) * own) for lane in range(width // lanes)]
        return jnp.concatenate(
            [
                jnp.concatenate([found[flip][at, place] for place in places], axis=1)
                for flip, at in slots
            ],
            axis=0,
        )

    gated = (gates(0) * jnp.concatenate(rows, axis=0)).astype(BF16)
    projected = gates(1) * jnp.dot(gated, weight[...], preferred_element_type=F32)
    for slot, (flip, at) in enumerate(slots):
        wide[first_sample(share, each, flip) + at] = projected[slot * own : (slot + 1) * own]
    out[...] = wide[...].reshape(count * own, width).astype(BF16)
    for store in start([(out, out_hbm)], sems):
        store.wait()


def local(
    pair_repr,
    tri_weight,
    tri_bias_weight,
    tri_output_weight,
    samples,
    levels,
    single_cond,
    noise_weight,
    modulation_weight,
    attention_weight,
    pair_bias_weight,
    output_weight,
    output_gate_weight,
):
    rows, cols, channels = pair_repr.shape
    ranks, high, low = (lax.axis_size(name) for name in ("row", "hi", "lo"))
    col_count = high * low
    sample_count, tokens, width = samples.shape
    own = rows // col_count
    span = high // ranks
    keys = ranks * rows
    shape = jax.ShapeDtypeStruct

    turned = jnp.transpose(tri_bias_weight)
    normed_shape = shape((cols, rows, channels), BF16)
    bias_shape = shape((HT, cols, rows), F32)
    wide = pltpu.VMEM((rows * cols, channels), F32)
    copies_shape = shape((ranks * high, *bias_shape.shape), F32)
    bias, normed = call(
        norm_kernel,
        (copies_shape, normed_shape),
        (pair_repr, turned),
        scratch=(held(pair_repr), held(turned), wide, held(bias_shape), held(normed_shape)),
        copies=6 + ranks * high,
        flops=2 * rows * cols * channels * HT,
    )
    groups = [
        [
            (r * high + h) * low + lo
            for r in range(ranks)
            for h in places(high, ranks, lo)
        ]
        for lo in range(low)
    ]
    placed = lax.all_to_all(
        bias, ("row", "hi", "lo"), split_axis=0, concat_axis=0, axis_index_groups=groups
    )
    peers = [
        lax.ppermute(normed, "row", [((r + step) % ranks, r) for r in range(ranks)])
        for step in range(1, ranks)
    ]

    share = 2 if low % 2 == 0 and sample_count % 2 == 0 else 1
    each = sample_count // share
    part = (each, tokens, width)
    extra = share * own
    key_shape = shape((each, tokens + 2 * extra, width), BF16)
    key, value = call(
        functools.partial(condition_kernel, share),
        (key_shape, shape(part, BF16)),
        (
            levels,
            single_cond,
            noise_weight,
            modulation_weight,
            samples,
            attention_weight,
        ),
        scratch=(
            pltpu.SMEM(levels.shape, levels.dtype),
            held(single_cond),
            held(noise_weight),
            held(modulation_weight),
            pltpu.VMEM(part, BF16),
            pltpu.VMEM((2, width, width), BF16),
            held(key_shape),
            pltpu.VMEM(part, BF16),
            pltpu.VMEM(part, BF16),
            pltpu.VMEM((each, *single_cond.shape), BF16),
        ),
        copies=9,
        after=(bias,),
        flops=4 * each * tokens * width * 2 * width,
        exps=each * tokens * width,
    )
    placed = placed.reshape(ranks, high, *bias_shape.shape)
    place = lax.axis_index("row") + ranks - lax.rem(lax.axis_index("lo"), ranks)
    gathered = [lax.dynamic_slice_in_dim(placed, lax.rem(place, ranks) * span, span, 1)]
    found_shape = shape((each, tokens + 2 * width // HD, HD * own), F32)
    found = list(
        call(
            functools.partial(token_kernel, share),
            (found_shape,) * share,
            (attention_weight, output_gate_weight, key),
            scratch=(
                pltpu.VMEM((2, width, width), BF16),
                held(output_gate_weight),
                held(key),
                pltpu.VMEM((share, *found_shape.shape), F32),
                pltpu.VMEM((2, each * extra, width), F32),
            ),
            copies=4 + share,
            after=(gathered[0],),
            mib=53,
            flops=64 * rows * cols * channels * HT * DT,
        )
    )
    bit = low // 2
    while bit:
        flip = [(c ^ bit, c) for c in range(low)]
        ready = [gathered[0], *(hold(part, found[0]) for part in gathered[1:])]
        more = [lax.ppermute(part, "lo", flip) for part in ready]
        gathered = [part for both in zip(ready, more) for part in both]
        bit //= 2
    values = [value]
    if share == 2:
        other = [(c ^ 1, c) for c in range(low)]
        values.append(lax.ppermute(value, "lo", other))
        found[1] = lax.ppermute(found[1], "lo", other)

    pair_weight = jnp.transpose(pair_bias_weight)
    outs = (shape((rows, cols, channels), BF16), shape((col_count, cols, HD * own), F32))
    new_pair, pair_bias = call(
        functools.partial(triangle_kernel, ranks, low),
        outs,
        (
            pair_repr,
            tri_weight,
            tri_output_weight,
            pair_weight,
            *gathered,
            normed,
            *peers,
        ),
        scratch=(
            pltpu.VMEM((ranks, cols, rows, channels), BF16),
            held(outs[0]),
            held(outs[1]),
            pltpu.VMEM((ranks, HT, rows, rows), F32),
            pltpu.VMEM((keys, HT * rows), F32),
            pltpu.VMEM((cols, HT * DT, rows), BF16),
            pltpu.VMEM((cols, keys, HT * DT), BF16),
            pltpu.VMEM((cols, HT * DT, keys), BF16),
            pltpu.VMEM((cols, HT * DT, rows), F32),
            wide,
            *[
                pltpu.VMEM(*slot)
                for slot in (
                    ((keys, HT * rows), F32),
                    ((1, HT * rows), F32),
                    ((keys, HT * rows), BF16),
                )
                * 2
            ],
            pltpu.VMEM((cols, HT * DT, rows), BF16),
            pltpu.VMEM((col_count, own, cols, channels), BF16),
        ),
        copies=2 + ranks,
        after=(found[0],),
        near=range(4 + low),
        mib=52,
        flops=4 * HT * rows * cols * keys * HT * DT,
        exps=HT * rows * cols * keys,
    )
    own_bias = lax.all_to_all(
        pair_bias, ("hi", "lo"), split_axis=0, concat_axis=0, axis_index_groups=[turns(high, low)]
    )

    outs = (shape((sample_count * own, width), BF16),)
    (attn_update,) = call(
        functools.partial(attend_kernel, share),
        outs,
        (own_bias, output_weight, *found, *values),
        scratch=(pltpu.VMEM((sample_count, own, width), F32), held(outs[0])),
        copies=1,
        near=range(2 + 2 * share),
        mib=48,
        flops=2 * sample_count * HD * own * tokens * width,
        exps=sample_count * HD * own * tokens,
    )
    return (new_pair, attn_update.reshape(sample_count, own, width))


def solution(mesh):
    ranks, col_count, groups = (mesh.shape[name] for name in ("row", "col", "smp"))
    low = math.gcd(col_count // ranks, 4)
    finer = jax.sharding.Mesh(
        mesh.devices.reshape(ranks, col_count // low, low, groups), ("row", "hi", "lo", "smp")
    )
    tile = P("row", ("hi", "lo"), None)
    return jax.shard_map(
        local,
        mesh=finer,
        in_specs=(tile, P(), P(), P(), P("smp", None, None), P("smp"), *[P()] * 7),
        out_specs=(tile, P("smp", ("row", "hi", "lo"), None)),
        check_vma=False,
    )
```
